32 devices in a mesh: seq: 4 (over y, core), fsdp: 8 (over z, x).
Axes of the slice: x: 2, y: 2, z: 4, core: 2. Of those that a mesh axis runs over, the one named last changes fastest.
Arguments:
- hidden_in: bfloat16 [8, 512, 1024], P('fsdp', 'seq'), may hold values from -6 to 6
- memory: bfloat16 [8, 64, 1024], P('fsdp', 'seq'), may hold values from -6 to 6
- out_grad: bfloat16 [8, 512, 1024], P('fsdp', 'seq'), may hold values from -6 to 6
- segment_ids: int32 [8, 512], P('fsdp', 'seq'), may hold values from 0 to 7, as said below
- memory_segments: int32 [8, 64], P('fsdp', 'seq'), may hold values from 1 to 7, as said below
- deal: int32 [8], replicated, may hold values from 0 to 7, as said below
- attn_in: float32 [2, 3, 1024, 1024], P(None, None, 'fsdp'), may hold values from -0.1875 to 0.1875
- attn_out: float32 [2, 1024, 1024], P(None, 'fsdp'), may hold values from -0.5 to 0.5
- fc1: float32 [1024, 8192], P('fsdp'), may hold values from -0.1875 to 0.1875
- fc2: float32 [8192, 1024], P('fsdp'), may hold values from -0.0625 to 0.0625
- proj_bias: float32 [7, 1024], P(None, 'fsdp'), may hold values from -4 to 4
- fc1_bias: float32 [8192], P('fsdp'), may hold values from -4 to 4
- norm_gain: float32 [3, 1024], P(None, 'fsdp'), may hold values from 0.1 to 1.9
- norm_bias: float32 [3, 1024], P(None, 'fsdp'), may hold values from -3 to 3
Outputs:
- out: bfloat16 [8, 512, 1024], P('fsdp', 'seq')
- grad_hidden: float32 [8, 512, 1024], P('fsdp', 'seq')
- grad_memory: float32 [8, 64, 1024], P('fsdp', 'seq')
- grad_attn_in: float32 [2, 3, 1024, 1024], P(None, None, ('seq', 'fsdp'))
- grad_attn_out: float32 [2, 1024, 1024], P(None, ('seq', 'fsdp'))
- grad_fc1: float32 [1024, 8192], P(('seq', 'fsdp'))
- grad_fc2: float32 [8192, 1024], P(('seq', 'fsdp'))
- grad_proj_bias: float32 [7, 1024], P(None, ('seq', 'fsdp'))
- grad_fc1_bias: float32 [8192], P(('seq', 'fsdp'))
- grad_norm_gain: float32 [3, 1024], P(None, ('seq', 'fsdp'))
- grad_norm_bias: float32 [3, 1024], P(None, ('seq', 'fsdp'))
The draws below stay inside these ranges and needn't reach their ends.
Inputs may be any that keep to these rules, and one draw needn't show every extreme that they name: `deal`: entry i names the block of 64 consecutive positions stored i-th; entries 2 * d and 2 * d + 1 sum to 7. `segment_ids`: 0 marks padding; in position order the tokens of one nonzero id form one run. `memory_segments`: ids never fall along a row.
All inputs are finite; a program needn't handle non-finite values.
Results may differ from the reference program's by a relative error of at most 0.018.
Values may be sent and summed in bfloat16 or wider, within the bound.
No kernel may reach another device: no remote copies, remote signals or barrier semaphores. Data moves between devices by JAX's collectives and lax.ppermute only.
A program may use at most 384 MiB of HBM per device.

```python
import math
import jax
import jax.numpy as jnp
from jax import lax

D = 1024
HEADS = 16
FF = 8192
TOK_DEV = 128
GROUPS = 8
LEN = 512
MEM = 64
N_SEQ = 4


def dealt_order(key):
    firsts = jax.random.permutation(key, N_SEQ).astype(jnp.int32)
    seconds = 2 * N_SEQ - 1 - firsts
    return jnp.stack([firsts, seconds], axis=1).reshape(2 * N_SEQ).astype(jnp.int32)


def draw_deal(key, part):
    return dealt_order(key)


def draw_segment_ids(key, part):
    order = dealt_order(key)
    key = jax.random.fold_in(key, 2)
    cut_key, pad_key = jax.random.split(key)
    middle = LEN // 2
    cuts = jax.random.randint(cut_key, (GROUPS, 5), 1, middle, dtype=jnp.int32)
    padding = jax.random.randint(pad_key, (GROUPS, 1), 1, LEN // 16 + 1, dtype=jnp.int32)
    places = jnp.arange(LEN, dtype=jnp.int32)
    labels = 1 + jnp.sum((places[None, :, None] >= cuts[:, None, :]).astype(jnp.int32), axis=-1)
    labels = jnp.where(places[None, :] >= middle, 7, labels)
    labels = jnp.where((places[None, :] >= middle - padding) & (places[None, :] < middle), 0, labels)
    labels = labels.reshape(GROUPS, 2 * N_SEQ, LEN // (2 * N_SEQ))[:, order]
    return labels.reshape(GROUPS, LEN).astype(jnp.int32)


def draw_memory_segments(key, part):
    key = jax.random.fold_in(key, 3)
    cuts = jax.random.randint(key, (GROUPS, 6), 1, MEM, dtype=jnp.int32)
    places = jnp.arange(MEM, dtype=jnp.int32)
    labels = 1 + jnp.sum((places[None, :, None] >= cuts[:, None, :]).astype(jnp.int32), axis=-1)
    return labels.astype(jnp.int32)


def with_spikes(entries, stream_key, source, target, parts, factor):
    def block_of(dim):
        return (jnp.arange(entries.shape[dim]) // (entries.shape[dim] // parts)).reshape((-1,) + (1,) * (entries.ndim - 1 - dim))

    first = jax.random.permutation(stream_key, parts)[block_of(target)]
    other_side = (block_of(target) + parts // 2) % parts
    return jnp.where((block_of(source) == first) | (block_of(source) == other_side), factor * entries, entries)


def block_scale(stream_key, extent, cuts, smallest, high):
    def one(position, parts):
        draws = jax.random.uniform(jax.random.fold_in(jax.random.fold_in(stream_key, 6), position), (parts,), jnp.float32, smallest / len(cuts), high / len(cuts))
        return jnp.repeat(jnp.exp(draws), extent[position] // parts).reshape((-1,) + (1,) * (len(extent) - position - 1))

    level = one(*cuts[0])
    for cut in cuts[1:]:
        level = level * one(*cut)
    return level


def scatter_about(key, dims, scale, most, shards=(), held_as=jnp.bfloat16):
    drawn = scale * jax.random.normal(key, dims, jnp.float32)
    if shards:
        drawn = drawn * block_scale(key, dims, shards, -0.22, 0.18)
    return jnp.clip(drawn, -most, most).astype(held_as)


def bell_draw_with(rng, dims, width, reach, cuts, heavy, kind=jnp.bfloat16):
    entries = width * jax.random.normal(rng, dims, jnp.float32)
    if cuts:
        entries = entries * block_scale(rng, dims, cuts, -0.22, 0.18)
    return jnp.clip(with_spikes(entries, jax.random.fold_in(rng, 3), *heavy), -reach, reach).astype(kind)


def setup_inputs(seed: int = 0) -> dict:
    key_list = jax.random.split(jax.random.key(seed), 15)
    hidden_in = scatter_about(key_list[0], (GROUPS, LEN, D), 1.0, 6.0, ((0, 8), (1, 4)))
    memory = scatter_about(key_list[1], (GROUPS, MEM, D), 1.0, 6.0, ((0, 8), (1, 4)))
    out_grad = bell_draw_with(key_list[2], (GROUPS, LEN, D), 1.0, 6.0, ((0, 8), (1, 4)), (1, 2, 4, 2.0))
    segment_ids = draw_segment_ids(jax.random.fold_in(key_list[14], 71), 0)
    memory_segments = draw_memory_segments(jax.random.fold_in(key_list[14], 71), 0)
    deal = draw_deal(jax.random.fold_in(key_list[14], 71), 0)
    attn_in = scatter_about(key_list[6], (2, 3, D, D), D ** -0.5, 0.1875, ((2, 8),), jnp.float32)
    attn_out = scatter_about(key_list[7], (2, D, D), (D // 8) ** -0.5, 0.5, ((1, 8),), jnp.float32)
    fc1 = scatter_about(key_list[8], (D, FF), D ** -0.5, 0.1875, ((0, 8),), jnp.float32)
    fc2 = scatter_about(key_list[9], (FF, D), FF ** -0.5, 0.0625, ((0, 8),), jnp.float32)
    proj_bias = scatter_about(key_list[10], (7, D), 0.3, 4.0, ((1, 8),), jnp.float32)
    fc1_bias = scatter_about(key_list[11], (FF,), 0.3, 4.0, ((0, 8),), jnp.float32)
    norm_gain = jnp.clip(1.0 + 0.18 * jax.random.normal(key_list[12], (3, D), jnp.float32), 0.1, 1.9)
    norm_bias = scatter_about(key_list[13], (3, D), 0.2, 3.0, ((1, 8),), jnp.float32)
    return {"hidden_in": hidden_in, "memory": memory, "out_grad": out_grad, "segment_ids": segment_ids, "memory_segments": memory_segments, "deal": deal, "attn_in": attn_in, "attn_out": attn_out, "fc1": fc1, "fc2": fc2, "proj_bias": proj_bias, "fc1_bias": fc1_bias, "norm_gain": norm_gain, "norm_bias": norm_bias}


EPSILON = 1e-05
NEGATIVE = -1e+30
HIGHEST = lax.Precision.HIGHEST

@jax.custom_vjp
def low(v):
    return lax.optimization_barrier(v.astype(jnp.bfloat16)).astype(jnp.float32)

@jax.custom_vjp
def low_back(v):
    return v

def low_keep(v):
    return (low(v), None)

def low_pass(kept, grad):
    return (grad,)

def back_keep(v):
    return (v, None)

def back_low(kept, grad):
    return (low(grad),)
low.defvjp(low_keep, low_pass)
low_back.defvjp(back_keep, back_low)

def product(left, right):
    return jnp.dot(left, right, precision=HIGHEST)

def layer_norm(values, gain, shift):
    centre = lax.optimization_barrier(jnp.mean(values, axis=-1, keepdims=True))
    centred = values - centre
    spread = lax.optimization_barrier(jnp.mean(centred * centred, axis=-1, keepdims=True))
    return centred * lax.rsqrt(spread + EPSILON) * gain + shift

def attention(queries, key_rows, value_rows, allowed):
    row_count = queries.shape[0]
    block_size = math.gcd(row_count, 512)
    head_size = D // HEADS
    score_scale = 1.0 / math.sqrt(head_size)
    key_heads = key_rows.reshape(key_rows.shape[0], HEADS, head_size)
    value_heads = value_rows.reshape(value_rows.shape[0], HEADS, head_size)

    def one_block(entry):
        query_block, allowed_block = entry
        query_heads = query_block.reshape(block_size, HEADS, head_size)
        scores = low_back(jnp.einsum('qhd,khd->hqk', query_heads, key_heads, precision=HIGHEST) * score_scale)
        masked = jnp.where(allowed_block[None], scores, NEGATIVE)
        row_top = lax.optimization_barrier(jnp.max(masked, axis=-1, keepdims=True))
        raised = jnp.where(allowed_block[None], jnp.exp(masked - row_top), 0.0)
        row_total = lax.optimization_barrier(jnp.sum(raised, axis=-1, keepdims=True))
        chance = low(raised / jnp.maximum(row_total, 1.0))
        mixed = jnp.einsum('hqk,khd->qhd', chance, value_heads, precision=HIGHEST)
        return mixed.reshape(block_size, D)
    blocks = (queries.reshape(row_count // block_size, block_size, D), allowed.reshape(row_count // block_size, block_size, allowed.shape[1]))
    return lax.map(jax.checkpoint(one_block), blocks).reshape(row_count, D)

def one_group(params, inputs, sources, segments, source_segments, positions):
    w_in, w_out, w_up, w_down, biases, up_bias, gains, shifts = params
    self_mask = (segments[:, None] == segments[None, :]) & (segments[:, None] != 0) & (positions[None, :] <= positions[:, None])
    cross_mask = (segments[:, None] == source_segments[None, :]) & (segments[:, None] != 0)
    normed_one = low(layer_norm(inputs, gains[0], shifts[0]))
    query_self = low(low_back(product(normed_one, w_in[0, 0]) + biases[0]))
    key_self = low(low_back(product(normed_one, w_in[0, 1])))
    value_self = low(low_back(product(normed_one, w_in[0, 2]) + biases[1]))
    self_out = low(low_back(attention(query_self, key_self, value_self, self_mask)))
    after_self = inputs + low_back(product(self_out, w_out[0]) + biases[2])
    normed_two = low(layer_norm(after_self, gains[1], shifts[1]))
    query_cross = low(low_back(product(normed_two, w_in[1, 0]) + biases[3]))
    key_cross = low(low_back(product(sources, w_in[1, 1])))
    value_cross = low(low_back(product(sources, w_in[1, 2]) + biases[4]))
    cross_out = low(low_back(attention(query_cross, key_cross, value_cross, cross_mask)))
    after_cross = after_self + low_back(product(cross_out, w_out[1]) + biases[5])
    normed_three = low(layer_norm(after_cross, gains[2], shifts[2]))
    pre_act = low_back(product(normed_three, w_up) + up_bias)
    activated = low(jax.nn.gelu(pre_act, approximate=True))
    return after_cross + low_back(product(activated, w_down) + biases[6])

def reference(hidden_in, memory, out_grad, segment_ids, memory_segments, deal, attn_in, attn_out, fc1, fc2, proj_bias, fc1_bias, norm_gain, norm_bias):
    half_rows = TOK_DEV // 2
    positions = (deal[:, None].astype(jnp.int32) * half_rows + jnp.arange(half_rows, dtype=jnp.int32)[None, :]).reshape(-1).astype(jnp.int32)
    params = (attn_in, attn_out, fc1, fc2, proj_bias, fc1_bias, norm_gain, norm_bias)

    def forward(weights, inputs, sources):
        lowered = jax.tree.map(low, weights)

        def group_step(group_item):
            return one_group(lowered, group_item[0], group_item[1], group_item[2], group_item[3], positions)
        return lax.map(jax.checkpoint(group_step), (inputs, sources, segment_ids, memory_segments))
    result, pullback = jax.vjp(forward, params, hidden_in.astype(jnp.float32), memory.astype(jnp.float32))
    grad_params, grad_inputs, grad_sources = pullback(out_grad.astype(jnp.float32))
    return (result.astype(jnp.bfloat16), grad_inputs, grad_sources, grad_params[0], grad_params[1], grad_params[2], grad_params[3], grad_params[4], grad_params[5], grad_params[6], grad_params[7])
```

```python
import math

import jax
import jax.numpy as jnp
from jax import lax
from jax.sharding import Mesh
from jax.sharding import PartitionSpec as P

HEADS = 16
EPSILON = 1e-05
NEGATIVE = -1e30
GELU_IN = math.sqrt(2.0 / math.pi)
GELU_CUBE = 0.044715
SEQ = ("y", "core")
FSDP = ("z", "x")
PLANE = ("y", "core", "x")
ALL = ("y", "core", "z", "x")
BF = jnp.bfloat16
F32 = jnp.float32


def matmul(left, right):
    return jnp.dot(left, right, preferred_element_type=F32)


def contract_rows(left, right):
    return lax.dot_general(left, right, (((0,), (0,)), ((), ())), preferred_element_type=F32)


def times_transpose(left, right):
    return lax.dot_general(left, right, (((1,), (1,)), ((), ())), preferred_element_type=F32)


def column_sums(values):
    return jnp.sum(values.astype(F32), axis=0)


def swap(value, axis, step):
    return lax.ppermute(value, axis, [(i, i ^ step) for i in range(lax.axis_size(axis))])


def norm_parts(values):
    centred = values - jnp.mean(values, axis=-1, keepdims=True)
    scale = lax.rsqrt(jnp.mean(centred * centred, axis=-1, keepdims=True) + EPSILON)
    return centred * scale, scale


def norm_back(normed, scale, gain, grad):
    inner = grad * gain
    means = jnp.mean(inner, axis=-1, keepdims=True)
    along = jnp.mean(inner * normed, axis=-1, keepdims=True)
    return (
        scale * (inner - means - normed * along),
        jnp.sum(grad * normed, axis=0),
        jnp.sum(grad, axis=0),
    )


def heads_first(values):
    return values.reshape(values.shape[0], HEADS, -1).transpose(1, 0, 2)


def heads_last(values):
    return values.transpose(1, 0, 2).reshape(values.shape[1], -1)


def batched(left, right, left_dim, right_dim):
    return lax.dot_general(
        left, right, (((left_dim,), (right_dim,)), ((0,), (0,))), preferred_element_type=F32
    )


def attend(queries, keys, values, allowed):
    score_scale = 1.0 / math.sqrt(queries.shape[2])
    scores = jnp.where(allowed[None], batched(queries, keys, 2, 2) * score_scale, NEGATIVE)
    top = jnp.max(scores, axis=-1, keepdims=True)
    raised = jnp.where(allowed[None], jnp.exp(scores - top), 0.0)
    chance = raised / jnp.maximum(jnp.sum(raised, axis=-1, keepdims=True), 1.0)
    return batched(chance.astype(BF), values, 2, 1), chance


def attend_back(queries, keys, values, chance, grad):
    score_scale = 1.0 / math.sqrt(queries.shape[2])
    chance_grad = batched(grad, values, 2, 2)
    delta = jnp.sum(chance * chance_grad, axis=-1, keepdims=True)
    score_grad = (chance * (chance_grad - delta)).astype(BF)
    return (
        batched(score_grad, keys, 2, 1) * score_scale,
        batched(score_grad, queries, 1, 1) * score_scale,
        batched(chance.astype(BF), grad, 1, 1),
    )


def body(
    hidden_in,
    memory,
    out_grad,
    segment_ids,
    memory_segments,
    deal,
    attn_in,
    attn_out,
    fc1,
    fc2,
    proj_bias,
    fc1_bias,
    norm_gain,
    norm_bias,
):
    y_size, z_size, x_size = lax.axis_size("y"), lax.axis_size("z"), lax.axis_size("x")
    s_size, f_size = y_size * 2, z_size * x_size
    y_place, core_place = lax.axis_index("y"), lax.axis_index("core")
    z_place = lax.axis_index("z")
    s_place = y_place * 2 + core_place
    f_place = z_place * x_size + lax.axis_index("x")
    place = s_place * f_size + f_place
    count = s_size * f_size
    tokens, width = hidden_in.shape[1:]
    sources_len = memory.shape[1]
    held = attn_in.shape[2]
    share = held // s_size

    wi_share = lax.dynamic_slice_in_dim(attn_in, s_place * share, share, 2).astype(BF)
    wo_share = lax.dynamic_slice_in_dim(attn_out, s_place * share, share, 1).astype(BF)
    small = jnp.concatenate(
        [
            proj_bias.reshape(-1).astype(BF),
            norm_gain.reshape(-1).astype(BF),
            norm_bias.reshape(-1).astype(BF),
            fc1_bias.astype(BF),
            segment_ids.reshape(-1).astype(BF),
            memory_segments.reshape(-1).astype(BF),
        ]
    )
    small_rows = -(-small.shape[0] // (16 * width)) * 16
    small = jnp.pad(small, (0, small_rows * width - small.shape[0])).reshape(small_rows, width)
    first = jnp.concatenate([wi_share[0].reshape(3 * share, width), small])
    second = jnp.concatenate([wi_share[1].reshape(3 * share, width), wo_share.reshape(2 * share, width)])
    first = lax.all_gather(first, ALL)
    second = lax.all_gather(second, ALL)

    def in_order(gathered, number):
        parts = gathered.reshape(s_size, f_size, number, share, width)
        return parts.transpose(2, 1, 0, 3, 4).reshape(number, width, width)

    w_self = in_order(first[:, : 3 * share], 3)
    w_rest = in_order(second, 5)
    small = first[:, 3 * share :].reshape(s_size, f_size, small_rows * width)
    by_fsdp = small[0]
    lane = width // f_size

    def columns(start, number):
        part = by_fsdp[:, start : start + number * lane].reshape(f_size, number, lane)
        return part.transpose(1, 0, 2).reshape(number, width).astype(F32)

    biases = columns(0, 7)
    gains = columns(7 * lane, 3)
    shifts = columns(10 * lane, 3)
    up_bias = by_fsdp[:, 13 * lane : 13 * lane + fc1_bias.shape[0]].reshape(-1).astype(F32)
    seg_start = 13 * lane + fc1_bias.shape[0]
    segs = lax.dynamic_index_in_dim(
        small[:, :, seg_start : seg_start + tokens + sources_len], f_place, 1, keepdims=False
    ).astype(jnp.int32)

    unit = fc2.shape[0] // s_size
    down_share = lax.dynamic_slice_in_dim(fc2, s_place * unit, unit, 0).astype(BF)
    down_share = lax.ppermute(
        down_share,
        ALL,
        [(s * f_size + f, f * s_size + s) for s in range(s_size) for f in range(f_size)],
    )
    w_down = lax.all_gather(down_share, PLANE, axis=0, tiled=True)
    up_share = lax.dynamic_slice_in_dim(fc1, s_place * share, share, 0).astype(BF)
    up_share = up_share.reshape(share, s_size, z_size, x_size, unit).transpose(2, 0, 1, 3, 4)
    hidden = s_size * x_size * unit
    up_share = up_share.reshape(z_size, share, hidden)
    up_parts = jnp.stack(
        [
            swap(lax.dynamic_index_in_dim(up_share, z_place ^ k, 0, keepdims=False), "z", k)
            if k
            else lax.dynamic_index_in_dim(up_share, z_place, 0, keepdims=False)
            for k in range(z_size)
        ]
    )
    up_parts = jnp.stack(
        [
            lax.dynamic_index_in_dim(up_parts, z_place ^ j, 0, keepdims=False)
            for j in range(z_size)
        ]
    )
    w_up = lax.all_gather(up_parts, PLANE).reshape(s_size, x_size, z_size, share, hidden)
    w_up = w_up.transpose(2, 1, 0, 3, 4).reshape(width, hidden)
    up_bias = lax.dynamic_index_in_dim(
        up_bias.reshape(s_size, z_size, x_size * unit), z_place, 1, keepdims=False
    ).reshape(hidden)

    down_grad = out_grad[0]
    down_all = jnp.concatenate([down_grad] + [swap(down_grad, "z", k) for k in range(1, z_size)])

    half_rows = tokens // 2
    offsets = jnp.arange(half_rows, dtype=jnp.int32)
    owners = jnp.stack([(y_place ^ k) * 2 + (core_place ^ c) for k in range(y_size) for c in range(2)])
    deal_pairs = deal.reshape(s_size, 2)
    key_pos = (deal_pairs[owners][:, :, None] * half_rows + offsets).reshape(-1)
    key_seg = segs[owners][:, :tokens].reshape(-1)
    query_pos = key_pos[:tokens]
    query_seg = segment_ids[0]
    source_seg = segs[:, tokens:].reshape(-1)
    real = query_seg[:, None] != 0
    self_allowed = (
        (query_seg[:, None] == key_seg[None]) & real & (key_pos[None] <= query_pos[:, None])
    )
    cross_allowed = (query_seg[:, None] == source_seg[None]) & real

    inputs = hidden_in[0].astype(F32)
    sources = memory[0]
    unit_one, scale_one = norm_parts(inputs)
    normed_one = (unit_one * gains[0] + shifts[0]).astype(BF)
    query_self = (matmul(normed_one, w_self[0]) + biases[0]).astype(BF)
    pair = jnp.concatenate(
        [
            matmul(normed_one, w_self[1]).astype(BF),
            (matmul(normed_one, w_self[2]) + biases[1]).astype(BF),
        ],
        axis=1,
    )
    pairs = []
    for k in range(y_size):
        mine = swap(pair, "y", k) if k else pair
        pairs += [mine, swap(mine, "core", 1)]
    pair_all = jnp.concatenate(pairs)
    query_heads = heads_first(query_self)
    key_heads = heads_first(pair_all[:, :width])
    value_heads = heads_first(pair_all[:, width:])
    self_mixed, self_chance = attend(query_heads, key_heads, value_heads, self_allowed)
    self_out = heads_last(self_mixed).astype(BF)
    after_self = inputs + matmul(self_out, w_rest[3]) + biases[2]

    source_pair = jnp.concatenate(
        [
            matmul(sources, w_rest[1]).astype(BF),
            (matmul(sources, w_rest[2]) + biases[4]).astype(BF),
        ],
        axis=1,
    )
    source_all = lax.all_gather(source_pair, SEQ, axis=0, tiled=True)
    unit_two, scale_two = norm_parts(after_self)
    normed_two = (unit_two * gains[1] + shifts[1]).astype(BF)
    query_cross = (matmul(normed_two, w_rest[0]) + biases[3]).astype(BF)
    query_cross_heads = heads_first(query_cross)
    source_key_heads = heads_first(source_all[:, :width])
    source_value_heads = heads_first(source_all[:, width:])
    cross_mixed, cross_chance = attend(
        query_cross_heads, source_key_heads, source_value_heads, cross_allowed
    )
    cross_out = heads_last(cross_mixed).astype(BF)
    after_cross = after_self + matmul(cross_out, w_rest[4]) + biases[5]

    unit_three, scale_three = norm_parts(after_cross)
    normed_three = (unit_three * gains[2] + shifts[2]).astype(BF)
    normed_all = jnp.concatenate(
        [normed_three] + [swap(normed_three, "z", k) for k in range(1, z_size)]
    )
    pre_act = matmul(normed_all, w_up) + up_bias
    bent = jnp.tanh(GELU_IN * (pre_act + GELU_CUBE * pre_act * pre_act * pre_act))
    activated = (0.5 * pre_act * (1.0 + bent)).astype(BF)
    slope = 0.5 * (1.0 + bent) + 0.5 * pre_act * (1.0 - bent * bent) * GELU_IN * (
        1.0 + 3.0 * GELU_CUBE * pre_act * pre_act
    )
    pre_grad = (times_transpose(down_all, w_down) * slope).astype(BF)

    def to_owners(partial):
        parts = partial.reshape(z_size, tokens, width)
        total = parts[0]
        for k in range(1, z_size):
            total = total + swap(parts[k].astype(BF), "z", k).astype(F32)
        return total

    normed_grad_three = to_owners(times_transpose(pre_grad, w_up))
    result = after_cross + to_owners(matmul(activated, w_down)) + biases[6]
    grad_up = contract_rows(normed_all, pre_grad).astype(BF)
    grad_down = contract_rows(activated, down_all).astype(BF)
    up_rows = width // count
    grad_up = grad_up.reshape(s_size, z_size, x_size, up_rows, hidden).transpose(0, 2, 1, 3, 4)
    grad_up = lax.psum_scatter(
        grad_up.reshape(s_size * x_size, z_size, up_rows, hidden), PLANE, scatter_dimension=0
    )
    grad_down = lax.psum_scatter(grad_down, PLANE, scatter_dimension=0, tiled=True).astype(F32)
    grad_up = jnp.stack(
        [
            swap(lax.dynamic_index_in_dim(grad_up, z_place ^ k, 0, keepdims=False), "z", k)
            if k
            else lax.dynamic_index_in_dim(grad_up, z_place, 0, keepdims=False)
            for k in range(z_size)
        ]
    )
    grad_up = jnp.stack(
        [lax.dynamic_index_in_dim(grad_up, z_place ^ j, 0, keepdims=False) for j in range(z_size)]
    )
    grad_up = grad_up.reshape(z_size, up_rows, s_size, x_size, unit).transpose(1, 2, 0, 3, 4)
    grad_up = grad_up.reshape(up_rows, -1).astype(F32)
    grad_up_bias = column_sums(pre_grad)

    result_grad = down_grad.astype(F32)
    moved, gain_three, shift_three = norm_back(unit_three, scale_three, gains[2], normed_grad_three)
    after_grad = result_grad + moved
    cross_branch = after_grad.astype(BF)
    cross_head_grad = times_transpose(cross_branch, w_rest[4]).astype(BF)
    query_cross_grad, source_key_grad, source_value_grad = attend_back(
        query_cross_heads,
        source_key_heads,
        source_value_heads,
        cross_chance,
        heads_first(cross_head_grad),
    )
    query_cross_grad = heads_last(query_cross_grad).astype(BF)
    source_grad = jnp.concatenate([heads_last(source_key_grad), heads_last(source_value_grad)], axis=1)
    source_grad = lax.psum_scatter(source_grad.astype(BF), SEQ, scatter_dimension=0, tiled=True)
    grad_memory = times_transpose(source_grad[:, :width], w_rest[1]) + times_transpose(
        source_grad[:, width:], w_rest[2]
    )
    normed_grad_two = times_transpose(query_cross_grad, w_rest[0])
    moved, gain_two, shift_two = norm_back(unit_two, scale_two, gains[1], normed_grad_two)
    self_grad = after_grad + moved

    def to_shares(grads):
        parts = [g.astype(BF).reshape(s_size, z_size, x_size, up_rows, width) for g in grads]
        parts = jnp.stack(parts, axis=3).transpose(0, 2, 1, 3, 4, 5)
        parts = parts.reshape(s_size * x_size, z_size, len(grads) * up_rows, width)
        parts = lax.psum_scatter(parts, PLANE, scatter_dimension=0)
        parts = lax.psum_scatter(parts, "z", scatter_dimension=0)
        return parts.reshape(len(grads), up_rows, width).astype(F32)

    cross_shares = to_shares(
        [
            contract_rows(normed_two, query_cross_grad),
            contract_rows(sources, source_grad[:, :width]),
            contract_rows(sources, source_grad[:, width:]),
            contract_rows(cross_out, cross_branch),
        ]
    )

    self_branch = self_grad.astype(BF)
    self_head_grad = times_transpose(self_branch, w_rest[3]).astype(BF)
    query_self_grad, key_grad, value_grad = attend_back(
        query_heads, key_heads, value_heads, self_chance, heads_first(self_head_grad)
    )
    query_self_grad = heads_last(query_self_grad).astype(BF)
    pair_grad = jnp.concatenate([heads_last(key_grad), heads_last(value_grad)], axis=1).astype(BF)
    pair_grad = pair_grad.reshape(y_size, 2, tokens, 2 * width)
    pair_grad = pair_grad[:, 0].astype(F32) + swap(pair_grad[:, 1], "core", 1).astype(F32)
    pair_sum = pair_grad[0]
    for k in range(1, y_size):
        pair_sum = pair_sum + swap(pair_grad[k].astype(BF), "y", k).astype(F32)
    key_self_grad = pair_sum[:, :width].astype(BF)
    value_self_grad = pair_sum[:, width:].astype(BF)
    self_shares = to_shares(
        [
            contract_rows(normed_one, query_self_grad),
            contract_rows(normed_one, key_self_grad),
            contract_rows(normed_one, value_self_grad),
            contract_rows(self_out, self_branch),
        ]
    )
    normed_grad_one = (
        times_transpose(query_self_grad, w_self[0])
        + times_transpose(key_self_grad, w_self[1])
        + times_transpose(value_self_grad, w_self[2])
    )
    moved, gain_one, shift_one = norm_back(unit_one, scale_one, gains[0], normed_grad_one)
    grad_hidden = self_grad + moved

    rows = [
        column_sums(query_self_grad),
        column_sums(value_self_grad),
        column_sums(self_branch),
        column_sums(query_cross_grad),
        column_sums(source_grad[:, width:]),
        column_sums(cross_branch),
        column_sums(down_grad),
        gain_one,
        gain_two,
        gain_three,
        shift_one,
        shift_two,
        shift_three,
    ]
    spread = jnp.zeros((s_size, z_size, x_size * unit), F32)
    spread = lax.dynamic_update_slice_in_dim(
        spread, grad_up_bias.reshape(s_size, 1, x_size * unit), z_place, 1
    )
    vector = lax.psum(jnp.concatenate(rows + [spread.reshape(-1)]), ALL)
    table = lax.dynamic_index_in_dim(
        vector[: len(rows) * width].reshape(len(rows), count, up_rows), place, 1, keepdims=False
    )
    grad_up_bias = lax.dynamic_slice_in_dim(vector[len(rows) * width :], place * unit, unit)
    return (
        result.astype(BF)[None],
        grad_hidden[None],
        grad_memory[None],
        jnp.stack([self_shares[:3], cross_shares[:3]]),
        jnp.stack([self_shares[3], cross_shares[3]]),
        grad_up,
        grad_down,
        table[:7],
        grad_up_bias,
        table[7:10],
        table[10:13],
    )


def solution(mesh):
    seq, fsdp = mesh.shape["seq"], mesh.shape["fsdp"]
    split = Mesh(mesh.devices.reshape(seq // 2, 2, 4, fsdp // 4), ALL)
    placed = (
        P(FSDP, SEQ, None),
        P(FSDP, SEQ, None),
        P(FSDP, SEQ, None),
        P(FSDP, SEQ),
        P(FSDP, SEQ),
        P(),
        P(None, None, FSDP, None),
        P(None, FSDP, None),
        P(FSDP, None),
        P(FSDP, None),
        P(None, FSDP),
        P(FSDP),
        P(None, FSDP),
        P(None, FSDP),
    )
    return jax.shard_map(
        body,
        mesh=split,
        in_specs=placed,
        out_specs=(
            P(FSDP, SEQ, None),
            P(FSDP, SEQ, None),
            P(FSDP, SEQ, None),
            P(None, None, ALL, None),
            P(None, ALL, None),
            P(ALL, None),
            P(ALL, None),
            P(None, ALL),
            P(ALL),
            P(None, ALL),
            P(None, ALL),
        ),
        check_vma=False,
    )
```

```python
import math

import jax
import jax.numpy as jnp
from jax import lax
from jax.sharding import Mesh
from jax.sharding import PartitionSpec as P

HEADS = 16
EPSILON = 1e-05
NEGATIVE = -1e30
GELU_IN = math.sqrt(2.0 / math.pi)
GELU_CUBE = 0.044715
SEQ = ("y", "core")
FSDP = ("z", "x")
PLANE = ("y", "core", "x")
ALL = ("y", "core", "z", "x")
BF = jnp.bfloat16
F32 = jnp.float32


def matmul(left, right):
    return jnp.dot(left, right, preferred_element_type=F32)


def contract_rows(left, right):
    return lax.dot_general(left, right, (((0,), (0,)), ((), ())), preferred_element_type=F32)


def times_transpose(left, right):
    return lax.dot_general(left, right, (((1,), (1,)), ((), ())), preferred_element_type=F32)


def column_sums(values):
    return jnp.sum(values.astype(F32), axis=0)


def swap(value, axis, step):
    return lax.ppermute(value, axis, [(i, i ^ step) for i in range(lax.axis_size(axis))])


def norm_parts(values):
    centred = values - jnp.mean(values, axis=-1, keepdims=True)
    scale = lax.rsqrt(jnp.mean(centred * centred, axis=-1, keepdims=True) + EPSILON)
    return centred * scale, scale


def norm_back(normed, scale, gain, grad):
    inner = grad * gain
    means = jnp.mean(inner, axis=-1, keepdims=True)
    along = jnp.mean(inner * normed, axis=-1, keepdims=True)
    return (
        scale * (inner - means - normed * along),
        jnp.sum(grad * normed, axis=0),
        jnp.sum(grad, axis=0),
    )


def heads_first(values, heads):
    return values.reshape(values.shape[0], heads, -1).transpose(1, 0, 2)


def heads_last(values):
    return values.transpose(1, 0, 2).reshape(values.shape[1], -1)


def batched(left, right, left_dim, right_dim):
    return lax.dot_general(
        left, right, (((left_dim,), (right_dim,)), ((0,), (0,))), preferred_element_type=F32
    )


def attend(queries, keys, values, allowed):
    score_scale = 1.0 / math.sqrt(queries.shape[2])
    scores = jnp.where(allowed[None], batched(queries, keys, 2, 2) * score_scale, NEGATIVE)
    top = jnp.max(scores, axis=-1, keepdims=True)
    raised = jnp.where(allowed[None], jnp.exp(scores - top), 0.0)
    chance = raised / jnp.maximum(jnp.sum(raised, axis=-1, keepdims=True), 1.0)
    return batched(chance.astype(BF), values, 2, 1), chance


def attend_back(queries, keys, values, chance, grad):
    score_scale = 1.0 / math.sqrt(queries.shape[2])
    chance_grad = batched(grad, values, 2, 2)
    delta = jnp.sum(chance * chance_grad, axis=-1, keepdims=True)
    score_grad = (chance * (chance_grad - delta)).astype(BF)
    return (
        batched(score_grad, keys, 2, 1) * score_scale,
        batched(score_grad, queries, 1, 1) * score_scale,
        batched(chance.astype(BF), grad, 1, 1),
    )


def gather_seq(value):
    lines = [value] + [swap(value, "y", k) for k in range(1, lax.axis_size("y"))]
    lines = jnp.concatenate(lines) if len(lines) > 1 else value
    return jnp.concatenate([lines, swap(lines, "core", 1)])


def scatter_seq(partial):
    line = partial[0].astype(F32) + swap(partial[1].astype(BF), "core", 1).astype(F32)
    total = line[0]
    for k in range(1, lax.axis_size("y")):
        total = total + swap(line[k].astype(BF), "y", k).astype(F32)
    return total


def exchange_seq(value):
    line = jnp.stack([value[0], swap(value[1], "core", 1)])
    lines = [line[:, 0]] + [swap(line[:, k], "y", k) for k in range(1, lax.axis_size("y"))]
    return jnp.stack(lines, axis=1)


def pick(value, at, axis=0):
    return lax.dynamic_index_in_dim(value, at, axis, keepdims=False)


def body(
    hidden_in,
    memory,
    out_grad,
    segment_ids,
    memory_segments,
    deal,
    attn_in,
    attn_out,
    fc1,
    fc2,
    proj_bias,
    fc1_bias,
    norm_gain,
    norm_bias,
):
    y_size, z_size, x_size = lax.axis_size("y"), lax.axis_size("z"), lax.axis_size("x")
    s_size, f_size = y_size * 2, z_size * x_size
    y_place, core_place = lax.axis_index("y"), lax.axis_index("core")
    z_place, x_place = lax.axis_index("z"), lax.axis_index("x")
    s_place = y_place * 2 + core_place
    f_place = z_place * x_size + x_place
    place = s_place * f_size + f_place
    count = s_size * f_size
    tokens, width = hidden_in.shape[1:]
    sources_len = memory.shape[1]
    held = attn_in.shape[2]
    share = held // s_size
    lane = width // f_size
    cut = width // s_size
    row_len = s_size * tokens
    blocks = [(c, k) for c in range(2) for k in range(y_size)]
    block_of = [((j % 2) ^ core_place) * y_size + ((j // 2) ^ y_place) for j in range(s_size)]
    owners = jnp.stack([(y_place ^ k) * 2 + (core_place ^ c) for c, k in blocks])

    def cut_cols(value, at):
        return lax.dynamic_slice_in_dim(value, at * cut, cut, value.ndim - 1)

    small = jnp.concatenate(
        [
            proj_bias.reshape(-1).astype(BF),
            norm_gain.reshape(-1).astype(BF),
            norm_bias.reshape(-1).astype(BF),
            fc1_bias.astype(BF),
        ]
    )
    small_len = small.shape[0]
    small_rows = -(-small_len // (16 * cut)) * 16
    small = jnp.pad(small, (0, small_rows * cut - small_len)).reshape(small_rows, cut)
    early = jnp.concatenate([cut_cols(attn_in[0], s_place).astype(BF).reshape(3 * held, cut), small])
    early = jnp.stack([early] + [swap(early, "x", k) for k in range(1, x_size)])
    early = jnp.stack([early] + [swap(early, "z", k) for k in range(1, z_size)])
    early = early.reshape((f_size,) + early.shape[2:])
    early = jnp.stack(
        [
            pick(early, ((j // x_size) ^ z_place) * x_size + ((j % x_size) ^ x_place))
            for j in range(f_size)
        ]
    )
    w_self = early[:, : 3 * held].reshape(f_size, 3, held, cut).transpose(1, 0, 2, 3)
    w_self = w_self.reshape(3, width, cut)
    by_fsdp = early[:, 3 * held :].reshape(f_size, small_rows * cut)

    def columns(start, number):
        part = by_fsdp[:, start : start + number * lane].reshape(f_size, number, lane)
        return part.transpose(1, 0, 2).reshape(number, width).astype(F32)

    biases = columns(0, 7)
    gains = columns(7 * lane, 3)
    shifts = columns(10 * lane, 3)
    up_bias = by_fsdp[:, 13 * lane : small_len].reshape(-1).astype(F32)

    wi_share = lax.dynamic_slice_in_dim(attn_in[1], s_place * share, share, 1).astype(BF)
    wo_share = lax.dynamic_slice_in_dim(attn_out, s_place * share, share, 1).astype(BF)
    rest = jnp.concatenate([wi_share.reshape(3 * share, width), wo_share.reshape(2 * share, width)])
    rest = lax.all_gather(rest, ALL)
    w_rest = rest.reshape(s_size, f_size, 5, share, width).transpose(2, 1, 0, 3, 4)
    w_rest = w_rest.reshape(5, width, width)

    unit = fc2.shape[0] // s_size
    hidden = s_size * x_size * unit
    down_share = lax.dynamic_slice_in_dim(fc2, s_place * unit, unit, 0).astype(BF)
    down_share = lax.ppermute(
        down_share,
        ALL,
        [(s * f_size + f, f * s_size + s) for s in range(s_size) for f in range(f_size)],
    )
    up_share = lax.dynamic_slice_in_dim(fc1, s_place * share, share, 0).astype(BF)
    up_share = up_share.reshape(share, s_size, z_size, x_size, unit).transpose(2, 0, 1, 3, 4)
    up_share = up_share.reshape(z_size, share, hidden)
    up_parts = jnp.stack(
        [swap(pick(up_share, z_place ^ k), "z", k) if k else pick(up_share, z_place) for k in range(z_size)]
    )
    up_parts = jnp.stack([pick(up_parts, z_place ^ j) for j in range(z_size)])
    mlp_share = jnp.concatenate(
        [up_parts.reshape(z_size * share, hidden), down_share.reshape(-1, hidden)]
    )
    mlp_share, _ = lax.optimization_barrier((mlp_share, rest))
    w_mlp = lax.all_gather(mlp_share, PLANE)
    w_up = w_mlp[:, : z_size * share].reshape(s_size, x_size, z_size, share, hidden)
    w_up = w_up.transpose(2, 1, 0, 3, 4).reshape(width, hidden)
    w_down = w_mlp[:, z_size * share :].reshape(hidden, width)
    up_bias = pick(up_bias.reshape(s_size, z_size, x_size * unit), z_place, 1).reshape(hidden)

    down_grad = out_grad[0]
    down_all = jnp.concatenate([down_grad] + [swap(down_grad, "z", k) for k in range(1, z_size)])

    labels = jnp.concatenate([segment_ids[0], memory_segments[0]]).astype(BF)
    label_rows = -(-labels.shape[0] // (16 * width)) * 16
    labels = jnp.pad(labels, (0, label_rows * width - labels.shape[0])).reshape(label_rows, width)
    row = gather_seq(jnp.concatenate([hidden_in[0], memory[0], labels]))
    row = row.reshape(s_size, tokens + sources_len + label_rows, width)
    row_inputs = row[:, :tokens].reshape(row_len, width).astype(F32)
    labels = row[:, tokens + sources_len :].reshape(s_size, label_rows * width).astype(jnp.int32)
    row_seg = labels[:, :tokens].reshape(-1)
    row_sources = jnp.concatenate(
        [pick(row, block_of[j])[tokens : tokens + sources_len] for j in range(s_size)]
    )
    source_seg = jnp.concatenate(
        [pick(labels, block_of[j])[tokens : tokens + sources_len] for j in range(s_size)]
    )
    half_rows = tokens // 2
    offsets = jnp.arange(half_rows, dtype=jnp.int32)
    row_pos = (deal.reshape(s_size, 2)[owners][:, :, None] * half_rows + offsets).reshape(-1)
    real = row_seg[:, None] != 0
    self_allowed = (row_seg[:, None] == row_seg[None]) & real & (row_pos[None] <= row_pos[:, None])
    cross_allowed = (segment_ids[0][:, None] == source_seg[None]) & (segment_ids[0][:, None] != 0)

    heads = HEADS // s_size
    unit_row, _ = norm_parts(row_inputs)
    normed_row = (unit_row * gains[0] + shifts[0]).astype(BF)
    query_self = (matmul(normed_row, w_self[0]) + cut_cols(biases[0], s_place)).astype(BF)
    key_self = matmul(normed_row, w_self[1]).astype(BF)
    value_self = (matmul(normed_row, w_self[2]) + cut_cols(biases[1], s_place)).astype(BF)
    query_heads = heads_first(query_self, heads)
    key_heads = heads_first(key_self, heads)
    value_heads = heads_first(value_self, heads)
    self_mixed, self_chance = attend(query_heads, key_heads, value_heads, self_allowed)
    self_cut = heads_last(self_mixed).astype(BF)
    self_out = exchange_seq(self_cut.reshape(2, y_size, tokens, cut)).reshape(s_size, tokens, cut)
    self_out = jnp.concatenate([pick(self_out, block_of[j]) for j in range(s_size)], axis=1)
    inputs = hidden_in[0].astype(F32)
    after_self = inputs + matmul(self_out, w_rest[3]) + biases[2]

    source_key = matmul(row_sources, cut_cols(w_rest[1], s_place)).astype(BF)
    source_value = matmul(row_sources, cut_cols(w_rest[2], s_place)) + cut_cols(biases[4], s_place)
    source_pair = jnp.stack([source_key, source_value.astype(BF)])
    sources_row = s_size * sources_len
    source_all = gather_seq(source_pair[None]).reshape(s_size, 2, sources_row, cut)
    source_all = jnp.stack([pick(source_all, block_of[j]) for j in range(s_size)])
    source_all = source_all.reshape(s_size, 2, sources_row, heads, cut // heads)
    source_all = source_all.transpose(1, 0, 3, 2, 4).reshape(2, HEADS, sources_row, cut // heads)
    source_key_heads, source_value_heads = source_all[0], source_all[1]
    unit_two, scale_two = norm_parts(after_self)
    normed_two = (unit_two * gains[1] + shifts[1]).astype(BF)
    query_cross = (matmul(normed_two, w_rest[0]) + biases[3]).astype(BF)
    query_cross_heads = heads_first(query_cross, HEADS)
    cross_mixed, cross_chance = attend(
        query_cross_heads, source_key_heads, source_value_heads, cross_allowed
    )
    cross_out = heads_last(cross_mixed).astype(BF)
    after_cross = after_self + matmul(cross_out, w_rest[4]) + biases[5]

    unit_three, scale_three = norm_parts(after_cross)
    normed_three = (unit_three * gains[2] + shifts[2]).astype(BF)
    normed_all = jnp.concatenate(
        [normed_three] + [swap(normed_three, "z", k) for k in range(1, z_size)]
    )
    pre_act = matmul(normed_all, w_up) + up_bias
    bent = jnp.tanh(GELU_IN * (pre_act + GELU_CUBE * pre_act * pre_act * pre_act))
    activated = (0.5 * pre_act * (1.0 + bent)).astype(BF)
    slope = 0.5 * (1.0 + bent) + 0.5 * pre_act * (1.0 - bent * bent) * GELU_IN * (
        1.0 + 3.0 * GELU_CUBE * pre_act * pre_act
    )
    pre_grad = (times_transpose(down_all, w_down) * slope).astype(BF)

    def to_owners(partial):
        parts = partial.reshape(z_size, tokens, width)
        total = parts[0]
        for k in range(1, z_size):
            total = total + swap(parts[k].astype(BF), "z", k).astype(F32)
        return total

    normed_grad_three = to_owners(times_transpose(pre_grad, w_up))
    result = after_cross + to_owners(matmul(activated, w_down)) + biases[6]
    grad_up = contract_rows(normed_all, pre_grad).astype(BF)
    grad_down = contract_rows(activated, down_all).astype(BF)
    up_rows = width // count
    grad_up = grad_up.reshape(s_size, z_size, x_size, up_rows, hidden).transpose(0, 2, 1, 3, 4)
    grad_up = lax.psum_scatter(
        grad_up.reshape(s_size * x_size, z_size, up_rows, hidden), PLANE, scatter_dimension=0
    )
    grad_down = lax.psum_scatter(grad_down, PLANE, scatter_dimension=0, tiled=True).astype(F32)
    grad_up = jnp.stack(
        [swap(pick(grad_up, z_place ^ k), "z", k) if k else pick(grad_up, z_place) for k in range(z_size)]
    )
    grad_up = jnp.stack([pick(grad_up, z_place ^ j) for j in range(z_size)])
    grad_up = grad_up.reshape(z_size, up_rows, s_size, x_size, unit).transpose(1, 2, 0, 3, 4)
    grad_up = grad_up.reshape(up_rows, -1).astype(F32)
    grad_up_bias = column_sums(pre_grad)

    result_grad = down_grad.astype(F32)
    moved, gain_three, shift_three = norm_back(unit_three, scale_three, gains[2], normed_grad_three)
    after_grad = result_grad + moved
    cross_branch = after_grad.astype(BF)
    cross_head_grad = times_transpose(cross_branch, w_rest[4]).astype(BF)
    query_cross_grad, source_key_grad, source_value_grad = attend_back(
        query_cross_heads,
        source_key_heads,
        source_value_heads,
        cross_chance,
        heads_first(cross_head_grad, HEADS),
    )
    query_cross_grad = heads_last(query_cross_grad).astype(BF)
    normed_grad_two = times_transpose(query_cross_grad, w_rest[0])
    moved, gain_two, shift_two = norm_back(unit_two, scale_two, gains[1], normed_grad_two)
    self_grad = after_grad + moved

    self_branch = self_grad.astype(BF)
    branch_row = gather_seq(self_branch)
    wo_rows = lax.dynamic_slice_in_dim(w_rest[3], s_place * cut, cut, 0)
    self_head_grad = times_transpose(branch_row, wo_rows).astype(BF)
    query_grad, key_grad, value_grad = attend_back(
        query_heads, key_heads, value_heads, self_chance, heads_first(self_head_grad, heads)
    )
    query_grad = heads_last(query_grad).astype(BF)
    key_grad = heads_last(key_grad).astype(BF)
    value_grad = heads_last(value_grad).astype(BF)
    normed_grad_one = (
        times_transpose(query_grad, w_self[0])
        + times_transpose(key_grad, w_self[1])
        + times_transpose(value_grad, w_self[2])
    )
    normed_grad_one = scatter_seq(normed_grad_one.reshape(2, y_size, tokens, width))
    unit_one, scale_one = norm_parts(inputs)
    moved, gain_one, shift_one = norm_back(unit_one, scale_one, gains[0], normed_grad_one)
    grad_hidden = self_grad + moved

    source_grad = jnp.concatenate([source_key_grad, source_value_grad], axis=2).astype(BF)
    source_grad = source_grad.reshape(s_size, heads, sources_row, 2, cut // heads)
    source_grad = source_grad.transpose(0, 3, 2, 1, 4).reshape(s_size, 2, sources_row, cut)
    source_grad = jnp.stack([pick(source_grad, owners[j]) for j in range(s_size)])
    source_grad = scatter_seq(source_grad.reshape(2, y_size, 2, sources_row, cut)).astype(BF)
    grad_memory = times_transpose(source_grad[0], cut_cols(w_rest[1], s_place)) + times_transpose(
        source_grad[1], cut_cols(w_rest[2], s_place)
    )
    grad_memory = grad_memory.reshape(s_size, sources_len, width)
    grad_memory = jnp.stack([pick(grad_memory, owners[j]) for j in range(s_size)])
    grad_memory = scatter_seq(grad_memory.reshape(2, y_size, sources_len, width))

    def row_sum(grads):
        parts = jnp.stack([g.astype(BF).reshape(y_size, 2, cut, width) for g in grads])
        kept = pick(parts, core_place, 2).astype(F32)
        kept = kept + swap(pick(parts, core_place ^ 1, 2), "core", 1).astype(F32)
        total = pick(kept, y_place, 1)
        for k in range(1, y_size):
            total = total + swap(pick(kept, y_place ^ k, 1).astype(BF), "y", k).astype(F32)
        return total.astype(BF)

    def by_rows(grad):
        grad = grad.astype(BF).reshape(s_size, f_size, up_rows, -1)
        return grad.transpose(1, 0, 2, 3).reshape(f_size, -1, width)

    cross_pair = row_sum(
        [contract_rows(normed_two, query_cross_grad), contract_rows(cross_out, cross_branch)]
    )
    first = jnp.concatenate(
        [
            cross_pair[0].reshape(f_size, up_rows, width),
            cross_pair[1].reshape(f_size, up_rows, width),
            contract_rows(self_cut, branch_row).astype(BF).reshape(f_size, up_rows, width),
            by_rows(contract_rows(row_sources, source_grad[0])),
            by_rows(contract_rows(row_sources, source_grad[1])),
        ],
        axis=1,
    )
    first = lax.psum_scatter(first, FSDP, scatter_dimension=0)
    second = jnp.concatenate(
        [by_rows(contract_rows(normed_row, g)) for g in (query_grad, key_grad, value_grad)], axis=1
    )
    second = lax.psum_scatter(second, FSDP, scatter_dimension=0)

    def to_rows(grads, number):
        grads = grads.reshape(number, s_size, up_rows, cut).transpose(1, 0, 2, 3)
        grads = lax.all_to_all(grads, SEQ, 0, 0)
        return grads.transpose(1, 2, 0, 3).reshape(number, up_rows, width)

    by_cut = to_rows(jnp.concatenate([second, first[3 * up_rows :]]), 5).astype(F32)
    first = first[: 3 * up_rows].reshape(3, up_rows, width).astype(F32)

    def spread_cut(values):
        return lax.dynamic_update_slice_in_dim(jnp.zeros(width, F32), values, s_place * cut, 0)

    rows = [
        spread_cut(column_sums(query_grad)),
        spread_cut(column_sums(value_grad)),
        column_sums(self_branch),
        column_sums(query_cross_grad),
        spread_cut(column_sums(source_grad[1])),
        column_sums(cross_branch),
        column_sums(down_grad),
        gain_one,
        gain_two,
        gain_three,
        shift_one,
        shift_two,
        shift_three,
    ]
    spread = jnp.zeros((s_size, z_size, x_size * unit), F32)
    spread = lax.dynamic_update_slice_in_dim(
        spread, grad_up_bias.reshape(s_size, 1, x_size * unit), z_place, 1
    )
    table = jnp.stack(rows).reshape(len(rows), count, up_rows).transpose(1, 0, 2).reshape(count, -1)
    table = jnp.concatenate([table, spread.reshape(count, unit)], axis=1)
    table = jnp.sum(lax.all_to_all(table, ALL, 0, 0), axis=0)
    grad_up_bias = table[len(rows) * up_rows :]
    table = table[: len(rows) * up_rows].reshape(len(rows), up_rows)
    return (
        result.astype(BF)[None],
        grad_hidden[None],
        grad_memory[None],
        jnp.stack([by_cut[:3], jnp.stack([first[0], by_cut[3], by_cut[4]])]),
        jnp.stack([first[2], first[1]]),
        grad_up,
        grad_down,
        table[:7],
        grad_up_bias,
        table[7:10],
        table[10:13],
    )


def solution(mesh):
    seq, fsdp = mesh.shape["seq"], mesh.shape["fsdp"]
    split = Mesh(mesh.devices.reshape(seq // 2, 2, 4, fsdp // 4), ALL)
    placed = (
        P(FSDP, SEQ, None),
        P(FSDP, SEQ, None),
        P(FSDP, SEQ, None),
        P(FSDP, SEQ),
        P(FSDP, SEQ),
        P(),
        P(None, None, FSDP, None),
        P(None, FSDP, None),
        P(FSDP, None),
        P(FSDP, None),
        P(None, FSDP),
        P(FSDP),
        P(None, FSDP),
        P(None, FSDP),
    )
    return jax.shard_map(
        body,
        mesh=split,
        in_specs=placed,
        out_specs=(
            P(FSDP, SEQ, None),
            P(FSDP, SEQ, None),
            P(FSDP, SEQ, None),
            P(None, None, ALL, None),
            P(None, ALL, None),
            P(ALL, None),
            P(ALL, None),
            P(None, ALL),
            P(ALL),
            P(None, ALL),
            P(None, ALL),
        ),
        check_vma=False,
    )
```

```python
import functools
import math

import jax
import jax.numpy as jnp
from jax import lax
from jax.experimental import pallas as pl
from jax.experimental.pallas import tpu as pltpu
from jax.sharding import Mesh
from jax.sharding import PartitionSpec as P

HEADS = 16
EPSILON = 1e-05
NEGATIVE = -1e30
GELU_IN = math.sqrt(2.0 / math.pi)
GELU_CUBE = 0.044715
SEQ = ("y", "core")
FSDP = ("z", "x")
PLANE = ("x", "y", "core")
ALL = ("y", "core", "z", "x")
BF = jnp.bfloat16
F32 = jnp.float32
VMEM_LIMIT = 52 * 1024 * 1024


def matmul(left, right):
    return jnp.dot(left, right, preferred_element_type=F32)


def swap(value, axis, step):
    return lax.ppermute(value, axis, [(i, i ^ step) for i in range(lax.axis_size(axis))])


def norm_parts(values):
    centred = values - jnp.mean(values, axis=-1, keepdims=True)
    scale = lax.rsqrt(jnp.mean(centred * centred, axis=-1, keepdims=True) + EPSILON)
    return centred * scale, scale


def norm_back(normed, scale, gain, grad):
    inner = grad * gain
    means = jnp.mean(inner, axis=-1, keepdims=True)
    along = jnp.mean(inner * normed, axis=-1, keepdims=True)
    return (
        scale * (inner - means - normed * along),
        jnp.sum(grad * normed, axis=0, keepdims=True),
        jnp.sum(grad, axis=0, keepdims=True),
    )


def nt(left, right):
    return lax.dot_general(left, right, (((1,), (1,)), ((), ())), preferred_element_type=F32)


def tn(left, right):
    return lax.dot_general(left, right, (((0,), (0,)), ((), ())), preferred_element_type=F32)


def total_rows(values):
    return jnp.sum(values, axis=0, keepdims=True)


def call(kernel, outs, scratch, scalars, *operands, flops=0):
    vmem = pl.BlockSpec(memory_space=pltpu.VMEM)
    moved = sum(o.size * o.dtype.itemsize for o in operands)
    return pl.pallas_call(
        kernel,
        out_shape=[jax.ShapeDtypeStruct(shape, kind) for shape, kind in outs],
        in_specs=[pl.BlockSpec(memory_space=pltpu.SMEM)] + [vmem] * len(operands),
        out_specs=[vmem] * len(outs),
        scratch_shapes=[pltpu.VMEM(shape, kind) for shape, kind in scratch],
        compiler_params=pltpu.CompilerParams(vmem_limit_bytes=VMEM_LIMIT),
        cost_estimate=pl.CostEstimate(flops=flops, bytes_accessed=moved, transcendentals=0),
    )(scalars, *operands)


def softmax_rows(scores, bias):
    scores = scores + bias
    top = jnp.max(scores, axis=1, keepdims=True)
    raised = jnp.exp(scores - top)
    whole = jnp.maximum(jnp.sum(raised, axis=1, keepdims=True), 1.0)
    scale = jnp.where(top > 0.5 * NEGATIVE, 1.0 / whole, 0.0)
    return raised * scale, top, scale


def softmax_again(scores, bias, top, scale):
    return jnp.exp(scores + bias - top) * scale


def softmax_back(chance, chance_grad):
    return chance * (chance_grad - jnp.sum(chance * chance_grad, axis=1, keepdims=True))


def bias_of(query_seg, key_seg, query_pos=None, key_pos=None):
    allowed = (query_seg == key_seg) & (query_seg != 0)
    if query_pos is not None:
        allowed = allowed & (key_pos <= query_pos)
    return jnp.where(allowed, 0.0, NEGATIVE)


def self_forward(
    z_size, x_size, held, lane, heads, at, lines, row, seg, seg_line, pos, pos_line,
    weights, params, up_bias, normed, query, key, value, stats, mixed,
):
    z_place, x_place = at[0], at[1]
    width = row.shape[1]
    cut = query.shape[1]
    row_len = row.shape[0]
    block = min(row_len, 512)
    for j in range(z_size * x_size):
        kx, kz = (j % x_size) ^ x_place, (j // x_size) ^ z_place
        for m in range(3):
            weights[m, j * held : (j + 1) * held, :] = lines[kx, kz, m * held : (m + 1) * held, :]
        small = lines[kx, kz, 3 * held :, :].astype(F32)
        for r in range(13):
            o, c = divmod(r * lane, cut)
            params[r : r + 1, j * lane : (j + 1) * lane] = small[o : o + 1, c : c + lane]
    part = up_bias.shape[1] // x_size
    for xx in range(x_size):
        small = lines[xx ^ x_place, 0, 3 * held :, :].astype(F32)
        for r in range(part // lane):
            o, c = divmod((13 + r) * lane, cut)
            first = xx * part + r * lane
            up_bias[:, first : first + lane] = small[o : o + 1, c : c + lane]
    gain, shift = params[7:8, :], params[10:11, :]
    both = jnp.zeros((2, cut), F32)
    for j in range(width // cut):
        both = jnp.where(at[2] == j, params[0:2, j * cut : (j + 1) * cut], both)
    query_bias, value_bias = both[0:1], both[1:2]
    for b in range(row_len // block):
        rows = slice(b * block, (b + 1) * block)
        unit, _ = norm_parts(row[rows, :].astype(F32))
        h = (unit * gain + shift).astype(BF)
        normed[rows, :] = h
        query[rows, :] = (matmul(h, weights[0]) + query_bias).astype(BF)
        key[rows, :] = matmul(h, weights[1]).astype(BF)
        value[rows, :] = (matmul(h, weights[2]) + value_bias).astype(BF)
    size = cut // heads
    score_scale = 1.0 / math.sqrt(size)
    for b in range(row_len // block):
        rows = slice(b * block, (b + 1) * block)
        bias = bias_of(seg[rows, :], seg_line[...], pos[rows, :], pos_line[...])
        for h in range(heads):
            cols = slice(h * size, (h + 1) * size)
            scores = nt(query[rows, cols], key[:, cols]) * score_scale
            chance, top, scale = softmax_rows(scores, bias)
            stats[rows, h : h + 1] = top
            stats[rows, 64 + h : 65 + h] = scale
            mixed[rows, cols] = matmul(chance.astype(BF), value[:, cols]).astype(BF)


def matrix(rest, m):
    values = rest[:, m]
    return values.reshape(values.shape[0] * values.shape[1], values.shape[2])


def middle_forward(
    s_size, at, parts, inputs, rest, params, sources, seg, source_seg,
    after_self, after_cross, left, query, stats, keys, normed,
):
    width = inputs.shape[1]
    cut = width // s_size
    for j in range(s_size):
        left[:, 2 * width + j * cut : 2 * width + (j + 1) * cut] = parts[at[j]]
        for n in range(2):
            keys[n, :, j * cut : (j + 1) * cut] = sources[at[j], n]
    x1 = (
        inputs[...].astype(F32)
        + matmul(left[:, 2 * width :], matrix(rest, 1))
        + params[2:3, :]
    )
    after_self[...] = x1
    unit, _ = norm_parts(x1)
    left[:, :width] = (unit * params[8:9, :] + params[11:12, :]).astype(BF)
    query[...] = (matmul(left[:, :width], matrix(rest, 0)) + params[3:4, :]).astype(BF)
    bias = bias_of(seg[...], source_seg[...])
    size = width // HEADS
    score_scale = 1.0 / math.sqrt(size)
    for h in range(HEADS):
        cols = slice(h * size, (h + 1) * size)
        scores = nt(query[:, cols], keys[0, :, cols]) * score_scale
        chance, top, scale = softmax_rows(scores, bias)
        stats[:, h : h + 1] = top
        stats[:, 64 + h : 65 + h] = scale
        left[:, width + h * size : width + (h + 1) * size] = matmul(
            chance.astype(BF), keys[1, :, cols]
        ).astype(BF)
    x2 = x1 + matmul(left[:, width : 2 * width], matrix(rest, 2)) + params[5:6, :]
    after_cross[...] = x2
    unit, _ = norm_parts(x2)
    normed[...] = (unit * params[9:10, :] + params[12:13, :]).astype(BF)


def middle_backward(
    s_size, at, terms, out_grad, after_self, after_cross, rest, params, query,
    keys, stats, seg, source_seg,
    branch, self_grad, pair, sums,
):
    tokens, width = out_grad.shape
    cut = width // s_size
    size = width // HEADS
    score_scale = 1.0 / math.sqrt(size)
    down = out_grad[...].astype(F32)
    grad = terms[...].astype(F32)
    unit, scale = norm_parts(after_cross[...])
    moved, gain, shift = norm_back(unit, scale, params[9:10, :], grad)
    sums[2:3, :] = gain
    sums[5:6, :] = shift
    x2_grad = down + moved
    d2 = x2_grad.astype(BF)
    sums[6:7, :] = total_rows(d2.astype(F32))
    sums[7:8, :] = total_rows(down)
    for j in range(s_size):
        pair[at[j], :tokens, cut:] = d2[:, j * cut : (j + 1) * cut]
    head_grad = nt(d2, matrix(rest, 2)).astype(BF)
    bias = bias_of(seg[...], source_seg[...])
    per = HEADS // s_size
    grads = []
    for h in range(HEADS):
        cols = slice(h * size, (h + 1) * size)
        q, do = query[:, cols], head_grad[:, cols]
        k, v = keys[0, :, cols], keys[1, :, cols]
        scores = nt(q, k) * score_scale
        chance = softmax_again(scores, bias, stats[:, h : h + 1], stats[:, 64 + h : 65 + h])
        score_grad = softmax_back(chance, nt(do, v)).astype(BF)
        grads.append((matmul(score_grad, k) * score_scale).astype(BF))
        to = slice((h % per) * size, (h % per + 1) * size)
        pair[at[h // per], tokens:, to] = (tn(score_grad, q) * score_scale).astype(BF)
        to = slice(cut + to.start, cut + to.stop)
        pair[at[h // per], tokens:, to] = tn(chance.astype(BF), do).astype(BF)
    query_grad = jnp.concatenate(grads, axis=1)
    sums[8:9, :] = total_rows(query_grad.astype(F32))
    for j in range(s_size):
        pair[at[j], :tokens, :cut] = query_grad[:, j * cut : (j + 1) * cut]
    unit, scale = norm_parts(after_self[...])
    moved, gain, shift = norm_back(unit, scale, params[8:9, :], nt(query_grad, matrix(rest, 0)))
    sums[1:2, :] = gain
    sums[4:5, :] = shift
    x1_grad = x2_grad + moved
    self_grad[...] = x1_grad
    d1 = x1_grad.astype(BF)
    branch[...] = d1
    sums[9:10, :] = total_rows(d1.astype(F32))


def feed_forward(
    steps, normed, down, w_up, w_down, up_bias,
    activated, pre_grad, partial, bias_grad,
    held, total,
):
    step = pl.program_id(0)
    groups, z_size, share, columns = w_up.shape
    per = groups * share
    for z in range(z_size):
        held[z * per : (z + 1) * per, :] = w_up[:, z].reshape(per, columns)
    u = matmul(normed[...], held[...]) + up_bias[...]
    square = u * u
    bent = jnp.tanh(GELU_IN * (u + GELU_CUBE * square * u))
    half = 0.5 * (1.0 + bent)
    activated[...] = (u * half).astype(BF)
    slope = half + 0.5 * u * (1.0 - bent * bent) * (GELU_IN + 3.0 * GELU_IN * GELU_CUBE * square)
    du = (nt(down[...], w_down[...]) * slope).astype(BF)
    pre_grad[...] = du
    bias_grad[...] = total_rows(du.astype(F32))
    term = nt(du, held[...])

    @pl.when(step == 0)
    def _():
        total[...] = term

    @pl.when(step > 0)
    def _():
        total[...] += term

    @pl.when(step == steps - 1)
    def _():
        partial[...] = total[...].astype(BF)


def feed_forward_gradients(
    s_size, z_size, x_size, up_rows, at, normed, pre_grad, activated, down, w_down,
    out, mixed,
):
    width = normed.shape[1]
    half = pre_grad.shape[1] // 2
    places = z_size * x_size
    unit = out.shape[1] - 2 * z_size * up_rows
    for b in range(x_size * s_size):
        term = tn(activated[:, b * unit : (b + 1) * unit], down[...])
        out[b, 2 * z_size * up_rows :, :] = term.astype(BF)
    for t in range(width // 256):
        cols = slice(t * 256, (t + 1) * 256)
        mixed[:, cols] = matmul(activated[...], w_down[:, cols]).astype(BF)
    tile = places * up_rows
    for s in range(s_size):
        for i in range(2):
            term = tn(normed[:, s * tile : (s + 1) * tile], pre_grad[:, i * half : (i + 1) * half])
            term = term.astype(BF)
            for f in range(places):
                z, x = divmod(f, x_size)
                first = (i * z_size + z) * up_rows
                out[x * s_size + s, first : first + up_rows, :] = term[f * up_rows : (f + 1) * up_rows]


def self_backward(
    heads, at, branch, w_out, query, key, value, stats, seg, seg_line, pos, pos_line, weights, normed,
    cuts, partial, sums,
    grads, key_total, value_total,
):
    row_len, cut = query.shape
    block = min(row_len, 512)
    size = cut // heads
    score_scale = 1.0 / math.sqrt(size)
    for b in range(row_len // block):
        rows = slice(b * block, (b + 1) * block)
        head_grad = nt(branch[rows, :], w_out[...]).astype(BF)
        bias = bias_of(seg[rows, :], seg_line[...], pos[rows, :], pos_line[...])
        for h in range(heads):
            cols = slice(h * size, (h + 1) * size)
            q, do, k, v = query[rows, cols], head_grad[:, cols], key[:, cols], value[:, cols]
            chance = softmax_again(
                nt(q, k) * score_scale, bias, stats[rows, h : h + 1], stats[rows, 64 + h : 65 + h]
            )
            score_grad = softmax_back(chance, nt(do, v)).astype(BF)
            grads[rows, cols] = (matmul(score_grad, k) * score_scale).astype(BF)
            key_term = tn(score_grad, q) * score_scale
            value_term = tn(chance.astype(BF), do)
            if b == 0:
                key_total[:, cols] = key_term
                value_total[:, cols] = value_term
            else:
                key_total[:, cols] += key_term
                value_total[:, cols] += value_term
    grads[:, cut : 2 * cut] = key_total[...].astype(BF)
    grads[:, 2 * cut :] = value_total[...].astype(BF)
    sums[0:1, :] = total_rows(grads[:, :cut].astype(F32))
    sums[1:2, :] = total_rows(grads[:, 2 * cut :].astype(F32))
    tile = min(256, normed.shape[1])
    for t in range(normed.shape[1] // tile):
        rows = slice(t * tile, (t + 1) * tile)
        cuts[rows, :] = tn(normed[:, rows], grads[...]).astype(BF)
    for b in range(row_len // block):
        rows = slice(b * block, (b + 1) * block)
        grad = nt(grads[rows, :cut], weights[0]) + nt(grads[rows, cut : 2 * cut], weights[1])
        partial[rows, :] = (grad + nt(grads[rows, 2 * cut :], weights[2])).astype(BF)


def group_gradients(at, own, swapped, pair, branch_cut, sources, source_grad, out):
    rows, cut = own.shape[0], branch_cut.shape[1]
    width = sources.shape[1]
    tile = min(256, width)
    for t in range(width // tile):
        to = slice(t * tile, (t + 1) * tile)
        for n in range(3):
            cols = slice(n * width + t * tile, n * width + (t + 1) * tile)
            right = branch_cut if n == 2 else pair
            first = n * cut if n < 2 else 0
            term = tn(own[:, cols], right[:rows, first : first + cut])
            term = term + tn(swapped[:, cols], right[rows:, first : first + cut])
            out[to, n * cut : (n + 1) * cut] = term.astype(BF)
        for n in range(2):
            out[to, (3 + n) * cut : (4 + n) * cut] = tn(sources[:, to], source_grad[n]).astype(BF)


def last_step(at, line, others, inputs, params, self_grad, sums, cut_sums, up_bias_grad, grad_hidden, table, rows):
    count, _, lanes = table.shape
    width = inputs.shape[1]
    unit, scale = norm_parts(inputs[...].astype(F32))
    grad = line[...] + jnp.sum(others[...].astype(F32), axis=0)
    moved, gain, shift = norm_back(unit, scale, params[7:8, :], grad)
    grad_hidden[...] = self_grad[...] + moved
    rows[...] = jnp.zeros(rows.shape, F32)
    rows[0:2, :] = cut_sums[0:2, :]
    rows[2:3, :] = sums[9:10, :]
    rows[3:4, :] = sums[8:9, :]
    rows[4:5, :] = cut_sums[2:3, :]
    rows[5:7, :] = sums[6:8, :]
    rows[7:8, :] = gain
    rows[8:10, :] = sums[1:3, :]
    rows[10:11, :] = shift
    rows[11:13, :] = sums[4:6, :]
    for j in range(count):
        table[j, 0:16, :] = rows[:, j * lanes : (j + 1) * lanes]
    table[:, 16:24, :] = jnp.zeros((count, 8, lanes), F32)
    mine = up_bias_grad.shape[1] // (8 * lanes)
    for j in range(mine):
        for r in range(8):
            first = (j * 8 + r) * lanes
            table[at[0] * mine + j, 16 + r : 17 + r, :] = up_bias_grad[:, first : first + lanes]


def gather_pair(value):
    lines = [value] + [swap(value, "y", k) for k in range(1, lax.axis_size("y"))]
    lines = jnp.concatenate(lines) if len(lines) > 1 else value
    return lines, swap(lines, "core", 1)


def gather_seq(value):
    return jnp.concatenate(gather_pair(value))


def scatter_seq(partial):
    line = partial[0].astype(F32) + swap(partial[1].astype(BF), "core", 1).astype(F32)
    total = line[0]
    for k in range(1, lax.axis_size("y")):
        total = total + swap(line[k].astype(BF), "y", k).astype(F32)
    return total


def exchange_seq(value):
    line = jnp.stack([value[0], swap(value[1], "core", 1)])
    lines = [line[:, 0]] + [swap(line[:, k], "y", k) for k in range(1, lax.axis_size("y"))]
    return jnp.stack(lines, axis=1)


def trade_z(parts):
    return lax.all_to_all(parts, "z", 0, 0)


def gather_z(value):
    return trade_z(jnp.broadcast_to(value, (lax.axis_size("z"),) + value.shape))


def behind(value, other):
    last = other[(-1,) * other.ndim].astype(F32) * 0.0
    return value + last.astype(value.dtype)


def pick(value, at, axis=0):
    return lax.dynamic_index_in_dim(value, at, axis, keepdims=False)


def body(
    hidden_in,
    memory,
    out_grad,
    segment_ids,
    memory_segments,
    deal,
    attn_in,
    attn_out,
    fc1,
    fc2,
    proj_bias,
    fc1_bias,
    norm_gain,
    norm_bias,
):
    y_size, z_size, x_size = lax.axis_size("y"), lax.axis_size("z"), lax.axis_size("x")
    s_size, f_size = y_size * 2, z_size * x_size
    y_place, core_place = lax.axis_index("y"), lax.axis_index("core")
    z_place, x_place = lax.axis_index("z"), lax.axis_index("x")
    s_place = y_place * 2 + core_place
    f_place = z_place * x_size + x_place
    place = s_place * f_size + f_place
    count = s_size * f_size
    tokens, width = hidden_in.shape[1:]
    sources_len = memory.shape[1]
    held = attn_in.shape[2]
    share = held // s_size
    lane = width // f_size
    cut = width // s_size
    row_len = s_size * tokens
    blocks = [(c, k) for c in range(2) for k in range(y_size)]
    block_of = [((j % 2) ^ core_place) * y_size + ((j // 2) ^ y_place) for j in range(s_size)]
    owners = jnp.stack([(y_place ^ k) * 2 + (core_place ^ c) for c, k in blocks])

    def cut_cols(value, at):
        return lax.dynamic_slice_in_dim(value, at * cut, cut, value.ndim - 1)

    here = jnp.stack([z_place, x_place, s_place]).astype(jnp.int32)
    block_list = jnp.stack(block_of).astype(jnp.int32)

    small = jnp.concatenate(
        [
            proj_bias.reshape(-1).astype(BF),
            norm_gain.reshape(-1).astype(BF),
            norm_bias.reshape(-1).astype(BF),
            fc1_bias.astype(BF),
        ]
    )
    small_len = small.shape[0]
    small_rows = -(-small_len // (16 * cut)) * 16
    small = jnp.pad(small, (0, small_rows * cut - small_len)).reshape(small_rows, cut)
    early = jnp.concatenate([cut_cols(attn_in[0], s_place).astype(BF).reshape(3 * held, cut), small])

    rest = jnp.concatenate(
        [
            lax.dynamic_slice_in_dim(attn_in[1, 0], s_place * share, share, 0),
            lax.dynamic_slice_in_dim(attn_out, s_place * share, share, 1).reshape(-1, width),
        ]
    ).astype(BF)
    labels = jnp.concatenate([segment_ids[0], memory_segments[0]]).astype(BF)
    label_rows = -(-labels.shape[0] // (16 * width)) * 16
    labels = jnp.pad(labels, (0, label_rows * width - labels.shape[0])).reshape(label_rows, width)
    row = jnp.concatenate([hidden_in[0], memory[0], labels])
    row_lines = [row] + [swap(row, "y", k) for k in range(1, y_size)]
    row_lines = jnp.concatenate(row_lines)
    row = jnp.concatenate([row_lines, swap(row_lines, "core", 1)])
    early_lines = [early] + [swap(early, "z", k) for k in range(1, z_size)]
    early_lines = jnp.stack(early_lines)
    unit = fc2.shape[0] // s_size
    hidden = x_size * fc2.shape[0]
    down_share = lax.dynamic_slice_in_dim(fc2, s_place * unit, unit, 0).astype(BF)
    down_lines = [swap(down_share, "x", k) for k in range(1, x_size)]
    send = behind(early_lines, down_lines[-1])

    up_share = lax.dynamic_slice_in_dim(fc1, s_place * share, share, 0).astype(BF)
    up_share = up_share.reshape(share, z_size, hidden).transpose(1, 0, 2).reshape(z_size, -1, width)
    memory_cuts = cut_cols(attn_in[1, 1:], s_place).astype(BF).reshape(1, -1, width)
    memory_cuts = jnp.broadcast_to(memory_cuts, (z_size,) + memory_cuts.shape[1:])
    over_z = trade_z(jnp.concatenate([up_share, memory_cuts], axis=1))

    rest = lax.all_gather(rest, FSDP + SEQ).reshape(count, 3, share, width)
    if share % 16:
        rest = rest.transpose(1, 0, 2, 3).reshape(1, 3, width, width)
    early = jnp.stack([early_lines] + [swap(send, "x", k) for k in range(1, x_size)])

    row = row.reshape(s_size, tokens + sources_len + label_rows, width)
    row_inputs = row[:, :tokens].reshape(row_len, width)
    labels = row[:, tokens + sources_len :].reshape(s_size, label_rows * width).astype(jnp.int32)
    row_seg = labels[:, :tokens].reshape(-1)
    row_sources = jnp.concatenate(
        [pick(row, block_of[j])[tokens : tokens + sources_len] for j in range(s_size)]
    )
    source_seg = jnp.concatenate(
        [pick(labels, block_of[j])[tokens : tokens + sources_len] for j in range(s_size)]
    )
    half_rows = tokens // 2
    offsets = jnp.arange(half_rows, dtype=jnp.int32)
    row_pos = (deal.reshape(s_size, 2)[owners][:, :, None] * half_rows + offsets).reshape(-1)
    row_places = (row_seg[:, None], row_seg[None], row_pos[:, None], row_pos[None])
    places = (segment_ids[0][:, None], source_seg[None])

    heads = HEADS // s_size
    weights, params, up_bias, normed_row, query, key, value, stats, self_cut = call(
        functools.partial(self_forward, z_size, x_size, held, lane, heads),
        [
            ((3, width, cut), BF),
            ((16, width), F32),
            ((1, hidden), F32),
            ((row_len, width), BF),
            ((row_len, cut), BF),
            ((row_len, cut), BF),
            ((row_len, cut), BF),
            ((row_len, 128), F32),
            ((row_len, cut), BF),
        ],
        [],
        here,
        early,
        row_inputs,
        *row_places,
        flops=2 * row_len * cut * (3 * width + 2 * row_len),
    )
    parts = exchange_seq(self_cut.reshape(2, y_size, tokens, cut)).reshape(s_size, tokens, cut)

    late_z = behind(over_z, self_cut)
    up_parts = late_z[:, : up_share.shape[1]].reshape(z_size, share, hidden)
    memory_lines = late_z[:, up_share.shape[1] :].reshape(z_size, 2, held, cut)
    memory_lines = jnp.stack([memory_lines] + [swap(memory_lines, "x", k) for k in range(1, x_size)])
    w_memory = jnp.stack([pick(memory_lines, j ^ x_place) for j in range(x_size)])
    w_memory = w_memory.transpose(2, 1, 0, 3, 4).reshape(2, width, cut)
    source_key = matmul(row_sources, w_memory[0]).astype(BF)
    value_bias = cut_cols(params[4], s_place)
    source_value = (matmul(row_sources, w_memory[1]) + value_bias).astype(BF)
    sources_row = s_size * sources_len
    source_all = gather_seq(jnp.stack([source_key, source_value])[None])

    down_grad = out_grad[0]
    down_all = gather_z(behind(down_grad, late_z)).reshape(z_size * tokens, width)

    after_self, after_cross, left, query_cross, cross_stats, source_keys, normed_three = call(
        functools.partial(middle_forward, s_size),
        [
            ((tokens, width), F32),
            ((tokens, width), F32),
            ((tokens, 3 * width), BF),
            ((tokens, width), BF),
            ((tokens, 128), F32),
            ((2, sources_row, width), BF),
            ((tokens, width), BF),
        ],
        [],
        behind(block_list, down_all),
        parts,
        hidden_in[0],
        rest,
        params,
        source_all,
        *places,
        flops=2 * tokens * width * (3 * width + 2 * sources_row),
    )

    w_up = lax.all_gather(up_parts, PLANE).reshape(s_size * x_size, z_size, share, hidden)
    if share % 16:
        w_up = w_up.transpose(1, 0, 2, 3).reshape(1, 1, width, hidden)
    down_lines = [behind(line, normed_three) for line in down_lines]
    down_lines = [gather_seq(line).reshape(s_size, unit, width) for line in down_lines]
    down_lines = [
        jnp.concatenate([pick(line, block_of[j]) for j in range(s_size)]) for line in down_lines
    ]
    down_lines = jnp.stack([fc2.astype(BF)] + down_lines)
    w_down = jnp.concatenate([pick(down_lines, j ^ x_place) for j in range(x_size)])

    normed_all = gather_z(normed_three).reshape(z_size * tokens, width)
    group = z_size * tokens
    columns = 512
    activated, pre_grad, partial, grad_up_bias = pl.pallas_call(
        functools.partial(feed_forward, hidden // columns),
        grid=(hidden // columns,),
        out_shape=[
            jax.ShapeDtypeStruct((group, hidden), BF),
            jax.ShapeDtypeStruct((group, hidden), BF),
            jax.ShapeDtypeStruct((group, width), BF),
            jax.ShapeDtypeStruct((1, hidden), F32),
        ],
        in_specs=[
            pl.BlockSpec((group, width), lambda i: (0, 0)),
            pl.BlockSpec((group, width), lambda i: (0, 0)),
            pl.BlockSpec(w_up.shape[:3] + (columns,), lambda i: (0, 0, 0, i)),
            pl.BlockSpec((columns, width), lambda i: (i, 0)),
            pl.BlockSpec((1, columns), lambda i: (0, i)),
        ],
        out_specs=[
            pl.BlockSpec((group, columns), lambda i: (0, i)),
            pl.BlockSpec((group, columns), lambda i: (0, i)),
            pl.BlockSpec((group, width), lambda i: (0, 0)),
            pl.BlockSpec((1, columns), lambda i: (0, i)),
        ],
        scratch_shapes=[pltpu.VMEM((width, columns), BF), pltpu.VMEM((group, width), F32)],
        compiler_params=pltpu.CompilerParams(vmem_limit_bytes=VMEM_LIMIT),
        cost_estimate=pl.CostEstimate(
            flops=6 * group * width * hidden, bytes_accessed=12 << 20, transcendentals=group * hidden
        ),
    )(normed_all, down_all, w_up, w_down, up_bias)
    terms = lax.psum_scatter(partial.reshape(z_size, tokens, width), "z", scatter_dimension=0)
    up_rows = width // count
    half = hidden // 2
    first_rows = 2 * z_size * up_rows
    if up_rows % 16:
        late = behind(activated, partial)
        grad_down = tn(late, down_all).astype(BF)
        grad_up = [tn(normed_all, pre_grad[:, i * half : (i + 1) * half]) for i in range(2)]
        grad_up = jnp.stack(grad_up).astype(BF)
        grad_up = grad_up.reshape(2, s_size, z_size, x_size, up_rows, half)
        grad_up = grad_up.transpose(3, 1, 0, 2, 4, 5).reshape(x_size * s_size, -1, width)
        grad_down = grad_down.reshape(x_size * s_size, unit, width)
        grad_mlp = jnp.concatenate([grad_up, grad_down], axis=1)
        mixed_down = matmul(activated, w_down).astype(BF)
    else:
        grad_mlp, mixed_down = call(
            functools.partial(feed_forward_gradients, s_size, z_size, x_size, up_rows),
            [((x_size * s_size, first_rows + unit, width), BF), ((group, width), BF)],
            [],
            behind(here, partial),
            normed_all,
            pre_grad,
            activated,
            down_all,
            w_down,
            flops=6 * group * width * hidden,
        )
    terms = behind(terms, mixed_down)
    grad_mlp = lax.psum_scatter(grad_mlp, PLANE, scatter_dimension=0)
    grad_up = grad_mlp[:-unit].reshape(2, z_size, up_rows, half)
    grad_down = lax.ppermute(
        grad_mlp[-unit:],
        ALL,
        [(s * f_size + f, f * s_size + s) for s in range(s_size) for f in range(f_size)],
    ).astype(F32)
    grad_up = jnp.stack(
        [
            swap(pick(grad_up, z_place ^ k, 1), "z", k) if k else pick(grad_up, z_place, 1)
            for k in range(z_size)
        ]
    )
    grad_up = jnp.stack([pick(grad_up, z_place ^ j) for j in range(z_size)])
    grad_up = grad_up.transpose(2, 0, 1, 3).reshape(up_rows, -1).astype(F32)

    branch, self_grad, pair, sums = call(
        functools.partial(middle_backward, s_size),
        [
            ((tokens, width), BF),
            ((tokens, width), F32),
            ((s_size, tokens + sources_row, 2 * cut), BF),
            ((16, width), F32),
        ],
        [],
        block_list,
        terms,
        down_grad,
        after_self,
        after_cross,
        rest,
        params,
        query_cross,
        source_keys,
        cross_stats,
        *places,
        flops=2 * tokens * width * (2 * width + 5 * sources_row),
    )

    results = trade_z(behind(mixed_down, terms).reshape(z_size, tokens, width))

    branch_row = gather_seq(branch)
    left_own, left_swapped = gather_pair(behind(left, branch_row))
    pair = behind(pair, branch_row)
    pair = exchange_seq(pair.reshape((2, y_size) + pair.shape[1:])).reshape(pair.shape)
    source_grad = jnp.sum(pair[:, tokens:].astype(F32), axis=0).astype(BF)
    source_grad = jnp.stack([source_grad[:, :cut], source_grad[:, cut:]])
    pair = pair[:, :tokens].reshape(row_len, 2 * cut)
    w_out = rest[:, 1].reshape(width, width)
    w_out = lax.dynamic_slice_in_dim(w_out, s_place * cut, cut, 0)
    self_cuts, partial, cut_sums = call(
        functools.partial(self_backward, heads),
        [((width, 3 * cut), BF), ((row_len, width), BF), ((8, cut), F32)],
        [((row_len, 3 * cut), BF), ((row_len, cut), F32), ((row_len, cut), F32)],
        behind(here, results),
        branch_row,
        w_out,
        query,
        key,
        value,
        stats,
        *row_places,
        weights,
        normed_row,
        flops=2 * row_len * cut * (7 * width + 5 * row_len),
    )

    result = after_cross + jnp.sum(results.astype(F32), axis=0) + params[6]

    (group_cuts,) = call(
        group_gradients,
        [((width, 5 * cut), BF)],
        [],
        here,
        left_own,
        left_swapped,
        pair,
        cut_cols(branch_row, s_place),
        row_sources,
        source_grad,
        flops=2 * row_len * cut * 3 * width,
    )
    group_cuts = group_cuts.reshape(s_size * z_size, x_size, up_rows, 5 * cut)
    kept = pick(group_cuts, x_place, 1).astype(F32)
    for k in range(1, x_size):
        kept = kept + swap(pick(group_cuts, x_place ^ k, 1), "x", k).astype(F32)

    def whole_columns(grads, number):
        grads = jnp.sum(grads.astype(F32), axis=1).reshape(s_size, up_rows, number, cut)
        return grads.transpose(2, 1, 0, 3).reshape(number, up_rows, width)

    grad_memory = nt(source_grad[0], w_memory[0]) + nt(source_grad[1], w_memory[1])
    grad_memory = grad_memory.reshape(s_size, sources_len, width)
    grad_memory = jnp.stack([pick(grad_memory, owners[j]) for j in range(s_size)])
    grad_memory = scatter_seq(grad_memory.reshape(2, y_size, sources_len, width))

    partial = partial.reshape(2, y_size, tokens, width)
    line = partial[0].astype(F32) + swap(partial[1], "core", 1).astype(F32)
    others = jnp.stack([swap(line[k].astype(BF), "y", k) for k in range(1, y_size)])
    cut_sums = jnp.concatenate([cut_sums[:2], jnp.sum(source_grad[1].astype(F32), axis=0)[None]])
    cut_sums = lax.dynamic_update_slice(
        jnp.zeros((3, width), F32), cut_sums, (jnp.int32(0), (s_place * cut).astype(jnp.int32))
    )
    grad_hidden, table = call(
        last_step,
        [((tokens, width), F32), ((count, 24, up_rows), F32)],
        [((16, width), F32)],
        here,
        line[0],
        others,
        hidden_in[0],
        params,
        self_grad,
        sums,
        cut_sums,
        grad_up_bias,
    )

    self_cuts = self_cuts.reshape(count, up_rows, 3 * cut)
    self_cuts = lax.all_to_all(self_cuts, ALL, 0, 0).reshape(s_size, f_size, up_rows, 3 * cut)
    table = behind(behind(table, self_cuts), grad_memory)
    table = jnp.sum(lax.all_to_all(table, ALL, 0, 0), axis=0)
    kept = behind(kept, table)
    kept = lax.all_to_all(kept.astype(BF), ("y", "core", "z"), 0, 0)
    group_cuts = whole_columns(kept.reshape(s_size, z_size, up_rows, 5 * cut), 5)
    self_cuts = whole_columns(self_cuts, 3)
    return (
        result.astype(BF)[None],
        grad_hidden[None],
        grad_memory[None],
        jnp.stack([self_cuts, jnp.concatenate([group_cuts[:1], group_cuts[3:]])]),
        jnp.stack([group_cuts[2], group_cuts[1]]),
        grad_up,
        grad_down,
        table[:7],
        table[16:].reshape(-1),
        table[7:10],
        table[10:13],
    )


def solution(mesh):
    seq, fsdp = mesh.shape["seq"], mesh.shape["fsdp"]
    split = Mesh(mesh.devices.reshape(seq // 2, 2, 4, fsdp // 4), ALL)
    placed = (
        P(FSDP, SEQ, None),
        P(FSDP, SEQ, None),
        P(FSDP, SEQ, None),
        P(FSDP, SEQ),
        P(FSDP, SEQ),
        P(),
        P(None, None, FSDP, None),
        P(None, FSDP, None),
        P(FSDP, None),
        P(FSDP, None),
        P(None, FSDP),
        P(FSDP),
        P(None, FSDP),
        P(None, FSDP),
    )
    return jax.shard_map(
        body,
        mesh=split,
        in_specs=placed,
        out_specs=(
            P(FSDP, SEQ, None),
            P(FSDP, SEQ, None),
            P(FSDP, SEQ, None),
            P(None, None, ALL, None),
            P(None, ALL, None),
            P(ALL, None),
            P(ALL, None),
            P(None, ALL),
            P(ALL),
            P(None, ALL),
            P(None, ALL),
        ),
        check_vma=False,
    )
```

```python
import functools
import math

import jax
import jax.numpy as jnp
from jax import lax
from jax.experimental import pallas as pl
from jax.experimental.pallas import tpu as pltpu
from jax.sharding import Mesh
from jax.sharding import PartitionSpec as P

HEADS = 16
EPSILON = 1e-05
NEGATIVE = -1e30
GELU_IN = math.sqrt(2.0 / math.pi)
GELU_CUBE = 0.044715
SEQ = ("y", "core")
FSDP = ("z", "x")
PLANE = ("x", "y", "core")
ALL = ("y", "core", "z", "x")
BF = jnp.bfloat16
F32 = jnp.float32
VMEM_LIMIT = 52 * 1024 * 1024


def matmul(left, right):
    return jnp.dot(left, right, preferred_element_type=F32)


def swap(value, axis, step):
    return lax.ppermute(value, axis, [(i, i ^ step) for i in range(lax.axis_size(axis))])


def norm_parts(values):
    centred = values - jnp.mean(values, axis=-1, keepdims=True)
    scale = lax.rsqrt(jnp.mean(centred * centred, axis=-1, keepdims=True) + EPSILON)
    return centred * scale, scale


def norm_back(normed, scale, gain, grad):
    inner = grad * gain
    means = jnp.mean(inner, axis=-1, keepdims=True)
    along = jnp.mean(inner * normed, axis=-1, keepdims=True)
    return (
        scale * (inner - means - normed * along),
        jnp.sum(grad * normed, axis=0, keepdims=True),
        jnp.sum(grad, axis=0, keepdims=True),
    )


def nt(left, right):
    return lax.dot_general(left, right, (((1,), (1,)), ((), ())), preferred_element_type=F32)


def tn(left, right):
    return lax.dot_general(left, right, (((0,), (0,)), ((), ())), preferred_element_type=F32)


def total_rows(values):
    return jnp.sum(values, axis=0, keepdims=True)


def call(kernel, outs, scratch, scalars, *operands, flops=0):
    vmem = pl.BlockSpec(memory_space=pltpu.VMEM)
    moved = sum(o.size * o.dtype.itemsize for o in operands)
    return pl.pallas_call(
        kernel,
        out_shape=[jax.ShapeDtypeStruct(shape, kind) for shape, kind in outs],
        in_specs=[pl.BlockSpec(memory_space=pltpu.SMEM)] + [vmem] * len(operands),
        out_specs=[vmem] * len(outs),
        scratch_shapes=[pltpu.VMEM(shape, kind) for shape, kind in scratch],
        compiler_params=pltpu.CompilerParams(vmem_limit_bytes=VMEM_LIMIT),
        cost_estimate=pl.CostEstimate(flops=flops, bytes_accessed=moved, transcendentals=0),
    )(scalars, *operands)


def softmax_rows(scores, bias):
    scores = scores + bias
    top = jnp.max(scores, axis=1, keepdims=True)
    raised = jnp.exp(scores - top)
    whole = jnp.maximum(jnp.sum(raised, axis=1, keepdims=True), 1.0)
    scale = jnp.where(top > 0.5 * NEGATIVE, 1.0 / whole, 0.0)
    return raised * scale, top, scale


def softmax_again(scores, bias, top, scale):
    return jnp.exp(scores + bias - top) * scale


def softmax_back(chance, chance_grad):
    return chance * (chance_grad - jnp.sum(chance * chance_grad, axis=1, keepdims=True))


def bias_of(query_seg, key_seg, query_pos=None, key_pos=None):
    allowed = (query_seg == key_seg) & (query_seg != 0)
    if query_pos is not None:
        allowed = allowed & (key_pos <= query_pos)
    return jnp.where(allowed, 0.0, NEGATIVE)


def self_forward(
    z_size, x_size, held, lane, heads, at, lines, row, seg, seg_line, pos, pos_line,
    weights, params, up_bias, normed, query, key, value, stats, mixed,
):
    z_place, x_place = at[0], at[1]
    width = row.shape[1]
    cut = query.shape[1]
    row_len = row.shape[0]
    block = min(row_len, 512)
    for j in range(z_size * x_size):
        kx, kz = (j % x_size) ^ x_place, (j // x_size) ^ z_place
        for m in range(3):
            weights[m, j * held : (j + 1) * held, :] = lines[kx, kz, m * held : (m + 1) * held, :]
        small = lines[kx, kz, 3 * held :, :].astype(F32)
        for r in range(13):
            o, c = divmod(r * lane, cut)
            params[r : r + 1, j * lane : (j + 1) * lane] = small[o : o + 1, c : c + lane]
    part = up_bias.shape[1] // x_size
    for xx in range(x_size):
        small = lines[xx ^ x_place, 0, 3 * held :, :].astype(F32)
        for r in range(part // lane):
            o, c = divmod((13 + r) * lane, cut)
            first = xx * part + r * lane
            up_bias[:, first : first + lane] = small[o : o + 1, c : c + lane]
    gain, shift = params[7:8, :], params[10:11, :]
    both = jnp.zeros((2, cut), F32)
    for j in range(width // cut):
        both = jnp.where(at[2] == j, params[0:2, j * cut : (j + 1) * cut], both)
    query_bias, value_bias = both[0:1], both[1:2]
    for b in range(row_len // block):
        rows = slice(b * block, (b + 1) * block)
        unit, _ = norm_parts(row[rows, :].astype(F32))
        h = (unit * gain + shift).astype(BF)
        normed[rows, :] = h
        query[rows, :] = (matmul(h, weights[0]) + query_bias).astype(BF)
        key[rows, :] = matmul(h, weights[1]).astype(BF)
        value[rows, :] = (matmul(h, weights[2]) + value_bias).astype(BF)
    size = cut // heads
    score_scale = 1.0 / math.sqrt(size)
    for b in range(row_len // block):
        rows = slice(b * block, (b + 1) * block)
        bias = bias_of(seg[rows, :], seg_line[...], pos[rows, :], pos_line[...])
        for h in range(heads):
            cols = slice(h * size, (h + 1) * size)
            scores = nt(query[rows, cols], key[:, cols]) * score_scale
            chance, top, scale = softmax_rows(scores, bias)
            stats[rows, h : h + 1] = top
            stats[rows, 64 + h : 65 + h] = scale
            mixed[rows, cols] = matmul(chance.astype(BF), value[:, cols]).astype(BF)


def matrix(rest, m):
    values = rest[:, m]
    return values.reshape(values.shape[0] * values.shape[1], values.shape[2])


def middle_forward(
    s_size, at, parts, inputs, rest, params, sources, seg, source_seg,
    after_self, after_cross, left, query, stats, keys, normed,
):
    width = inputs.shape[1]
    cut = width // s_size
    for j in range(s_size):
        left[:, 2 * width + j * cut : 2 * width + (j + 1) * cut] = parts[at[j]]
        for n in range(2):
            keys[n, :, j * cut : (j + 1) * cut] = sources[at[j], n]
    x1 = (
        inputs[...].astype(F32)
        + matmul(left[:, 2 * width :], matrix(rest, 1))
        + params[2:3, :]
    )
    after_self[...] = x1
    unit, _ = norm_parts(x1)
    left[:, :width] = (unit * params[8:9, :] + params[11:12, :]).astype(BF)
    query[...] = (matmul(left[:, :width], matrix(rest, 0)) + params[3:4, :]).astype(BF)
    bias = bias_of(seg[...], source_seg[...])
    size = width // HEADS
    score_scale = 1.0 / math.sqrt(size)
    for h in range(HEADS):
        cols = slice(h * size, (h + 1) * size)
        scores = nt(query[:, cols], keys[0, :, cols]) * score_scale
        chance, top, scale = softmax_rows(scores, bias)
        stats[:, h : h + 1] = top
        stats[:, 64 + h : 65 + h] = scale
        left[:, width + h * size : width + (h + 1) * size] = matmul(
            chance.astype(BF), keys[1, :, cols]
        ).astype(BF)
    x2 = x1 + matmul(left[:, width : 2 * width], matrix(rest, 2)) + params[5:6, :]
    after_cross[...] = x2
    unit, _ = norm_parts(x2)
    normed[...] = (unit * params[9:10, :] + params[12:13, :]).astype(BF)


def middle_backward(
    s_size, at, terms, out_grad, after_self, after_cross, rest, params, query,
    keys, stats, seg, source_seg,
    branch, self_grad, pair, sums,
):
    tokens, width = out_grad.shape
    cut = width // s_size
    size = width // HEADS
    score_scale = 1.0 / math.sqrt(size)
    down = out_grad[...].astype(F32)
    grad = terms[...].astype(F32)
    unit, scale = norm_parts(after_cross[...])
    moved, gain, shift = norm_back(unit, scale, params[9:10, :], grad)
    sums[2:3, :] = gain
    sums[5:6, :] = shift
    x2_grad = down + moved
    d2 = x2_grad.astype(BF)
    sums[6:7, :] = total_rows(d2.astype(F32))
    sums[7:8, :] = total_rows(down)
    for j in range(s_size):
        pair[at[j], :tokens, cut:] = d2[:, j * cut : (j + 1) * cut]
    head_grad = nt(d2, matrix(rest, 2)).astype(BF)
    bias = bias_of(seg[...], source_seg[...])
    per = HEADS // s_size
    grads = []
    for h in range(HEADS):
        cols = slice(h * size, (h + 1) * size)
        q, do = query[:, cols], head_grad[:, cols]
        k, v = keys[0, :, cols], keys[1, :, cols]
        scores = nt(q, k) * score_scale
        chance = softmax_again(scores, bias, stats[:, h : h + 1], stats[:, 64 + h : 65 + h])
        score_grad = softmax_back(chance, nt(do, v)).astype(BF)
        grads.append((matmul(score_grad, k) * score_scale).astype(BF))
        to = slice((h % per) * size, (h % per + 1) * size)
        pair[at[h // per], tokens:, to] = (tn(score_grad, q) * score_scale).astype(BF)
        to = slice(cut + to.start, cut + to.stop)
        pair[at[h // per], tokens:, to] = tn(chance.astype(BF), do).astype(BF)
    query_grad = jnp.concatenate(grads, axis=1)
    sums[8:9, :] = total_rows(query_grad.astype(F32))
    for j in range(s_size):
        pair[at[j], :tokens, :cut] = query_grad[:, j * cut : (j + 1) * cut]
    unit, scale = norm_parts(after_self[...])
    moved, gain, shift = norm_back(unit, scale, params[8:9, :], nt(query_grad, matrix(rest, 0)))
    sums[1:2, :] = gain
    sums[4:5, :] = shift
    x1_grad = x2_grad + moved
    self_grad[...] = x1_grad
    d1 = x1_grad.astype(BF)
    branch[...] = d1
    sums[9:10, :] = total_rows(d1.astype(F32))


def feed_forward(
    steps, normed, down, w_up, w_down, up_bias,
    activated, pre_grad, partial, bias_grad,
    held, total,
):
    step = pl.program_id(0)
    groups, z_size, share, columns = w_up.shape
    per = groups * share
    for z in range(z_size):
        held[z * per : (z + 1) * per, :] = w_up[:, z].reshape(per, columns)
    u = matmul(normed[...], held[...]) + up_bias[...]
    square = u * u
    bent = jnp.tanh(GELU_IN * (u + GELU_CUBE * square * u))
    half = 0.5 * (1.0 + bent)
    activated[...] = (u * half).astype(BF)
    slope = half + 0.5 * u * (1.0 - bent * bent) * (GELU_IN + 3.0 * GELU_IN * GELU_CUBE * square)
    du = (nt(down[...], w_down[...]) * slope).astype(BF)
    pre_grad[...] = du
    bias_grad[...] = total_rows(du.astype(F32))
    term = nt(du, held[...])

    @pl.when(step == 0)
    def _():
        total[...] = term

    @pl.when(step > 0)
    def _():
        total[...] += term

    @pl.when(step == steps - 1)
    def _():
        partial[...] = total[...].astype(BF)


def feed_forward_gradients(
    s_size, z_size, x_size, up_rows, at, normed, pre_grad, activated, down, w_down,
    out, mixed,
):
    width = normed.shape[1]
    half = pre_grad.shape[1] // 2
    places = z_size * x_size
    unit = out.shape[1] - 2 * z_size * up_rows
    for b in range(x_size * s_size):
        term = tn(activated[:, b * unit : (b + 1) * unit], down[...])
        out[b, 2 * z_size * up_rows :, :] = term.astype(BF)
    for t in range(width // 256):
        cols = slice(t * 256, (t + 1) * 256)
        mixed[:, cols] = matmul(activated[...], w_down[:, cols]).astype(BF)
    tile = places * up_rows
    for s in range(s_size):
        for i in range(2):
            term = tn(normed[:, s * tile : (s + 1) * tile], pre_grad[:, i * half : (i + 1) * half])
            term = term.astype(BF)
            for f in range(places):
                z, x = divmod(f, x_size)
                first = (i * z_size + z) * up_rows
                out[x * s_size + s, first : first + up_rows, :] = term[f * up_rows : (f + 1) * up_rows]


def self_backward(
    heads, at, branch, w_out, query, key, value, stats, seg, seg_line, pos, pos_line, weights, normed,
    cuts, partial, sums,
    grads, key_total, value_total,
):
    row_len, cut = query.shape
    block = min(row_len, 512)
    size = cut // heads
    score_scale = 1.0 / math.sqrt(size)
    for b in range(row_len // block):
        rows = slice(b * block, (b + 1) * block)
        head_grad = nt(branch[rows, :], w_out[...]).astype(BF)
        bias = bias_of(seg[rows, :], seg_line[...], pos[rows, :], pos_line[...])
        for h in range(heads):
            cols = slice(h * size, (h + 1) * size)
            q, do, k, v = query[rows, cols], head_grad[:, cols], key[:, cols], value[:, cols]
            chance = softmax_again(
                nt(q, k) * score_scale, bias, stats[rows, h : h + 1], stats[rows, 64 + h : 65 + h]
            )
            score_grad = softmax_back(chance, nt(do, v)).astype(BF)
            grads[rows, cols] = (matmul(score_grad, k) * score_scale).astype(BF)
            key_term = tn(score_grad, q) * score_scale
            value_term = tn(chance.astype(BF), do)
            if b == 0:
                key_total[:, cols] = key_term
                value_total[:, cols] = value_term
            else:
                key_total[:, cols] += key_term
                value_total[:, cols] += value_term
    grads[:, cut : 2 * cut] = key_total[...].astype(BF)
    grads[:, 2 * cut :] = value_total[...].astype(BF)
    sums[0:1, :] = total_rows(grads[:, :cut].astype(F32))
    sums[1:2, :] = total_rows(grads[:, 2 * cut :].astype(F32))
    tile = min(256, normed.shape[1])
    for t in range(normed.shape[1] // tile):
        rows = slice(t * tile, (t + 1) * tile)
        cuts[rows, :] = tn(normed[:, rows], grads[...]).astype(BF)
    for b in range(row_len // block):
        rows = slice(b * block, (b + 1) * block)
        grad = nt(grads[rows, :cut], weights[0]) + nt(grads[rows, cut : 2 * cut], weights[1])
        partial[rows, :] = (grad + nt(grads[rows, 2 * cut :], weights[2])).astype(BF)


def group_gradients(at, own, swapped, pair, branch_cut, sources, source_grad, out):
    rows, cut = own.shape[0], branch_cut.shape[1]
    width = sources.shape[1]
    tile = min(256, width)
    for t in range(width // tile):
        to = slice(t * tile, (t + 1) * tile)
        for n in range(3):
            cols = slice(n * width + t * tile, n * width + (t + 1) * tile)
            right = branch_cut if n == 2 else pair
            first = n * cut if n < 2 else 0
            term = tn(own[:, cols], right[:rows, first : first + cut])
            term = term + tn(swapped[:, cols], right[rows:, first : first + cut])
            out[to, n * cut : (n + 1) * cut] = term.astype(BF)
        for n in range(2):
            out[to, (3 + n) * cut : (4 + n) * cut] = tn(sources[:, to], source_grad[n]).astype(BF)


def last_step(
    lanes, at, line, others, inputs, params, self_grad, sums, cut_sums, up_bias_grad,
    grad_hidden, table, rows,
):
    unit, scale = norm_parts(inputs[...].astype(F32))
    grad = line[...] + jnp.sum(others[...].astype(F32), axis=0)
    moved, gain, shift = norm_back(unit, scale, params[7:8, :], grad)
    grad_hidden[...] = self_grad[...] + moved
    rows[...] = jnp.zeros(rows.shape, F32)
    rows[0:2, :] = cut_sums[0:2, :]
    rows[2:3, :] = sums[9:10, :]
    rows[3:4, :] = sums[8:9, :]
    rows[4:5, :] = cut_sums[2:3, :]
    rows[5:7, :] = sums[6:8, :]
    rows[7:8, :] = gain
    rows[8:10, :] = sums[1:3, :]
    rows[10:11, :] = shift
    rows[11:13, :] = sums[4:6, :]
    mine = up_bias_grad.shape[1] // 8
    at_lane = pl.ds(pl.multiple_of(at[0] * mine, mine), mine)
    for k in range(8):
        parts = [
            up_bias_grad[:, first : first + lanes]
            for first in range(k * lanes, up_bias_grad.shape[1], 8 * lanes)
        ]
        rows[16 + k : 17 + k, at_lane] = jnp.concatenate(parts, axis=1)
    table[...] = rows[...].T.astype(BF)


def gather_pair(value):
    lines = [value] + [swap(value, "y", k) for k in range(1, lax.axis_size("y"))]
    lines = jnp.concatenate(lines) if len(lines) > 1 else value
    return lines, swap(lines, "core", 1)


def gather_seq(value):
    return jnp.concatenate(gather_pair(value))


def scatter_seq(partial):
    line = partial[0].astype(F32) + swap(partial[1].astype(BF), "core", 1).astype(F32)
    total = line[0]
    for k in range(1, lax.axis_size("y")):
        total = total + swap(line[k].astype(BF), "y", k).astype(F32)
    return total


def exchange_seq(value):
    line = jnp.stack([value[0], swap(value[1], "core", 1)])
    lines = [line[:, 0]] + [swap(line[:, k], "y", k) for k in range(1, lax.axis_size("y"))]
    return jnp.stack(lines, axis=1)


def trade_z(parts):
    return lax.all_to_all(parts, "z", 0, 0)


def gather_z(value):
    return trade_z(jnp.broadcast_to(value, (lax.axis_size("z"),) + value.shape))


def behind(value, other):
    last = other[(-1,) * other.ndim].astype(F32) * 0.0
    return value + last.astype(value.dtype)


def pick(value, at, axis=0):
    return lax.dynamic_index_in_dim(value, at, axis, keepdims=False)


def body(
    hidden_in,
    memory,
    out_grad,
    segment_ids,
    memory_segments,
    deal,
    attn_in,
    attn_out,
    fc1,
    fc2,
    proj_bias,
    fc1_bias,
    norm_gain,
    norm_bias,
):
    y_size, z_size, x_size = lax.axis_size("y"), lax.axis_size("z"), lax.axis_size("x")
    s_size, f_size = y_size * 2, z_size * x_size
    y_place, core_place = lax.axis_index("y"), lax.axis_index("core")
    z_place, x_place = lax.axis_index("z"), lax.axis_index("x")
    s_place = y_place * 2 + core_place
    f_place = z_place * x_size + x_place
    place = s_place * f_size + f_place
    count = s_size * f_size
    tokens, width = hidden_in.shape[1:]
    sources_len = memory.shape[1]
    held = attn_in.shape[2]
    share = held // s_size
    lane = width // f_size
    cut = width // s_size
    row_len = s_size * tokens
    blocks = [(c, k) for c in range(2) for k in range(y_size)]
    block_of = [((j % 2) ^ core_place) * y_size + ((j // 2) ^ y_place) for j in range(s_size)]
    owners = jnp.stack([(y_place ^ k) * 2 + (core_place ^ c) for c, k in blocks])

    def cut_cols(value, at):
        return lax.dynamic_slice_in_dim(value, at * cut, cut, value.ndim - 1)

    here = jnp.stack([z_place, x_place, s_place, core_place]).astype(jnp.int32)
    block_list = jnp.stack(block_of).astype(jnp.int32)

    small = jnp.concatenate(
        [
            proj_bias.reshape(-1).astype(BF),
            norm_gain.reshape(-1).astype(BF),
            norm_bias.reshape(-1).astype(BF),
            fc1_bias.astype(BF),
        ]
    )
    small_len = small.shape[0]
    small_rows = -(-small_len // (16 * cut)) * 16
    small = jnp.pad(small, (0, small_rows * cut - small_len)).reshape(small_rows, cut)
    early = jnp.concatenate([cut_cols(attn_in[0], s_place).astype(BF).reshape(3 * held, cut), small])

    rest = jnp.concatenate(
        [
            lax.dynamic_slice_in_dim(attn_in[1, 0], s_place * share, share, 0),
            lax.dynamic_slice_in_dim(attn_out, s_place * share, share, 1).reshape(-1, width),
        ]
    ).astype(BF)
    labels = jnp.concatenate([segment_ids[0], memory_segments[0]]).astype(BF)
    label_rows = -(-labels.shape[0] // (16 * width)) * 16
    labels = jnp.pad(labels, (0, label_rows * width - labels.shape[0])).reshape(label_rows, width)
    row = jnp.concatenate([hidden_in[0], memory[0], labels])
    row_lines = [row] + [swap(row, "y", k) for k in range(1, y_size)]
    row_lines = jnp.concatenate(row_lines)
    row = jnp.concatenate([row_lines, swap(row_lines, "core", 1)])
    early_lines = [early] + [swap(early, "z", k) for k in range(1, z_size)]
    early_lines = jnp.stack(early_lines)
    unit = fc2.shape[0] // s_size
    hidden = x_size * fc2.shape[0]
    down_share = lax.dynamic_slice_in_dim(fc2, s_place * unit, unit, 0).astype(BF)
    down_lines = [swap(down_share, "x", k) for k in range(1, x_size)]
    send = behind(early_lines, down_lines[-1])
    down_lines = [behind(line, early_lines) for line in down_lines]
    down_lines = [[line] + [swap(line, "y", k) for k in range(1, y_size)] for line in down_lines]

    up_share = lax.dynamic_slice_in_dim(fc1, s_place * share, share, 0).astype(BF)
    up_share = up_share.reshape(share, z_size, hidden).transpose(1, 0, 2).reshape(z_size, -1, width)
    memory_cuts = cut_cols(attn_in[1, 1:], s_place).astype(BF).reshape(1, -1, width)
    memory_cuts = jnp.broadcast_to(memory_cuts, (z_size,) + memory_cuts.shape[1:])
    down_grad = out_grad[0]
    down_copies = jnp.broadcast_to(down_grad, (z_size,) + down_grad.shape)
    over_z = trade_z(jnp.concatenate([up_share, memory_cuts, down_copies], axis=1))
    down_all = over_z[:, -tokens:].reshape(z_size * tokens, width)
    over_z = over_z[:, :-tokens]

    rest = lax.all_gather(rest, FSDP + SEQ).reshape(count, 3, share, width)
    if share % 16:
        rest = rest.transpose(1, 0, 2, 3).reshape(1, 3, width, width)
    early = jnp.stack([early_lines] + [swap(send, "x", k) for k in range(1, x_size)])

    row = row.reshape(s_size, tokens + sources_len + label_rows, width)
    row_inputs = row[:, :tokens].reshape(row_len, width)
    labels = row[:, tokens + sources_len :].reshape(s_size, label_rows * width).astype(jnp.int32)
    row_seg = labels[:, :tokens].reshape(-1)
    row_sources = jnp.concatenate(
        [pick(row, block_of[j])[tokens : tokens + sources_len] for j in range(s_size)]
    )
    source_seg = jnp.concatenate(
        [pick(labels, block_of[j])[tokens : tokens + sources_len] for j in range(s_size)]
    )
    half_rows = tokens // 2
    offsets = jnp.arange(half_rows, dtype=jnp.int32)
    row_pos = (deal.reshape(s_size, 2)[owners][:, :, None] * half_rows + offsets).reshape(-1)
    row_places = (row_seg[:, None], row_seg[None], row_pos[:, None], row_pos[None])
    places = (segment_ids[0][:, None], source_seg[None])

    heads = HEADS // s_size
    weights, params, up_bias, normed_row, query, key, value, stats, self_cut = call(
        functools.partial(self_forward, z_size, x_size, held, lane, heads),
        [
            ((3, width, cut), BF),
            ((16, width), F32),
            ((1, hidden), F32),
            ((row_len, width), BF),
            ((row_len, cut), BF),
            ((row_len, cut), BF),
            ((row_len, cut), BF),
            ((row_len, 128), F32),
            ((row_len, cut), BF),
        ],
        [],
        behind(here, down_lines[-1][-1]),
        early,
        row_inputs,
        *row_places,
        flops=2 * row_len * cut * (3 * width + 2 * row_len),
    )
    parts = exchange_seq(self_cut.reshape(2, y_size, tokens, cut)).reshape(s_size, tokens, cut)

    late_z = behind(over_z, self_cut)
    memory_lines = late_z[:, up_share.shape[1] :].reshape(z_size, 2, held, cut)
    memory_lines = jnp.stack([memory_lines] + [swap(memory_lines, "x", k) for k in range(1, x_size)])
    w_memory = jnp.stack([pick(memory_lines, j ^ x_place) for j in range(x_size)])
    w_memory = w_memory.transpose(2, 1, 0, 3, 4).reshape(2, width, cut)
    source_key = matmul(row_sources, w_memory[0]).astype(BF)
    value_bias = cut_cols(params[4], s_place)
    source_value = (matmul(row_sources, w_memory[1]) + value_bias).astype(BF)
    sources_row = s_size * sources_len
    source_all = gather_seq(jnp.stack([source_key, source_value])[None])

    up_parts = behind(late_z[:, : up_share.shape[1]], source_all)
    up_parts = behind(behind(up_parts, parts), rest)
    up_parts = up_parts.reshape(z_size, share, hidden)

    after_self, after_cross, left, query_cross, cross_stats, source_keys, normed_three = call(
        functools.partial(middle_forward, s_size),
        [
            ((tokens, width), F32),
            ((tokens, width), F32),
            ((tokens, 3 * width), BF),
            ((tokens, width), BF),
            ((tokens, 128), F32),
            ((2, sources_row, width), BF),
            ((tokens, width), BF),
        ],
        [],
        block_list,
        parts,
        hidden_in[0],
        rest,
        params,
        source_all,
        *places,
        flops=2 * tokens * width * (3 * width + 2 * sources_row),
    )

    w_up = lax.all_gather(up_parts, PLANE).reshape(s_size * x_size, z_size, share, hidden)
    if share % 16:
        w_up = w_up.transpose(1, 0, 2, 3).reshape(1, 1, width, hidden)
    down_lines = [behind(jnp.concatenate(lines), parts) for lines in down_lines]
    down_lines = [jnp.concatenate([lines, swap(lines, "core", 1)]) for lines in down_lines]
    down_lines = [line.reshape(s_size, unit, width) for line in down_lines]
    down_lines = [
        jnp.concatenate([pick(line, block_of[j]) for j in range(s_size)]) for line in down_lines
    ]
    down_lines = jnp.stack([fc2.astype(BF)] + down_lines)
    w_down = jnp.concatenate([pick(down_lines, j ^ x_place) for j in range(x_size)])

    normed_all = gather_z(normed_three).reshape(z_size * tokens, width)
    group = z_size * tokens
    columns = 512
    activated, pre_grad, partial, grad_up_bias = pl.pallas_call(
        functools.partial(feed_forward, hidden // columns),
        grid=(hidden // columns,),
        out_shape=[
            jax.ShapeDtypeStruct((group, hidden), BF),
            jax.ShapeDtypeStruct((group, hidden), BF),
            jax.ShapeDtypeStruct((group, width), BF),
            jax.ShapeDtypeStruct((1, hidden), F32),
        ],
        in_specs=[
            pl.BlockSpec((group, width), lambda i: (0, 0)),
            pl.BlockSpec((group, width), lambda i: (0, 0)),
            pl.BlockSpec(w_up.shape[:3] + (columns,), lambda i: (0, 0, 0, i)),
            pl.BlockSpec((columns, width), lambda i: (i, 0)),
            pl.BlockSpec((1, columns), lambda i: (0, i)),
        ],
        out_specs=[
            pl.BlockSpec((group, columns), lambda i: (0, i)),
            pl.BlockSpec((group, columns), lambda i: (0, i)),
            pl.BlockSpec((group, width), lambda i: (0, 0)),
            pl.BlockSpec((1, columns), lambda i: (0, i)),
        ],
        scratch_shapes=[pltpu.VMEM((width, columns), BF), pltpu.VMEM((group, width), F32)],
        compiler_params=pltpu.CompilerParams(vmem_limit_bytes=VMEM_LIMIT),
        cost_estimate=pl.CostEstimate(
            flops=6 * group * width * hidden, bytes_accessed=12 << 20, transcendentals=group * hidden
        ),
    )(normed_all, down_all, w_up, w_down, up_bias)
    terms = lax.psum_scatter(partial.reshape(z_size, tokens, width), "z", scatter_dimension=0)
    up_rows = width // count
    half = hidden // 2
    first_rows = 2 * z_size * up_rows
    if up_rows % 16:
        late = behind(activated, partial)
        grad_down = tn(late, down_all).astype(BF)
        grad_up = [tn(normed_all, pre_grad[:, i * half : (i + 1) * half]) for i in range(2)]
        grad_up = jnp.stack(grad_up).astype(BF)
        grad_up = grad_up.reshape(2, s_size, z_size, x_size, up_rows, half)
        grad_up = grad_up.transpose(3, 1, 0, 2, 4, 5).reshape(x_size * s_size, -1, width)
        grad_down = grad_down.reshape(x_size * s_size, unit, width)
        grad_mlp = jnp.concatenate([grad_up, grad_down], axis=1)
        mixed_down = matmul(activated, w_down).astype(BF)
    else:
        grad_mlp, mixed_down = call(
            functools.partial(feed_forward_gradients, s_size, z_size, x_size, up_rows),
            [((x_size * s_size, first_rows + unit, width), BF), ((group, width), BF)],
            [],
            behind(here, partial),
            normed_all,
            pre_grad,
            activated,
            down_all,
            w_down,
            flops=6 * group * width * hidden,
        )
    left_own = behind(left, partial)
    left_own = jnp.concatenate([left_own] + [swap(left_own, "y", k) for k in range(1, y_size)])
    terms = behind(behind(terms, mixed_down), left_own)
    grad_mlp = lax.psum_scatter(grad_mlp, PLANE, scatter_dimension=0)
    grad_up = grad_mlp[:-unit].reshape(2, z_size, up_rows, half)
    grad_down = lax.ppermute(
        grad_mlp[-unit:],
        ALL,
        [(s * f_size + f, f * s_size + s) for s in range(s_size) for f in range(f_size)],
    ).astype(F32)
    grad_up = jnp.stack(
        [
            swap(pick(grad_up, z_place ^ k, 1), "z", k) if k else pick(grad_up, z_place, 1)
            for k in range(z_size)
        ]
    )
    grad_up = jnp.stack([pick(grad_up, z_place ^ j) for j in range(z_size)])
    grad_up = grad_up.transpose(2, 0, 1, 3).reshape(up_rows, -1).astype(F32)

    branch, self_grad, pair, sums = call(
        functools.partial(middle_backward, s_size),
        [
            ((tokens, width), BF),
            ((tokens, width), F32),
            ((s_size, tokens + sources_row, 2 * cut), BF),
            ((16, width), F32),
        ],
        [],
        block_list,
        terms,
        down_grad,
        after_self,
        after_cross,
        rest,
        params,
        query_cross,
        source_keys,
        cross_stats,
        *places,
        flops=2 * tokens * width * (2 * width + 5 * sources_row),
    )

    branch_row = gather_seq(branch)
    left_swapped = swap(behind(left_own, terms), "core", 1)
    w_out = rest[:, 1].reshape(width, width)
    w_out = lax.dynamic_slice_in_dim(w_out, s_place * cut, cut, 0)
    self_cuts, partial, cut_sums = call(
        functools.partial(self_backward, heads),
        [((width, 3 * cut), BF), ((row_len, width), BF), ((8, cut), F32)],
        [((row_len, 3 * cut), BF), ((row_len, cut), F32), ((row_len, cut), F32)],
        here,
        branch_row,
        w_out,
        query,
        key,
        value,
        stats,
        *row_places,
        weights,
        normed_row,
        flops=2 * row_len * cut * (7 * width + 5 * row_len),
    )

    pair = exchange_seq(pair.reshape((2, y_size) + pair.shape[1:])).reshape(pair.shape)
    pair = behind(pair, self_cuts)
    source_grad = jnp.sum(pair[:, tokens:].astype(F32), axis=0).astype(BF)
    source_grad = jnp.stack([source_grad[:, :cut], source_grad[:, cut:]])
    pair = pair[:, :tokens].reshape(row_len, 2 * cut)

    results = trade_z(behind(mixed_down, branch).reshape(z_size, tokens, width))
    result = after_cross + jnp.sum(results.astype(F32), axis=0) + params[6]
    def whole_columns(grads, number):
        grads = jnp.sum(grads.astype(F32), axis=1).reshape(s_size, up_rows, number, cut)
        return grads.transpose(2, 1, 0, 3).reshape(number, up_rows, width)

    grad_memory = nt(source_grad[0], w_memory[0]) + nt(source_grad[1], w_memory[1])
    grad_memory = grad_memory.reshape(s_size, sources_len, width)
    grad_memory = jnp.stack([pick(grad_memory, owners[j]) for j in range(s_size)])
    grad_memory = scatter_seq(grad_memory.reshape(2, y_size, sources_len, width))

    partial = partial.reshape(2, y_size, tokens, width)
    line = partial[0].astype(F32) + swap(partial[1], "core", 1).astype(F32)
    others = jnp.stack([swap(line[k].astype(BF), "y", k) for k in range(1, y_size)])
    cut_sums = jnp.concatenate([cut_sums[:2], jnp.sum(source_grad[1].astype(F32), axis=0)[None]])
    cut_sums = lax.dynamic_update_slice(
        jnp.zeros((3, width), F32), cut_sums, (jnp.int32(0), (s_place * cut).astype(jnp.int32))
    )
    grad_hidden, table = call(
        functools.partial(last_step, up_rows),
        [((tokens, width), F32), ((width, 128), BF)],
        [((128, width), F32)],
        here,
        line[0],
        others,
        hidden_in[0],
        params,
        self_grad,
        sums,
        cut_sums,
        grad_up_bias,
    )

    (group_cuts,) = call(
        group_gradients,
        [((width, 5 * cut), BF)],
        [],
        here,
        left_own,
        left_swapped,
        pair,
        cut_cols(branch_row, s_place),
        row_sources,
        source_grad,
        flops=2 * row_len * cut * 3 * width,
    )
    group_cuts = group_cuts.reshape(s_size * z_size, x_size, up_rows, 5 * cut)
    kept = pick(group_cuts, x_place, 1).astype(F32)
    for k in range(1, x_size):
        kept = kept + swap(pick(group_cuts, x_place ^ k, 1), "x", k).astype(F32)

    self_cuts = behind(self_cuts, results).reshape(count, up_rows, 3 * cut)
    self_cuts = lax.all_to_all(self_cuts, ALL, 0, 0).reshape(s_size, f_size, up_rows, 3 * cut)
    kept = behind(behind(behind(behind(kept, self_cuts), grad_memory), grad_down), grad_up)
    table = behind(table, self_cuts)
    table = lax.all_to_all(table.reshape(count, up_rows, 128), ALL, 0, 0)
    table = jnp.sum(table.astype(F32), axis=0).T
    kept = behind(kept, table)
    kept = lax.all_to_all(kept.astype(BF), ("y", "core", "z"), 0, 0)
    group_cuts = whole_columns(kept.reshape(s_size, z_size, up_rows, 5 * cut), 5)
    self_cuts = whole_columns(self_cuts, 3)
    return (
        result.astype(BF)[None],
        grad_hidden[None],
        grad_memory[None],
        jnp.stack([self_cuts, jnp.concatenate([group_cuts[:1], group_cuts[3:]])]),
        jnp.stack([group_cuts[2], group_cuts[1]]),
        grad_up,
        grad_down,
        table[:7],
        table[16:24].reshape(-1),
        table[7:10],
        table[10:13],
    )


def solution(mesh):
    seq, fsdp = mesh.shape["seq"], mesh.shape["fsdp"]
    split = Mesh(mesh.devices.reshape(seq // 2, 2, 4, fsdp // 4), ALL)
    placed = (
        P(FSDP, SEQ, None),
        P(FSDP, SEQ, None),
        P(FSDP, SEQ, None),
        P(FSDP, SEQ),
        P(FSDP, SEQ),
        P(),
        P(None, None, FSDP, None),
        P(None, FSDP, None),
        P(FSDP, None),
        P(FSDP, None),
        P(None, FSDP),
        P(FSDP),
        P(None, FSDP),
        P(None, FSDP),
    )
    return jax.shard_map(
        body,
        mesh=split,
        in_specs=placed,
        out_specs=(
            P(FSDP, SEQ, None),
            P(FSDP, SEQ, None),
            P(FSDP, SEQ, None),
            P(None, None, ALL, None),
            P(None, ALL, None),
            P(ALL, None),
            P(ALL, None),
            P(None, ALL),
            P(ALL),
            P(None, ALL),
            P(None, ALL),
        ),
        check_vma=False,
    )
```

```python
import functools
import math

import jax
import jax.numpy as jnp
from jax import lax
from jax.experimental import pallas as pl
from jax.experimental.pallas import tpu as pltpu
from jax.sharding import Mesh
from jax.sharding import PartitionSpec as P

HEADS = 16
EPSILON = 1e-05
NEGATIVE = -1e30
GELU_IN = math.sqrt(2.0 / math.pi)
GELU_CUBE = 0.044715
SEQ = ("y", "core")
FSDP = ("z", "x")
PLANE = ("x", "y", "core")
ALL = ("y", "core", "z", "x")
BF = jnp.bfloat16
F32 = jnp.float32
VMEM_LIMIT = 52 * 1024 * 1024


def matmul(left, right):
    return jnp.dot(left, right, preferred_element_type=F32)


def swap(value, axis, step):
    return lax.ppermute(value, axis, [(i, i ^ step) for i in range(lax.axis_size(axis))])


def norm_parts(values):
    centred = values - jnp.mean(values, axis=-1, keepdims=True)
    scale = lax.rsqrt(jnp.mean(centred * centred, axis=-1, keepdims=True) + EPSILON)
    return centred * scale, scale


def norm_back(normed, scale, gain, grad):
    inner = grad * gain
    means = jnp.mean(inner, axis=-1, keepdims=True)
    along = jnp.mean(inner * normed, axis=-1, keepdims=True)
    return (
        scale * (inner - means - normed * along),
        jnp.sum(grad * normed, axis=0, keepdims=True),
        jnp.sum(grad, axis=0, keepdims=True),
    )


def nt(left, right):
    return lax.dot_general(left, right, (((1,), (1,)), ((), ())), preferred_element_type=F32)


def tn(left, right):
    return lax.dot_general(left, right, (((0,), (0,)), ((), ())), preferred_element_type=F32)


def total_rows(values):
    return jnp.sum(values, axis=0, keepdims=True)


def call(kernel, outs, scratch, scalars, *operands, flops=0):
    vmem = pl.BlockSpec(memory_space=pltpu.VMEM)
    moved = sum(o.size * o.dtype.itemsize for o in operands)
    return pl.pallas_call(
        kernel,
        out_shape=[jax.ShapeDtypeStruct(shape, kind) for shape, kind in outs],
        in_specs=[pl.BlockSpec(memory_space=pltpu.SMEM)] + [vmem] * len(operands),
        out_specs=[vmem] * len(outs),
        scratch_shapes=[pltpu.VMEM(shape, kind) for shape, kind in scratch],
        compiler_params=pltpu.CompilerParams(vmem_limit_bytes=VMEM_LIMIT),
        cost_estimate=pl.CostEstimate(flops=flops, bytes_accessed=moved, transcendentals=0),
    )(scalars, *operands)


def softmax_rows(scores, bias):
    scores = scores + bias
    top = jnp.max(scores, axis=1, keepdims=True)
    raised = jnp.exp(scores - top)
    whole = jnp.maximum(jnp.sum(raised, axis=1, keepdims=True), 1.0)
    scale = jnp.where(top > 0.5 * NEGATIVE, 1.0 / whole, 0.0)
    return raised * scale, top, scale


def softmax_again(scores, bias, top, scale):
    return jnp.exp(scores + bias - top) * scale


def softmax_back(chance, chance_grad):
    return chance * (chance_grad - jnp.sum(chance * chance_grad, axis=1, keepdims=True))


def bias_of(query_seg, key_seg, query_pos=None, key_pos=None):
    allowed = (query_seg == key_seg) & (query_seg != 0)
    if query_pos is not None:
        allowed = allowed & (key_pos <= query_pos)
    return jnp.where(allowed, 0.0, NEGATIVE)


def self_forward(
    z_size, x_size, held, lane, heads, at, lines, row, seg, seg_line, pos, pos_line,
    weights, params, up_bias, normed, query, key, value, stats, mixed,
):
    z_place, x_place = at[0], at[1]
    width = row.shape[1]
    cut = query.shape[1]
    row_len = row.shape[0]
    block = min(row_len, 512)
    for j in range(z_size * x_size):
        kx, kz = (j % x_size) ^ x_place, (j // x_size) ^ z_place
        for m in range(3):
            weights[m, j * held : (j + 1) * held, :] = lines[kx, kz, m * held : (m + 1) * held, :]
        small = lines[kx, kz, 3 * held :, :].astype(F32)
        for r in range(13):
            o, c = divmod(r * lane, cut)
            params[r : r + 1, j * lane : (j + 1) * lane] = small[o : o + 1, c : c + lane]
    part = up_bias.shape[1] // x_size
    for xx in range(x_size):
        small = lines[xx ^ x_place, 0, 3 * held :, :].astype(F32)
        for r in range(part // lane):
            o, c = divmod((13 + r) * lane, cut)
            first = xx * part + r * lane
            up_bias[:, first : first + lane] = small[o : o + 1, c : c + lane]
    gain, shift = params[7:8, :], params[10:11, :]
    both = jnp.zeros((2, cut), F32)
    for j in range(width // cut):
        both = jnp.where(at[2] == j, params[0:2, j * cut : (j + 1) * cut], both)
    query_bias, value_bias = both[0:1], both[1:2]
    for b in range(row_len // block):
        rows = slice(b * block, (b + 1) * block)
        unit, _ = norm_parts(row[rows, :].astype(F32))
        h = (unit * gain + shift).astype(BF)
        normed[rows, :] = h
        query[rows, :] = (matmul(h, weights[0]) + query_bias).astype(BF)
        key[rows, :] = matmul(h, weights[1]).astype(BF)
        value[rows, :] = (matmul(h, weights[2]) + value_bias).astype(BF)
    size = cut // heads
    score_scale = 1.0 / math.sqrt(size)
    for b in range(row_len // block):
        rows = slice(b * block, (b + 1) * block)
        bias = bias_of(seg[rows, :], seg_line[...], pos[rows, :], pos_line[...])
        for h in range(heads):
            cols = slice(h * size, (h + 1) * size)
            scores = nt(query[rows, cols], key[:, cols]) * score_scale
            chance, top, scale = softmax_rows(scores, bias)
            stats[rows, h : h + 1] = top
            stats[rows, 64 + h : 65 + h] = scale
            mixed[rows, cols] = matmul(chance.astype(BF), value[:, cols]).astype(BF)


def matrix(rest, m):
    values = rest[:, m]
    return values.reshape(values.shape[0] * values.shape[1], values.shape[2])


def middle_forward(
    s_size, at, parts, inputs, rest, params, sources, seg, source_seg,
    after_self, after_cross, left, query, stats, keys, normed,
):
    width = inputs.shape[1]
    cut = width // s_size
    for j in range(s_size):
        left[:, 2 * width + j * cut : 2 * width + (j + 1) * cut] = parts[at[j]]
        for n in range(2):
            keys[n, :, j * cut : (j + 1) * cut] = sources[at[j], n]
    x1 = (
        inputs[...].astype(F32)
        + matmul(left[:, 2 * width :], matrix(rest, 1))
        + params[2:3, :]
    )
    after_self[...] = x1
    unit, _ = norm_parts(x1)
    left[:, :width] = (unit * params[8:9, :] + params[11:12, :]).astype(BF)
    query[...] = (matmul(left[:, :width], matrix(rest, 0)) + params[3:4, :]).astype(BF)
    bias = bias_of(seg[...], source_seg[...])
    size = width // HEADS
    score_scale = 1.0 / math.sqrt(size)
    for h in range(HEADS):
        cols = slice(h * size, (h + 1) * size)
        scores = nt(query[:, cols], keys[0, :, cols]) * score_scale
        chance, top, scale = softmax_rows(scores, bias)
        stats[:, h : h + 1] = top
        stats[:, 64 + h : 65 + h] = scale
        left[:, width + h * size : width + (h + 1) * size] = matmul(
            chance.astype(BF), keys[1, :, cols]
        ).astype(BF)
    x2 = x1 + matmul(left[:, width : 2 * width], matrix(rest, 2)) + params[5:6, :]
    after_cross[...] = x2
    unit, _ = norm_parts(x2)
    normed[...] = (unit * params[9:10, :] + params[12:13, :]).astype(BF)


def middle_backward(
    s_size, at, terms, out_grad, after_self, after_cross, rest, params, query,
    keys, stats, seg, source_seg,
    branch, self_grad, pair, sums,
):
    tokens, width = out_grad.shape
    cut = width // s_size
    size = width // HEADS
    score_scale = 1.0 / math.sqrt(size)
    down = out_grad[...].astype(F32)
    grad = terms[...]
    unit, scale = norm_parts(after_cross[...])
    moved, gain, shift = norm_back(unit, scale, params[9:10, :], grad)
    sums[2:3, :] = gain
    sums[5:6, :] = shift
    x2_grad = down + moved
    d2 = x2_grad.astype(BF)
    sums[6:7, :] = total_rows(d2.astype(F32))
    sums[7:8, :] = total_rows(down)
    for j in range(s_size):
        pair[at[j], :tokens, cut:] = d2[:, j * cut : (j + 1) * cut]
    head_grad = nt(d2, matrix(rest, 2)).astype(BF)
    bias = bias_of(seg[...], source_seg[...])
    per = HEADS // s_size
    grads = []
    for h in range(HEADS):
        cols = slice(h * size, (h + 1) * size)
        q, do = query[:, cols], head_grad[:, cols]
        k, v = keys[0, :, cols], keys[1, :, cols]
        scores = nt(q, k) * score_scale
        chance = softmax_again(scores, bias, stats[:, h : h + 1], stats[:, 64 + h : 65 + h])
        score_grad = softmax_back(chance, nt(do, v)).astype(BF)
        grads.append((matmul(score_grad, k) * score_scale).astype(BF))
        to = slice((h % per) * size, (h % per + 1) * size)
        pair[at[h // per], tokens:, to] = (tn(score_grad, q) * score_scale).astype(BF)
        to = slice(cut + to.start, cut + to.stop)
        pair[at[h // per], tokens:, to] = tn(chance.astype(BF), do).astype(BF)
    query_grad = jnp.concatenate(grads, axis=1)
    sums[8:9, :] = total_rows(query_grad.astype(F32))
    for j in range(s_size):
        pair[at[j], :tokens, :cut] = query_grad[:, j * cut : (j + 1) * cut]
    unit, scale = norm_parts(after_self[...])
    moved, gain, shift = norm_back(unit, scale, params[8:9, :], nt(query_grad, matrix(rest, 0)))
    sums[1:2, :] = gain
    sums[4:5, :] = shift
    x1_grad = x2_grad + moved
    self_grad[...] = x1_grad
    d1 = x1_grad.astype(BF)
    branch[...] = d1
    sums[9:10, :] = total_rows(d1.astype(F32))


def feed_forward(
    steps, normed, down, w_up, w_down, up_bias,
    activated, pre_grad, partial, bias_grad,
    held, total,
):
    step = pl.program_id(0)
    groups, z_size, share, columns = w_up.shape
    per = groups * share
    for z in range(z_size):
        held[z * per : (z + 1) * per, :] = w_up[:, z].reshape(per, columns)
    u = matmul(normed[...], held[...]) + up_bias[...]
    square = u * u
    bent = jnp.tanh(GELU_IN * (u + GELU_CUBE * square * u))
    half = 0.5 * (1.0 + bent)
    activated[...] = (u * half).astype(BF)
    slope = half + 0.5 * u * (1.0 - bent * bent) * (GELU_IN + 3.0 * GELU_IN * GELU_CUBE * square)
    du = (nt(down[...], w_down[...]) * slope).astype(BF)
    pre_grad[...] = du
    bias_grad[...] = total_rows(du.astype(F32))
    term = nt(du, held[...])

    @pl.when(step == 0)
    def _():
        total[...] = term

    @pl.when(step > 0)
    def _():
        total[...] += term

    @pl.when(step == steps - 1)
    def _():
        partial[...] = total[...].astype(BF)


def feed_forward_gradients(
    s_size, z_size, x_size, up_rows, at, normed, pre_grad, activated, down, w_down,
    out, mixed,
):
    width = normed.shape[1]
    half = pre_grad.shape[1] // 2
    places = z_size * x_size
    unit = out.shape[1] - 2 * z_size * up_rows
    for b in range(x_size * s_size):
        term = tn(activated[:, b * unit : (b + 1) * unit], down[...])
        out[b, 2 * z_size * up_rows :, :] = term.astype(BF)
    for t in range(width // 256):
        cols = slice(t * 256, (t + 1) * 256)
        mixed[:, cols] = matmul(activated[...], w_down[:, cols]).astype(BF)
    tile = places * up_rows
    for s in range(s_size):
        for i in range(2):
            term = tn(normed[:, s * tile : (s + 1) * tile], pre_grad[:, i * half : (i + 1) * half])
            term = term.astype(BF)
            for f in range(places):
                z, x = divmod(f, x_size)
                first = (i * z_size + z) * up_rows
                b = ((s % 2) * (s_size // 2) + s // 2) * x_size + x
                out[b, first : first + up_rows, :] = term[f * up_rows : (f + 1) * up_rows]


def self_backward(
    heads, at, branch, w_out, query, key, value, stats, seg, seg_line, pos, pos_line, weights, normed,
    cuts, partial, sums,
    grads, key_total, value_total,
):
    row_len, cut = query.shape
    block = min(row_len, 512)
    size = cut // heads
    score_scale = 1.0 / math.sqrt(size)
    for b in range(row_len // block):
        rows = slice(b * block, (b + 1) * block)
        head_grad = nt(branch[rows, :], w_out[...]).astype(BF)
        bias = bias_of(seg[rows, :], seg_line[...], pos[rows, :], pos_line[...])
        for h in range(heads):
            cols = slice(h * size, (h + 1) * size)
            q, do, k, v = query[rows, cols], head_grad[:, cols], key[:, cols], value[:, cols]
            chance = softmax_again(
                nt(q, k) * score_scale, bias, stats[rows, h : h + 1], stats[rows, 64 + h : 65 + h]
            )
            score_grad = softmax_back(chance, nt(do, v)).astype(BF)
            grads[rows, cols] = (matmul(score_grad, k) * score_scale).astype(BF)
            key_term = tn(score_grad, q) * score_scale
            value_term = tn(chance.astype(BF), do)
            if b == 0:
                key_total[:, cols] = key_term
                value_total[:, cols] = value_term
            else:
                key_total[:, cols] += key_term
                value_total[:, cols] += value_term
    grads[:, cut : 2 * cut] = key_total[...].astype(BF)
    grads[:, 2 * cut :] = value_total[...].astype(BF)
    sums[0:1, :] = total_rows(grads[:, :cut].astype(F32))
    sums[1:2, :] = total_rows(grads[:, 2 * cut :].astype(F32))
    tile = min(256, normed.shape[1])
    for t in range(normed.shape[1] // tile):
        rows = slice(t * tile, (t + 1) * tile)
        cuts[rows, :] = tn(normed[:, rows], grads[...]).astype(BF)
    for b in range(row_len // block):
        rows = slice(b * block, (b + 1) * block)
        grad = nt(grads[rows, :cut], weights[0]) + nt(grads[rows, cut : 2 * cut], weights[1])
        partial[rows, :] = (grad + nt(grads[rows, 2 * cut :], weights[2])).astype(BF)


def group_gradients(at, own, swapped, pair, branch_cut, sources, source_grad, out):
    (y_size, rows, _), cut = own.shape, branch_cut.shape[1]
    y_place = lax.div(at[2], 2)
    width = sources.shape[1]
    tile = min(256, width)
    for t in range(width // tile):
        to = slice(t * tile, (t + 1) * tile)
        for n in range(3):
            cols = slice(n * width + t * tile, n * width + (t + 1) * tile)
            right = branch_cut if n == 2 else pair
            first = n * cut if n < 2 else 0
            term = jnp.zeros((tile, cut), F32)
            for k in range(y_size):
                near = slice(k * rows, (k + 1) * rows)
                far = slice((y_size + k) * rows, (y_size + k + 1) * rows)
                term = term + tn(own[y_place ^ k, :, cols], right[near, first : first + cut])
                term = term + tn(swapped[y_place ^ k, :, cols], right[far, first : first + cut])
            out[to, n * cut : (n + 1) * cut] = term.astype(BF)
        for n in range(2):
            out[to, (3 + n) * cut : (4 + n) * cut] = tn(sources[:, to], source_grad[n]).astype(BF)


def last_step(
    lanes, at, line, others, inputs, params, self_grad, sums, cut_sums, up_bias_grad,
    grad_hidden, table, rows,
):
    unit, scale = norm_parts(inputs[...].astype(F32))
    grad = line[...] + jnp.sum(others[...].astype(F32), axis=0)
    moved, gain, shift = norm_back(unit, scale, params[7:8, :], grad)
    grad_hidden[...] = self_grad[...] + moved
    rows[...] = jnp.zeros(rows.shape, F32)
    rows[0:2, :] = cut_sums[0:2, :]
    rows[2:3, :] = sums[9:10, :]
    rows[3:4, :] = sums[8:9, :]
    rows[4:5, :] = cut_sums[2:3, :]
    rows[5:7, :] = sums[6:8, :]
    rows[7:8, :] = gain
    rows[8:10, :] = sums[1:3, :]
    rows[10:11, :] = shift
    rows[11:13, :] = sums[4:6, :]
    mine = up_bias_grad.shape[1] // 8
    at_lane = pl.ds(pl.multiple_of(at[0] * mine, mine), mine)
    for k in range(8):
        parts = [
            up_bias_grad[:, first : first + lanes]
            for first in range(k * lanes, up_bias_grad.shape[1], 8 * lanes)
        ]
        rows[16 + k : 17 + k, at_lane] = jnp.concatenate(parts, axis=1)
    table[...] = rows[...].T.astype(BF)


def gather_pair(value):
    lines = [value] + [swap(value, "y", k) for k in range(1, lax.axis_size("y"))]
    lines = jnp.concatenate(lines) if len(lines) > 1 else value
    return lines, swap(lines, "core", 1)


def gather_seq(value):
    return jnp.concatenate(gather_pair(value))


def scatter_seq(partial):
    line = partial[0].astype(F32) + swap(partial[1].astype(BF), "core", 1).astype(F32)
    total = line[0]
    for k in range(1, lax.axis_size("y")):
        total = total + swap(line[k].astype(BF), "y", k).astype(F32)
    return total


def exchange_seq(value):
    line = jnp.stack([value[0], swap(value[1], "core", 1)])
    lines = [line[:, 0]] + [swap(line[:, k], "y", k) for k in range(1, lax.axis_size("y"))]
    return jnp.stack(lines, axis=1)


def trade_z(parts):
    return lax.all_to_all(parts, "z", 0, 0)


def gather_z(value):
    return trade_z(jnp.broadcast_to(value, (lax.axis_size("z"),) + value.shape))


def behind(value, other):
    last = other[(-1,) * other.ndim].astype(F32) * 0.0
    return value + last.astype(value.dtype)


def pick(value, at, axis=0):
    return lax.dynamic_index_in_dim(value, at, axis, keepdims=False)


def body(
    hidden_in,
    memory,
    out_grad,
    segment_ids,
    memory_segments,
    deal,
    attn_in,
    attn_out,
    fc1,
    fc2,
    proj_bias,
    fc1_bias,
    norm_gain,
    norm_bias,
):
    y_size, z_size, x_size = lax.axis_size("y"), lax.axis_size("z"), lax.axis_size("x")
    s_size, f_size = y_size * 2, z_size * x_size
    y_place, core_place = lax.axis_index("y"), lax.axis_index("core")
    z_place, x_place = lax.axis_index("z"), lax.axis_index("x")
    s_place = y_place * 2 + core_place
    f_place = z_place * x_size + x_place
    place = s_place * f_size + f_place
    count = s_size * f_size
    tokens, width = hidden_in.shape[1:]
    sources_len = memory.shape[1]
    held = attn_in.shape[2]
    share = held // s_size
    lane = width // f_size
    cut = width // s_size
    row_len = s_size * tokens
    blocks = [(c, k) for c in range(2) for k in range(y_size)]
    block_of = [((j % 2) ^ core_place) * y_size + ((j // 2) ^ y_place) for j in range(s_size)]
    owners = jnp.stack([(y_place ^ k) * 2 + (core_place ^ c) for c, k in blocks])

    def cut_cols(value, at):
        return lax.dynamic_slice_in_dim(value, at * cut, cut, value.ndim - 1)

    here = jnp.stack([z_place, x_place, s_place, core_place]).astype(jnp.int32)
    block_list = jnp.stack(block_of).astype(jnp.int32)

    small = jnp.concatenate(
        [
            proj_bias.reshape(-1).astype(BF),
            norm_gain.reshape(-1).astype(BF),
            norm_bias.reshape(-1).astype(BF),
            fc1_bias.astype(BF),
        ]
    )
    small_len = small.shape[0]
    small_rows = -(-small_len // (16 * cut)) * 16
    small = jnp.pad(small, (0, small_rows * cut - small_len)).reshape(small_rows, cut)
    early = jnp.concatenate([cut_cols(attn_in[0], s_place).astype(BF).reshape(3 * held, cut), small])

    rest = jnp.concatenate(
        [
            lax.dynamic_slice_in_dim(attn_in[1, 0], s_place * share, share, 0),
            lax.dynamic_slice_in_dim(attn_out, s_place * share, share, 1).reshape(-1, width),
        ]
    ).astype(BF)
    labels = jnp.concatenate([segment_ids[0], memory_segments[0]]).astype(BF)
    label_rows = -(-labels.shape[0] // (16 * width)) * 16
    labels = jnp.pad(labels, (0, label_rows * width - labels.shape[0])).reshape(label_rows, width)
    row = jnp.concatenate([hidden_in[0], memory[0], labels])
    row_lines = [row] + [swap(row, "y", k) for k in range(1, y_size)]
    row_lines = jnp.concatenate(row_lines)
    row = jnp.concatenate([row_lines, swap(row_lines, "core", 1)])
    early_lines = [early] + [swap(early, "z", k) for k in range(1, z_size)]
    early_lines = jnp.stack(early_lines)
    unit = fc2.shape[0] // s_size
    hidden = x_size * fc2.shape[0]
    down_share = lax.dynamic_slice_in_dim(fc2, s_place * unit, unit, 0).astype(BF)
    down_lines = [swap(down_share, "x", k) for k in range(1, x_size)]
    send = behind(early_lines, down_lines[-1])
    down_lines = [behind(line, early_lines) for line in down_lines]
    down_lines = [[line] + [swap(line, "y", k) for k in range(1, y_size)] for line in down_lines]

    up_share = lax.dynamic_slice_in_dim(fc1, s_place * share, share, 0).astype(BF)
    up_share = up_share.reshape(share, z_size, hidden).transpose(1, 0, 2).reshape(z_size, -1, width)
    memory_cuts = cut_cols(attn_in[1, 1:], s_place).astype(BF).reshape(1, -1, width)
    memory_cuts = jnp.broadcast_to(memory_cuts, (z_size,) + memory_cuts.shape[1:])
    down_grad = out_grad[0]
    down_copies = jnp.broadcast_to(down_grad, (z_size,) + down_grad.shape)
    over_z = trade_z(jnp.concatenate([up_share, memory_cuts, down_copies], axis=1))
    down_all = over_z[:, -tokens:].reshape(z_size * tokens, width)
    over_z = over_z[:, :-tokens]

    rest = lax.all_gather(rest, FSDP + SEQ).reshape(count, 3, share, width)
    if share % 16:
        rest = rest.transpose(1, 0, 2, 3).reshape(1, 3, width, width)
    early = jnp.stack([early_lines] + [swap(send, "x", k) for k in range(1, x_size)])

    row = row.reshape(s_size, tokens + sources_len + label_rows, width)
    row_inputs = row[:, :tokens].reshape(row_len, width)
    labels = row[:, tokens + sources_len :].reshape(s_size, label_rows * width).astype(jnp.int32)
    row_seg = labels[:, :tokens].reshape(-1)
    row_sources = jnp.concatenate(
        [pick(row, block_of[j])[tokens : tokens + sources_len] for j in range(s_size)]
    )
    source_seg = jnp.concatenate(
        [pick(labels, block_of[j])[tokens : tokens + sources_len] for j in range(s_size)]
    )
    half_rows = tokens // 2
    offsets = jnp.arange(half_rows, dtype=jnp.int32)
    row_pos = (deal.reshape(s_size, 2)[owners][:, :, None] * half_rows + offsets).reshape(-1)
    row_places = (row_seg[:, None], row_seg[None], row_pos[:, None], row_pos[None])
    places = (segment_ids[0][:, None], source_seg[None])

    heads = HEADS // s_size
    weights, params, up_bias, normed_row, query, key, value, stats, self_cut = call(
        functools.partial(self_forward, z_size, x_size, held, lane, heads),
        [
            ((3, width, cut), BF),
            ((16, width), F32),
            ((1, hidden), F32),
            ((row_len, width), BF),
            ((row_len, cut), BF),
            ((row_len, cut), BF),
            ((row_len, cut), BF),
            ((row_len, 128), F32),
            ((row_len, cut), BF),
        ],
        [],
        behind(here, down_lines[-1][-1]),
        early,
        row_inputs,
        *row_places,
        flops=2 * row_len * cut * (3 * width + 2 * row_len),
    )
    parts = exchange_seq(self_cut.reshape(2, y_size, tokens, cut)).reshape(s_size, tokens, cut)

    late_z = behind(over_z, self_cut)
    memory_lines = late_z[:, up_share.shape[1] :].reshape(z_size, 2, held, cut)
    memory_lines = jnp.stack([memory_lines] + [swap(memory_lines, "x", k) for k in range(1, x_size)])
    w_memory = jnp.stack([pick(memory_lines, j ^ x_place) for j in range(x_size)])
    w_memory = w_memory.transpose(2, 1, 0, 3, 4).reshape(2, width, cut)
    source_key = matmul(row_sources, w_memory[0]).astype(BF)
    value_bias = cut_cols(params[4], s_place)
    source_value = (matmul(row_sources, w_memory[1]) + value_bias).astype(BF)
    sources_row = s_size * sources_len
    source_all = gather_seq(jnp.stack([source_key, source_value])[None])

    up_parts = behind(late_z[:, : up_share.shape[1]], source_all)
    up_parts = behind(behind(up_parts, parts), rest)
    up_parts = up_parts.reshape(z_size, share, hidden)

    after_self, after_cross, left, query_cross, cross_stats, source_keys, normed_three = call(
        functools.partial(middle_forward, s_size),
        [
            ((tokens, width), F32),
            ((tokens, width), F32),
            ((tokens, 3 * width), BF),
            ((tokens, width), BF),
            ((tokens, 128), F32),
            ((2, sources_row, width), BF),
            ((tokens, width), BF),
        ],
        [],
        block_list,
        parts,
        hidden_in[0],
        rest,
        params,
        source_all,
        *places,
        flops=2 * tokens * width * (3 * width + 2 * sources_row),
    )

    w_up = lax.all_gather(up_parts, PLANE).reshape(s_size * x_size, z_size, share, hidden)
    if share % 16:
        w_up = w_up.transpose(1, 0, 2, 3).reshape(1, 1, width, hidden)
    down_lines = [behind(jnp.concatenate(lines), parts) for lines in down_lines]
    down_lines = [jnp.concatenate([lines, swap(lines, "core", 1)]) for lines in down_lines]
    down_lines = [line.reshape(s_size, unit, width) for line in down_lines]
    down_lines = [
        jnp.concatenate([pick(line, block_of[j]) for j in range(s_size)]) for line in down_lines
    ]
    down_lines = jnp.stack([fc2.astype(BF)] + down_lines)
    w_down = jnp.concatenate([pick(down_lines, j ^ x_place) for j in range(x_size)])

    normed_all = gather_z(normed_three).reshape(z_size * tokens, width)
    group = z_size * tokens
    columns = 512
    activated, pre_grad, partial, grad_up_bias = pl.pallas_call(
        functools.partial(feed_forward, hidden // columns),
        grid=(hidden // columns,),
        out_shape=[
            jax.ShapeDtypeStruct((group, hidden), BF),
            jax.ShapeDtypeStruct((group, hidden), BF),
            jax.ShapeDtypeStruct((group, width), BF),
            jax.ShapeDtypeStruct((1, hidden), F32),
        ],
        in_specs=[
            pl.BlockSpec((group, width), lambda i: (0, 0)),
            pl.BlockSpec((group, width), lambda i: (0, 0)),
            pl.BlockSpec(w_up.shape[:3] + (columns,), lambda i: (0, 0, 0, i)),
            pl.BlockSpec((columns, width), lambda i: (i, 0)),
            pl.BlockSpec((1, columns), lambda i: (0, i)),
        ],
        out_specs=[
            pl.BlockSpec((group, columns), lambda i: (0, i)),
            pl.BlockSpec((group, columns), lambda i: (0, i)),
            pl.BlockSpec((group, width), lambda i: (0, 0)),
            pl.BlockSpec((1, columns), lambda i: (0, i)),
        ],
        scratch_shapes=[pltpu.VMEM((width, columns), BF), pltpu.VMEM((group, width), F32)],
        compiler_params=pltpu.CompilerParams(vmem_limit_bytes=VMEM_LIMIT),
        cost_estimate=pl.CostEstimate(
            flops=6 * group * width * hidden, bytes_accessed=12 << 20, transcendentals=group * hidden
        ),
    )(normed_all, down_all, w_up, w_down, up_bias)
    terms = partial.reshape(z_size, tokens, width)
    terms = [swap(pick(terms, z_place ^ k), "z", k) if k else pick(terms, z_place) for k in range(z_size)]
    terms = sum(term.astype(F32) for term in terms)
    up_rows = width // count
    half = hidden // 2
    first_rows = 2 * z_size * up_rows
    if up_rows % 16:
        late = behind(activated, partial)
        grad_down = tn(late, down_all).astype(BF)
        grad_up = [tn(normed_all, pre_grad[:, i * half : (i + 1) * half]) for i in range(2)]
        grad_up = jnp.stack(grad_up).astype(BF)
        grad_up = grad_up.reshape(2, y_size, 2, z_size, x_size, up_rows, half)
        grad_up = grad_up.transpose(2, 1, 4, 0, 3, 5, 6).reshape(x_size * s_size, -1, width)
        grad_down = grad_down.reshape(x_size * s_size, unit, width)
        grad_mlp = jnp.concatenate([grad_up, grad_down], axis=1)
        mixed_down = matmul(activated, w_down).astype(BF)
    else:
        grad_mlp, mixed_down = call(
            functools.partial(feed_forward_gradients, s_size, z_size, x_size, up_rows),
            [((x_size * s_size, first_rows + unit, width), BF), ((group, width), BF)],
            [],
            behind(here, partial),
            normed_all,
            pre_grad,
            activated,
            down_all,
            w_down,
            flops=6 * group * width * hidden,
        )
    left_own = lax.all_gather(left, "y")
    terms = behind(behind(terms, mixed_down), left_own)
    grad_mlp = lax.psum_scatter(grad_mlp, ("core", "y", "x"), scatter_dimension=0)
    grad_up = grad_mlp[:-unit].reshape(2, z_size, up_rows, half)
    owner = [
        (((y * 2 + c) * z_size + z) * x_size + x, ((z * 2 + c) * y_size + y) * x_size + x)
        for y in range(y_size)
        for c in range(2)
        for z in range(z_size)
        for x in range(x_size)
    ]
    grad_down = lax.ppermute(grad_mlp[-unit:], ALL, owner).astype(F32)
    grad_up = jnp.stack(
        [
            swap(pick(grad_up, z_place ^ k, 1), "z", k) if k else pick(grad_up, z_place, 1)
            for k in range(z_size)
        ]
    )
    grad_up = jnp.stack([pick(grad_up, z_place ^ j) for j in range(z_size)])
    grad_up = grad_up.transpose(2, 0, 1, 3).reshape(up_rows, -1).astype(F32)

    branch, self_grad, pair, sums = call(
        functools.partial(middle_backward, s_size),
        [
            ((tokens, width), BF),
            ((tokens, width), F32),
            ((s_size, tokens + sources_row, 2 * cut), BF),
            ((16, width), F32),
        ],
        [],
        block_list,
        terms,
        down_grad,
        after_self,
        after_cross,
        rest,
        params,
        query_cross,
        source_keys,
        cross_stats,
        *places,
        flops=2 * tokens * width * (2 * width + 5 * sources_row),
    )

    branch_row = gather_seq(branch)
    left_swapped = swap(behind(left_own, terms), "core", 1)
    w_out = rest[:, 1].reshape(width, width)
    w_out = lax.dynamic_slice_in_dim(w_out, s_place * cut, cut, 0)
    self_cuts, partial, cut_sums = call(
        functools.partial(self_backward, heads),
        [((width, 3 * cut), BF), ((row_len, width), BF), ((8, cut), F32)],
        [((row_len, 3 * cut), BF), ((row_len, cut), F32), ((row_len, cut), F32)],
        here,
        branch_row,
        w_out,
        query,
        key,
        value,
        stats,
        *row_places,
        weights,
        normed_row,
        flops=2 * row_len * cut * (7 * width + 5 * row_len),
    )

    pair = exchange_seq(pair.reshape((2, y_size) + pair.shape[1:])).reshape(pair.shape)
    pair = behind(pair, self_cuts)
    source_grad = jnp.sum(pair[:, tokens:].astype(F32), axis=0).astype(BF)
    source_grad = jnp.stack([source_grad[:, :cut], source_grad[:, cut:]])
    pair = pair[:, :tokens].reshape(row_len, 2 * cut)

    results = trade_z(behind(mixed_down, branch).reshape(z_size, tokens, width))
    result = after_cross + jnp.sum(results.astype(F32), axis=0) + params[6]
    def whole_columns(grads, number):
        grads = jnp.sum(grads.astype(F32), axis=1).reshape(s_size, up_rows, number, cut)
        return grads.transpose(2, 1, 0, 3).reshape(number, up_rows, width)

    grad_memory = nt(source_grad[0], w_memory[0]) + nt(source_grad[1], w_memory[1])
    grad_memory = grad_memory.reshape(s_size, sources_len, width)
    grad_memory = jnp.stack([pick(grad_memory, owners[j]) for j in range(s_size)])
    grad_memory = scatter_seq(grad_memory.reshape(2, y_size, sources_len, width))

    partial = partial.reshape(2, y_size, tokens, width)
    line = partial[0].astype(F32) + swap(partial[1], "core", 1).astype(F32)
    others = jnp.stack([swap(line[k].astype(BF), "y", k) for k in range(1, y_size)])
    cut_sums = jnp.concatenate([cut_sums[:2], jnp.sum(source_grad[1].astype(F32), axis=0)[None]])
    cut_sums = lax.dynamic_update_slice(
        jnp.zeros((3, width), F32), cut_sums, (jnp.int32(0), (s_place * cut).astype(jnp.int32))
    )
    grad_hidden, table = call(
        functools.partial(last_step, up_rows),
        [((tokens, width), F32), ((width, 128), BF)],
        [((128, width), F32)],
        here,
        line[0],
        others,
        hidden_in[0],
        params,
        self_grad,
        sums,
        cut_sums,
        grad_up_bias,
    )

    (group_cuts,) = call(
        group_gradients,
        [((width, 5 * cut), BF)],
        [],
        here,
        left_own,
        left_swapped,
        pair,
        cut_cols(branch_row, s_place),
        row_sources,
        source_grad,
        flops=2 * row_len * cut * 3 * width,
    )
    group_cuts = group_cuts.reshape(s_size * z_size, x_size, up_rows, 5 * cut)
    kept = pick(group_cuts, x_place, 1).astype(F32)
    for k in range(1, x_size):
        kept = kept + swap(pick(group_cuts, x_place ^ k, 1), "x", k).astype(F32)

    self_cuts = behind(self_cuts, results).reshape(count, up_rows, 3 * cut)
    self_cuts = lax.all_to_all(self_cuts, ALL, 0, 0).reshape(s_size, f_size, up_rows, 3 * cut)
    kept = behind(behind(behind(kept, self_cuts), grad_memory), grad_up)
    table = behind(behind(table, self_cuts), grad_up)
    table = lax.all_to_all(table.reshape(count, up_rows, 128), ALL, 0, 0)
    table = jnp.sum(table.astype(F32), axis=0).T
    kept = behind(kept, table)
    kept = lax.all_to_all(kept.astype(BF), ("y", "core", "z"), 0, 0)
    kept = behind(kept, grad_down)
    group_cuts = whole_columns(kept.reshape(s_size, z_size, up_rows, 5 * cut), 5)
    self_cuts = whole_columns(self_cuts, 3)
    return (
        result.astype(BF)[None],
        grad_hidden[None],
        grad_memory[None],
        jnp.stack([self_cuts, jnp.concatenate([group_cuts[:1], group_cuts[3:]])]),
        jnp.stack([group_cuts[2], group_cuts[1]]),
        grad_up,
        grad_down,
        table[:7],
        table[16:24].reshape(-1),
        table[7:10],
        table[10:13],
    )


def solution(mesh):
    seq, fsdp = mesh.shape["seq"], mesh.shape["fsdp"]
    split = Mesh(mesh.devices.reshape(seq // 2, 2, 4, fsdp // 4), ALL)
    placed = (
        P(FSDP, SEQ, None),
        P(FSDP, SEQ, None),
        P(FSDP, SEQ, None),
        P(FSDP, SEQ),
        P(FSDP, SEQ),
        P(),
        P(None, None, FSDP, None),
        P(None, FSDP, None),
        P(FSDP, None),
        P(FSDP, None),
        P(None, FSDP),
        P(FSDP),
        P(None, FSDP),
        P(None, FSDP),
    )
    return jax.shard_map(
        body,
        mesh=split,
        in_specs=placed,
        out_specs=(
            P(FSDP, SEQ, None),
            P(FSDP, SEQ, None),
            P(FSDP, SEQ, None),
            P(None, None, ALL, None),
            P(None, ALL, None),
            P(ALL, None),
            P(ALL, None),
            P(None, ALL),
            P(ALL),
            P(None, ALL),
            P(None, ALL),
        ),
        check_vma=False,
    )
```

```python
import functools
import math

import jax
import jax.numpy as jnp
from jax import lax
from jax.experimental import pallas as pl
from jax.experimental.pallas import tpu as pltpu
from jax.sharding import Mesh
from jax.sharding import PartitionSpec as P

HEADS = 16
EPSILON = 1e-05
NEGATIVE = -1e30
GELU_IN = math.sqrt(2.0 / math.pi)
GELU_CUBE = 0.044715
SEQ = ("y", "core")
FSDP = ("z", "x")
PLANE = ("x", "y", "core")
ALL = ("y", "core", "z", "x")
BF = jnp.bfloat16
F32 = jnp.float32
VMEM_LIMIT = 52 * 1024 * 1024


def matmul(left, right):
    return jnp.dot(left, right, preferred_element_type=F32)


def swap(value, axis, step):
    return lax.ppermute(value, axis, [(i, i ^ step) for i in range(lax.axis_size(axis))])


def norm_parts(values):
    centred = values - jnp.mean(values, axis=-1, keepdims=True)
    scale = lax.rsqrt(jnp.mean(centred * centred, axis=-1, keepdims=True) + EPSILON)
    return centred * scale, scale


def norm_back(normed, scale, gain, grad):
    inner = grad * gain
    means = jnp.mean(inner, axis=-1, keepdims=True)
    along = jnp.mean(inner * normed, axis=-1, keepdims=True)
    return (
        scale * (inner - means - normed * along),
        jnp.sum(grad * normed, axis=0, keepdims=True),
        jnp.sum(grad, axis=0, keepdims=True),
    )


def nt(left, right):
    return lax.dot_general(left, right, (((1,), (1,)), ((), ())), preferred_element_type=F32)


def tn(left, right):
    return lax.dot_general(left, right, (((0,), (0,)), ((), ())), preferred_element_type=F32)


def total_rows(values):
    return jnp.sum(values, axis=0, keepdims=True)


def call(kernel, outs, scratch, scalars, *operands, flops=0):
    vmem = pl.BlockSpec(memory_space=pltpu.VMEM)
    moved = sum(o.size * o.dtype.itemsize for o in operands)
    return pl.pallas_call(
        kernel,
        out_shape=[jax.ShapeDtypeStruct(shape, kind) for shape, kind in outs],
        in_specs=[pl.BlockSpec(memory_space=pltpu.SMEM)] + [vmem] * len(operands),
        out_specs=[vmem] * len(outs),
        scratch_shapes=[pltpu.VMEM(shape, kind) for shape, kind in scratch],
        compiler_params=pltpu.CompilerParams(vmem_limit_bytes=VMEM_LIMIT),
        cost_estimate=pl.CostEstimate(flops=flops, bytes_accessed=moved, transcendentals=0),
    )(scalars, *operands)


def softmax_rows(scores, bias):
    scores = scores + bias
    top = jnp.max(scores, axis=1, keepdims=True)
    raised = jnp.exp(scores - top)
    whole = jnp.maximum(jnp.sum(raised, axis=1, keepdims=True), 1.0)
    scale = jnp.where(top > 0.5 * NEGATIVE, 1.0 / whole, 0.0)
    return raised * scale, top, scale


def softmax_again(scores, bias, top, scale):
    return jnp.exp(scores + bias - top) * scale


def softmax_back(chance, chance_grad):
    return chance * (chance_grad - jnp.sum(chance * chance_grad, axis=1, keepdims=True))


def bias_of(query_seg, key_seg, query_pos=None, key_pos=None):
    allowed = (query_seg == key_seg) & (query_seg != 0)
    if query_pos is not None:
        allowed = allowed & (key_pos <= query_pos)
    return jnp.where(allowed, 0.0, NEGATIVE)


def self_forward(
    z_size, x_size, held, lane, heads, at, lines, row, seg, seg_line, pos, pos_line,
    weights, params, up_bias, normed, query, key, value, stats, mixed,
):
    z_place, x_place = at[0], at[1]
    width = row.shape[1]
    cut = query.shape[1]
    row_len = row.shape[0]
    block = min(row_len, 512)
    for j in range(z_size * x_size):
        kx, kz = (j % x_size) ^ x_place, (j // x_size) ^ z_place
        for m in range(3):
            weights[m, j * held : (j + 1) * held, :] = lines[kx, kz, m * held : (m + 1) * held, :]
        small = lines[kx, kz, 3 * held :, :].astype(F32)
        for r in range(13):
            o, c = divmod(r * lane, cut)
            params[r : r + 1, j * lane : (j + 1) * lane] = small[o : o + 1, c : c + lane]
    part = up_bias.shape[1] // x_size
    for xx in range(x_size):
        small = lines[xx ^ x_place, 0, 3 * held :, :].astype(F32)
        for r in range(part // lane):
            o, c = divmod((13 + r) * lane, cut)
            first = xx * part + r * lane
            up_bias[:, first : first + lane] = small[o : o + 1, c : c + lane]
    gain, shift = params[7:8, :], params[10:11, :]
    both = jnp.zeros((2, cut), F32)
    for j in range(width // cut):
        both = jnp.where(at[2] == j, params[0:2, j * cut : (j + 1) * cut], both)
    query_bias, value_bias = both[0:1], both[1:2]
    for b in range(row_len // block):
        rows = slice(b * block, (b + 1) * block)
        unit, _ = norm_parts(row[rows, :].astype(F32))
        h = (unit * gain + shift).astype(BF)
        normed[rows, :] = h
        query[rows, :] = (matmul(h, weights[0]) + query_bias).astype(BF)
        key[rows, :] = matmul(h, weights[1]).astype(BF)
        value[rows, :] = (matmul(h, weights[2]) + value_bias).astype(BF)
    size = cut // heads
    score_scale = 1.0 / math.sqrt(size)
    for b in range(row_len // block):
        rows = slice(b * block, (b + 1) * block)
        bias = bias_of(seg[rows, :], seg_line[...], pos[rows, :], pos_line[...])
        for h in range(heads):
            cols = slice(h * size, (h + 1) * size)
            scores = nt(query[rows, cols], key[:, cols]) * score_scale
            chance, top, scale = softmax_rows(scores, bias)
            stats[rows, h : h + 1] = top
            stats[rows, 64 + h : 65 + h] = scale
            mixed[rows, cols] = matmul(chance.astype(BF), value[:, cols]).astype(BF)


def matrix(rest, m):
    values = rest[:, m]
    return values.reshape(values.shape[0] * values.shape[1], values.shape[2])


def middle_forward(
    s_size, at, parts, inputs, rest, params, sources, seg, source_seg,
    after_self, after_cross, left, query, stats, keys, normed,
):
    width = inputs.shape[1]
    cut = width // s_size
    for j in range(s_size):
        left[:, 2 * width + j * cut : 2 * width + (j + 1) * cut] = parts[at[j]]
        for n in range(2):
            keys[n, :, j * cut : (j + 1) * cut] = sources[at[j], n]
    x1 = (
        inputs[...].astype(F32)
        + matmul(left[:, 2 * width :], matrix(rest, 1))
        + params[2:3, :]
    )
    after_self[...] = x1
    unit, _ = norm_parts(x1)
    left[:, :width] = (unit * params[8:9, :] + params[11:12, :]).astype(BF)
    query[...] = (matmul(left[:, :width], matrix(rest, 0)) + params[3:4, :]).astype(BF)
    bias = bias_of(seg[...], source_seg[...])
    size = width // HEADS
    score_scale = 1.0 / math.sqrt(size)
    for h in range(HEADS):
        cols = slice(h * size, (h + 1) * size)
        scores = nt(query[:, cols], keys[0, :, cols]) * score_scale
        chance, top, scale = softmax_rows(scores, bias)
        stats[:, h : h + 1] = top
        stats[:, 64 + h : 65 + h] = scale
        left[:, width + h * size : width + (h + 1) * size] = matmul(
            chance.astype(BF), keys[1, :, cols]
        ).astype(BF)
    x2 = x1 + matmul(left[:, width : 2 * width], matrix(rest, 2)) + params[5:6, :]
    after_cross[...] = x2
    unit, _ = norm_parts(x2)
    normed[...] = (unit * params[9:10, :] + params[12:13, :]).astype(BF)


def middle_backward(
    s_size, at, terms, out_grad, after_self, after_cross, rest, params, query,
    keys, stats, seg, source_seg,
    branch, self_grad, pair, sums,
):
    tokens, width = out_grad.shape
    cut = width // s_size
    size = width // HEADS
    score_scale = 1.0 / math.sqrt(size)
    down = out_grad[...].astype(F32)
    grad = terms[...]
    unit, scale = norm_parts(after_cross[...])
    moved, gain, shift = norm_back(unit, scale, params[9:10, :], grad)
    sums[2:3, :] = gain
    sums[5:6, :] = shift
    x2_grad = down + moved
    d2 = x2_grad.astype(BF)
    sums[6:7, :] = total_rows(d2.astype(F32))
    sums[7:8, :] = total_rows(down)
    for j in range(s_size):
        pair[at[j], :tokens, cut:] = d2[:, j * cut : (j + 1) * cut]
    head_grad = nt(d2, matrix(rest, 2)).astype(BF)
    bias = bias_of(seg[...], source_seg[...])
    per = HEADS // s_size
    grads = []
    for h in range(HEADS):
        cols = slice(h * size, (h + 1) * size)
        q, do = query[:, cols], head_grad[:, cols]
        k, v = keys[0, :, cols], keys[1, :, cols]
        scores = nt(q, k) * score_scale
        chance = softmax_again(scores, bias, stats[:, h : h + 1], stats[:, 64 + h : 65 + h])
        score_grad = softmax_back(chance, nt(do, v)).astype(BF)
        grads.append((matmul(score_grad, k) * score_scale).astype(BF))
        to = slice((h % per) * size, (h % per + 1) * size)
        pair[at[h // per], tokens:, to] = (tn(score_grad, q) * score_scale).astype(BF)
        to = slice(cut + to.start, cut + to.stop)
        pair[at[h // per], tokens:, to] = tn(chance.astype(BF), do).astype(BF)
    query_grad = jnp.concatenate(grads, axis=1)
    sums[8:9, :] = total_rows(query_grad.astype(F32))
    for j in range(s_size):
        pair[at[j], :tokens, :cut] = query_grad[:, j * cut : (j + 1) * cut]
    unit, scale = norm_parts(after_self[...])
    moved, gain, shift = norm_back(unit, scale, params[8:9, :], nt(query_grad, matrix(rest, 0)))
    sums[1:2, :] = gain
    sums[4:5, :] = shift
    x1_grad = x2_grad + moved
    self_grad[...] = x1_grad
    d1 = x1_grad.astype(BF)
    branch[...] = d1
    sums[9:10, :] = total_rows(d1.astype(F32))


def feed_forward(
    steps, normed, down, w_up, w_down, up_bias,
    activated, pre_grad, partial, bias_grad,
    held, total,
):
    step = pl.program_id(0)
    groups, z_size, share, columns = w_up.shape
    per = groups * share
    for z in range(z_size):
        held[z * per : (z + 1) * per, :] = w_up[:, z].reshape(per, columns)
    u = matmul(normed[...], held[...]) + up_bias[...]
    square = u * u
    bent = jnp.tanh(GELU_IN * (u + GELU_CUBE * square * u))
    half = 0.5 * (1.0 + bent)
    activated[...] = (u * half).astype(BF)
    slope = half + 0.5 * u * (1.0 - bent * bent) * (GELU_IN + 3.0 * GELU_IN * GELU_CUBE * square)
    du = (nt(down[...], w_down[...]) * slope).astype(BF)
    pre_grad[...] = du
    bias_grad[...] = total_rows(du.astype(F32))
    term = nt(du, held[...])

    @pl.when(step == 0)
    def _():
        total[...] = term

    @pl.when(step > 0)
    def _():
        total[...] += term

    @pl.when(step == steps - 1)
    def _():
        partial[...] = total[...].astype(BF)


def feed_forward_gradients(
    s_size, z_size, x_size, up_rows, at, normed, pre_grad, activated, down, w_down,
    out, mixed,
):
    width = normed.shape[1]
    half = pre_grad.shape[1] // 2
    places = z_size * x_size
    unit = out.shape[1] - 2 * z_size * up_rows
    for b in range(x_size * s_size):
        term = tn(activated[:, b * unit : (b + 1) * unit], down[...])
        out[b, 2 * z_size * up_rows :, :] = term.astype(BF)
    for t in range(width // 256):
        cols = slice(t * 256, (t + 1) * 256)
        mixed[:, cols] = matmul(activated[...], w_down[:, cols]).astype(BF)
    tile = places * up_rows
    for s in range(s_size):
        for i in range(2):
            term = tn(normed[:, s * tile : (s + 1) * tile], pre_grad[:, i * half : (i + 1) * half])
            term = term.astype(BF)
            for f in range(places):
                z, x = divmod(f, x_size)
                first = (i * z_size + z) * up_rows
                b = ((s % 2) * (s_size // 2) + s // 2) * x_size + x
                out[b, first : first + up_rows, :] = term[f * up_rows : (f + 1) * up_rows]


def self_backward(
    heads, at, branch, w_out, query, key, value, stats, seg, seg_line, pos, pos_line, weights, normed,
    cuts, partial, sums,
    grads, key_total, value_total,
):
    row_len, cut = query.shape
    block = min(row_len, 512)
    size = cut // heads
    score_scale = 1.0 / math.sqrt(size)
    for b in range(row_len // block):
        rows = slice(b * block, (b + 1) * block)
        head_grad = nt(branch[rows, :], w_out[...]).astype(BF)
        bias = bias_of(seg[rows, :], seg_line[...], pos[rows, :], pos_line[...])
        for h in range(heads):
            cols = slice(h * size, (h + 1) * size)
            q, do, k, v = query[rows, cols], head_grad[:, cols], key[:, cols], value[:, cols]
            chance = softmax_again(
                nt(q, k) * score_scale, bias, stats[rows, h : h + 1], stats[rows, 64 + h : 65 + h]
            )
            score_grad = softmax_back(chance, nt(do, v)).astype(BF)
            grads[rows, cols] = (matmul(score_grad, k) * score_scale).astype(BF)
            key_term = tn(score_grad, q) * score_scale
            value_term = tn(chance.astype(BF), do)
            if b == 0:
                key_total[:, cols] = key_term
                value_total[:, cols] = value_term
            else:
                key_total[:, cols] += key_term
                value_total[:, cols] += value_term
    grads[:, cut : 2 * cut] = key_total[...].astype(BF)
    grads[:, 2 * cut :] = value_total[...].astype(BF)
    sums[0:1, :] = total_rows(grads[:, :cut].astype(F32))
    sums[1:2, :] = total_rows(grads[:, 2 * cut :].astype(F32))
    tile = min(256, normed.shape[1])
    for t in range(normed.shape[1] // tile):
        rows = slice(t * tile, (t + 1) * tile)
        cuts[rows, :] = tn(normed[:, rows], grads[...]).astype(BF)
    for b in range(row_len // block):
        rows = slice(b * block, (b + 1) * block)
        grad = nt(grads[rows, :cut], weights[0]) + nt(grads[rows, cut : 2 * cut], weights[1])
        partial[rows, :] = (grad + nt(grads[rows, 2 * cut :], weights[2])).astype(BF)


def group_gradients(at, own, swapped, pair, branch_cut, sources, source_grad, out):
    (y_size, rows, _), cut = own.shape, branch_cut.shape[1]
    y_place = lax.div(at[2], 2)
    width = sources.shape[1]
    tile = min(256, width)
    for t in range(width // tile):
        to = slice(t * tile, (t + 1) * tile)
        for n in range(3):
            cols = slice(n * width + t * tile, n * width + (t + 1) * tile)
            right = branch_cut if n == 2 else pair
            first = n * cut if n < 2 else 0
            term = jnp.zeros((tile, cut), F32)
            for k in range(y_size):
                near = slice(k * rows, (k + 1) * rows)
                far = slice((y_size + k) * rows, (y_size + k + 1) * rows)
                term = term + tn(own[y_place ^ k, :, cols], right[near, first : first + cut])
                term = term + tn(swapped[y_place ^ k, :, cols], right[far, first : first + cut])
            out[to, n * cut : (n + 1) * cut] = term.astype(BF)
        for n in range(2):
            out[to, (3 + n) * cut : (4 + n) * cut] = tn(sources[:, to], source_grad[n]).astype(BF)


def last_step(
    lanes, at, line, others, inputs, params, self_grad, sums, cut_sums, up_bias_grad,
    grad_hidden, table, rows,
):
    unit, scale = norm_parts(inputs[...].astype(F32))
    grad = line[...] + jnp.sum(others[...].astype(F32), axis=0)
    moved, gain, shift = norm_back(unit, scale, params[7:8, :], grad)
    grad_hidden[...] = self_grad[...] + moved
    rows[...] = jnp.zeros(rows.shape, F32)
    rows[0:2, :] = cut_sums[0:2, :]
    rows[2:3, :] = sums[9:10, :]
    rows[3:4, :] = sums[8:9, :]
    rows[4:5, :] = cut_sums[2:3, :]
    rows[5:7, :] = sums[6:8, :]
    rows[7:8, :] = gain
    rows[8:10, :] = sums[1:3, :]
    rows[10:11, :] = shift
    rows[11:13, :] = sums[4:6, :]
    mine = up_bias_grad.shape[1] // 8
    at_lane = pl.ds(pl.multiple_of(at[0] * mine, mine), mine)
    for k in range(8):
        parts = [
            up_bias_grad[:, first : first + lanes]
            for first in range(k * lanes, up_bias_grad.shape[1], 8 * lanes)
        ]
        rows[16 + k : 17 + k, at_lane] = jnp.concatenate(parts, axis=1)
    table[...] = rows[...].T.astype(BF)


def gather_pair(value):
    lines = [value] + [swap(value, "y", k) for k in range(1, lax.axis_size("y"))]
    lines = jnp.concatenate(lines) if len(lines) > 1 else value
    return lines, swap(lines, "core", 1)


def gather_seq(value):
    return jnp.concatenate(gather_pair(value))


def scatter_seq(partial):
    line = partial[0].astype(F32) + swap(partial[1].astype(BF), "core", 1).astype(F32)
    total = line[0]
    for k in range(1, lax.axis_size("y")):
        total = total + swap(line[k].astype(BF), "y", k).astype(F32)
    return total


def exchange_seq(value):
    line = jnp.stack([value[0], swap(value[1], "core", 1)])
    lines = [line[:, 0]] + [swap(line[:, k], "y", k) for k in range(1, lax.axis_size("y"))]
    return jnp.stack(lines, axis=1)


def trade_z(parts):
    return lax.all_to_all(parts, "z", 0, 0)


def gather_z(value):
    return trade_z(jnp.broadcast_to(value, (lax.axis_size("z"),) + value.shape))


def behind(value, other):
    last = other[(-1,) * other.ndim].astype(F32) * 0.0
    return value + last.astype(value.dtype)


def pick(value, at, axis=0):
    return lax.dynamic_index_in_dim(value, at, axis, keepdims=False)


def body(
    hidden_in,
    memory,
    out_grad,
    segment_ids,
    memory_segments,
    deal,
    attn_in,
    attn_out,
    fc1,
    fc2,
    proj_bias,
    fc1_bias,
    norm_gain,
    norm_bias,
):
    y_size, z_size, x_size = lax.axis_size("y"), lax.axis_size("z"), lax.axis_size("x")
    s_size, f_size = y_size * 2, z_size * x_size
    y_place, core_place = lax.axis_index("y"), lax.axis_index("core")
    z_place, x_place = lax.axis_index("z"), lax.axis_index("x")
    s_place = y_place * 2 + core_place
    f_place = z_place * x_size + x_place
    place = s_place * f_size + f_place
    count = s_size * f_size
    tokens, width = hidden_in.shape[1:]
    sources_len = memory.shape[1]
    held = attn_in.shape[2]
    share = held // s_size
    lane = width // f_size
    cut = width // s_size
    row_len = s_size * tokens
    blocks = [(c, k) for c in range(2) for k in range(y_size)]
    block_of = [((j % 2) ^ core_place) * y_size + ((j // 2) ^ y_place) for j in range(s_size)]
    owners = jnp.stack([(y_place ^ k) * 2 + (core_place ^ c) for c, k in blocks])

    def cut_cols(value, at):
        return lax.dynamic_slice_in_dim(value, at * cut, cut, value.ndim - 1)

    here = jnp.stack([z_place, x_place, s_place, core_place]).astype(jnp.int32)
    block_list = jnp.stack(block_of).astype(jnp.int32)

    small = jnp.concatenate(
        [
            proj_bias.reshape(-1).astype(BF),
            norm_gain.reshape(-1).astype(BF),
            norm_bias.reshape(-1).astype(BF),
            fc1_bias.astype(BF),
        ]
    )
    small_len = small.shape[0]
    small_rows = -(-small_len // (16 * cut)) * 16
    small = jnp.pad(small, (0, small_rows * cut - small_len)).reshape(small_rows, cut)
    early = jnp.concatenate([cut_cols(attn_in[0], s_place).astype(BF).reshape(3 * held, cut), small])

    rest = jnp.concatenate(
        [
            lax.dynamic_slice_in_dim(attn_in[1, 0], s_place * share, share, 0),
            lax.dynamic_slice_in_dim(attn_out, s_place * share, share, 1).reshape(-1, width),
        ]
    ).astype(BF)
    labels = jnp.concatenate([segment_ids[0], memory_segments[0]]).astype(BF)
    label_rows = -(-labels.shape[0] // (16 * width)) * 16
    labels = jnp.pad(labels, (0, label_rows * width - labels.shape[0])).reshape(label_rows, width)
    row = jnp.concatenate([hidden_in[0], memory[0], labels])
    row_lines = [row] + [swap(row, "y", k) for k in range(1, y_size)]
    row_lines = jnp.concatenate(row_lines)
    row = jnp.concatenate([row_lines, swap(row_lines, "core", 1)])
    early_lines = [early] + [swap(early, "z", k) for k in range(1, z_size)]
    early_lines = jnp.stack(early_lines)
    unit = fc2.shape[0] // s_size
    hidden = x_size * fc2.shape[0]
    down_share = lax.dynamic_slice_in_dim(fc2, s_place * unit, unit, 0).astype(BF)
    down_lines = [swap(down_share, "x", k) for k in range(1, x_size)]
    send = behind(early_lines, down_lines[-1])
    down_lines = [behind(line, early_lines) for line in down_lines]
    down_lines = [[line] + [swap(line, "y", k) for k in range(1, y_size)] for line in down_lines]

    up_share = lax.dynamic_slice_in_dim(fc1, s_place * share, share, 0).astype(BF)
    up_share = up_share.reshape(share, z_size, hidden).transpose(1, 0, 2).reshape(z_size, -1, width)
    memory_cuts = cut_cols(attn_in[1, 1:], s_place).astype(BF).reshape(1, -1, width)
    memory_cuts = jnp.broadcast_to(memory_cuts, (z_size,) + memory_cuts.shape[1:])
    down_grad = out_grad[0]
    down_copies = jnp.broadcast_to(down_grad, (z_size,) + down_grad.shape)
    over_z = trade_z(jnp.concatenate([up_share, memory_cuts, down_copies], axis=1))
    down_all = over_z[:, -tokens:].reshape(z_size * tokens, width)
    over_z = over_z[:, :-tokens]

    rest = lax.all_gather(rest, FSDP + SEQ).reshape(count, 3, share, width)
    if share % 16:
        rest = rest.transpose(1, 0, 2, 3).reshape(1, 3, width, width)
    early = jnp.stack([early_lines] + [swap(send, "x", k) for k in range(1, x_size)])

    row = row.reshape(s_size, tokens + sources_len + label_rows, width)
    row_inputs = row[:, :tokens].reshape(row_len, width)
    labels = row[:, tokens + sources_len :].reshape(s_size, label_rows * width).astype(jnp.int32)
    row_seg = labels[:, :tokens].reshape(-1)
    row_sources = jnp.concatenate(
        [pick(row, block_of[j])[tokens : tokens + sources_len] for j in range(s_size)]
    )
    source_seg = jnp.concatenate(
        [pick(labels, block_of[j])[tokens : tokens + sources_len] for j in range(s_size)]
    )
    half_rows = tokens // 2
    offsets = jnp.arange(half_rows, dtype=jnp.int32)
    row_pos = (deal.reshape(s_size, 2)[owners][:, :, None] * half_rows + offsets).reshape(-1)
    row_places = (row_seg[:, None], row_seg[None], row_pos[:, None], row_pos[None])
    places = (segment_ids[0][:, None], source_seg[None])

    heads = HEADS // s_size
    weights, params, up_bias, normed_row, query, key, value, stats, self_cut = call(
        functools.partial(self_forward, z_size, x_size, held, lane, heads),
        [
            ((3, width, cut), BF),
            ((16, width), F32),
            ((1, hidden), F32),
            ((row_len, width), BF),
            ((row_len, cut), BF),
            ((row_len, cut), BF),
            ((row_len, cut), BF),
            ((row_len, 128), F32),
            ((row_len, cut), BF),
        ],
        [],
        behind(here, down_lines[-1][-1]),
        early,
        row_inputs,
        *row_places,
        flops=2 * row_len * cut * (3 * width + 2 * row_len),
    )
    parts = exchange_seq(self_cut.reshape(2, y_size, tokens, cut)).reshape(s_size, tokens, cut)

    late_z = behind(over_z, self_cut)
    memory_lines = late_z[:, up_share.shape[1] :].reshape(z_size, 2, held, cut)
    memory_lines = jnp.stack([memory_lines] + [swap(memory_lines, "x", k) for k in range(1, x_size)])
    w_memory = jnp.stack([pick(memory_lines, j ^ x_place) for j in range(x_size)])
    w_memory = w_memory.transpose(2, 1, 0, 3, 4).reshape(2, width, cut)
    source_key = matmul(row_sources, w_memory[0]).astype(BF)
    value_bias = cut_cols(params[4], s_place)
    source_value = (matmul(row_sources, w_memory[1]) + value_bias).astype(BF)
    sources_row = s_size * sources_len
    source_all = gather_seq(jnp.stack([source_key, source_value])[None])

    up_parts = behind(late_z[:, : up_share.shape[1]], source_all)
    up_parts = behind(behind(up_parts, parts), rest)
    up_parts = up_parts.reshape(z_size, share, hidden)

    after_self, after_cross, left, query_cross, cross_stats, source_keys, normed_three = call(
        functools.partial(middle_forward, s_size),
        [
            ((tokens, width), F32),
            ((tokens, width), F32),
            ((tokens, 3 * width), BF),
            ((tokens, width), BF),
            ((tokens, 128), F32),
            ((2, sources_row, width), BF),
            ((tokens, width), BF),
        ],
        [],
        block_list,
        parts,
        hidden_in[0],
        rest,
        params,
        source_all,
        *places,
        flops=2 * tokens * width * (3 * width + 2 * sources_row),
    )

    w_up = lax.all_gather(up_parts, PLANE).reshape(s_size * x_size, z_size, share, hidden)
    if share % 16:
        w_up = w_up.transpose(1, 0, 2, 3).reshape(1, 1, width, hidden)
    down_lines = [behind(jnp.concatenate(lines), parts) for lines in down_lines]
    down_lines = [jnp.concatenate([lines, swap(lines, "core", 1)]) for lines in down_lines]
    down_lines = [line.reshape(s_size, unit, width) for line in down_lines]
    down_lines = [
        jnp.concatenate([pick(line, block_of[j]) for j in range(s_size)]) for line in down_lines
    ]
    down_lines = jnp.stack([fc2.astype(BF)] + down_lines)
    w_down = jnp.concatenate([pick(down_lines, j ^ x_place) for j in range(x_size)])

    normed_all = gather_z(normed_three).reshape(z_size * tokens, width)
    group = z_size * tokens
    columns = 512
    activated, pre_grad, partial, grad_up_bias = pl.pallas_call(
        functools.partial(feed_forward, hidden // columns),
        grid=(hidden // columns,),
        out_shape=[
            jax.ShapeDtypeStruct((group, hidden), BF),
            jax.ShapeDtypeStruct((group, hidden), BF),
            jax.ShapeDtypeStruct((group, width), BF),
            jax.ShapeDtypeStruct((1, hidden), F32),
        ],
        in_specs=[
            pl.BlockSpec((group, width), lambda i: (0, 0)),
            pl.BlockSpec((group, width), lambda i: (0, 0)),
            pl.BlockSpec(w_up.shape[:3] + (columns,), lambda i: (0, 0, 0, i)),
            pl.BlockSpec((columns, width), lambda i: (i, 0)),
            pl.BlockSpec((1, columns), lambda i: (0, i)),
        ],
        out_specs=[
            pl.BlockSpec((group, columns), lambda i: (0, i)),
            pl.BlockSpec((group, columns), lambda i: (0, i)),
            pl.BlockSpec((group, width), lambda i: (0, 0)),
            pl.BlockSpec((1, columns), lambda i: (0, i)),
        ],
        scratch_shapes=[pltpu.VMEM((width, columns), BF), pltpu.VMEM((group, width), F32)],
        compiler_params=pltpu.CompilerParams(vmem_limit_bytes=VMEM_LIMIT),
        cost_estimate=pl.CostEstimate(
            flops=6 * group * width * hidden, bytes_accessed=12 << 20, transcendentals=group * hidden
        ),
    )(normed_all, down_all, w_up, w_down, up_bias)
    terms = partial.reshape(z_size, tokens, width)
    terms = [swap(pick(terms, z_place ^ k), "z", k) if k else pick(terms, z_place) for k in range(z_size)]
    terms = sum(term.astype(F32) for term in terms)
    up_rows = width // count
    half = hidden // 2
    first_rows = 2 * z_size * up_rows
    if up_rows % 16:
        late = behind(activated, partial)
        grad_down = tn(late, down_all).astype(BF)
        grad_up = [tn(normed_all, pre_grad[:, i * half : (i + 1) * half]) for i in range(2)]
        grad_up = jnp.stack(grad_up).astype(BF)
        grad_up = grad_up.reshape(2, y_size, 2, z_size, x_size, up_rows, half)
        grad_up = grad_up.transpose(2, 1, 4, 0, 3, 5, 6).reshape(x_size * s_size, -1, width)
        grad_down = grad_down.reshape(x_size * s_size, unit, width)
        grad_mlp = jnp.concatenate([grad_up, grad_down], axis=1)
        mixed_down = matmul(activated, w_down).astype(BF)
    else:
        grad_mlp, mixed_down = call(
            functools.partial(feed_forward_gradients, s_size, z_size, x_size, up_rows),
            [((x_size * s_size, first_rows + unit, width), BF), ((group, width), BF)],
            [],
            here,
            normed_all,
            pre_grad,
            activated,
            down_all,
            w_down,
            flops=6 * group * width * hidden,
        )
    left_own = lax.all_gather(left, "y")
    terms = behind(behind(terms, mixed_down), left_own)
    grad_mlp = lax.psum_scatter(grad_mlp, ("core", "y", "x"), scatter_dimension=0)
    grad_up = grad_mlp[:-unit].reshape(2, z_size, up_rows, half)
    owner = [
        (((y * 2 + c) * z_size + z) * x_size + x, ((z * 2 + c) * y_size + y) * x_size + x)
        for y in range(y_size)
        for c in range(2)
        for z in range(z_size)
        for x in range(x_size)
    ]
    grad_down = lax.ppermute(grad_mlp[-unit:], ALL, owner).astype(F32)
    grad_up = jnp.stack(
        [
            swap(pick(grad_up, z_place ^ k, 1), "z", k) if k else pick(grad_up, z_place, 1)
            for k in range(z_size)
        ]
    )
    grad_up = jnp.stack([pick(grad_up, z_place ^ j) for j in range(z_size)])
    grad_up = grad_up.transpose(2, 0, 1, 3).reshape(up_rows, -1).astype(F32)

    branch, self_grad, pair, sums = call(
        functools.partial(middle_backward, s_size),
        [
            ((tokens, width), BF),
            ((tokens, width), F32),
            ((s_size, tokens + sources_row, 2 * cut), BF),
            ((16, width), F32),
        ],
        [],
        block_list,
        terms,
        down_grad,
        after_self,
        after_cross,
        rest,
        params,
        query_cross,
        source_keys,
        cross_stats,
        *places,
        flops=2 * tokens * width * (2 * width + 5 * sources_row),
    )

    branch_row = gather_seq(branch)
    left_swapped = swap(behind(left_own, terms), "core", 1)
    w_out = rest[:, 1].reshape(width, width)
    w_out = lax.dynamic_slice_in_dim(w_out, s_place * cut, cut, 0)
    self_cuts, partial, cut_sums = call(
        functools.partial(self_backward, heads),
        [((width, 3 * cut), BF), ((row_len, width), BF), ((8, cut), F32)],
        [((row_len, 3 * cut), BF), ((row_len, cut), F32), ((row_len, cut), F32)],
        here,
        branch_row,
        w_out,
        query,
        key,
        value,
        stats,
        *row_places,
        weights,
        normed_row,
        flops=2 * row_len * cut * (7 * width + 5 * row_len),
    )

    pair = exchange_seq(pair.reshape((2, y_size) + pair.shape[1:])).reshape(pair.shape)
    pair = behind(pair, self_cuts)
    source_grad = jnp.sum(pair[:, tokens:].astype(F32), axis=0).astype(BF)
    source_grad = jnp.stack([source_grad[:, :cut], source_grad[:, cut:]])
    pair = pair[:, :tokens].reshape(row_len, 2 * cut)

    results = trade_z(behind(mixed_down, branch).reshape(z_size, tokens, width))
    result = after_cross + jnp.sum(results.astype(F32), axis=0) + params[6]
    def whole_columns(grads, number):
        grads = jnp.sum(grads.astype(F32), axis=1).reshape(s_size, up_rows, number, cut)
        return grads.transpose(2, 1, 0, 3).reshape(number, up_rows, width)

    grad_memory = nt(source_grad[0], w_memory[0]) + nt(source_grad[1], w_memory[1])
    grad_memory = grad_memory.reshape(s_size, sources_len, width)
    grad_memory = jnp.stack([pick(grad_memory, owners[j]) for j in range(s_size)])
    grad_memory = scatter_seq(grad_memory.reshape(2, y_size, sources_len, width))

    partial = partial.reshape(2, y_size, tokens, width)
    line = partial[0].astype(F32) + swap(partial[1], "core", 1).astype(F32)
    others = jnp.stack([swap(line[k].astype(BF), "y", k) for k in range(1, y_size)])
    cut_sums = jnp.concatenate([cut_sums[:2], jnp.sum(source_grad[1].astype(F32), axis=0)[None]])
    cut_sums = lax.dynamic_update_slice(
        jnp.zeros((3, width), F32), cut_sums, (jnp.int32(0), (s_place * cut).astype(jnp.int32))
    )
    grad_hidden, table = call(
        functools.partial(last_step, up_rows),
        [((tokens, width), F32), ((width, 128), BF)],
        [((128, width), F32)],
        here,
        line[0],
        others,
        hidden_in[0],
        params,
        self_grad,
        sums,
        cut_sums,
        grad_up_bias,
    )

    (group_cuts,) = call(
        group_gradients,
        [((width, 5 * cut), BF)],
        [],
        here,
        left_own,
        left_swapped,
        pair,
        cut_cols(branch_row, s_place),
        row_sources,
        source_grad,
        flops=2 * row_len * cut * 3 * width,
    )
    group_cuts = group_cuts.reshape(s_size * z_size, x_size, up_rows, 5 * cut)
    kept = pick(group_cuts, x_place, 1).astype(F32)
    for k in range(1, x_size):
        kept = kept + swap(pick(group_cuts, x_place ^ k, 1), "x", k).astype(F32)

    self_cuts = behind(self_cuts, results).reshape(count, up_rows, 3 * cut)
    self_cuts = lax.all_to_all(self_cuts, ALL, 0, 0).reshape(s_size, f_size, up_rows, 3 * cut)
    kept = behind(behind(behind(kept, self_cuts), grad_memory), grad_up)
    table = behind(behind(table, self_cuts), grad_up)
    table = lax.all_to_all(table.reshape(count, up_rows, 128), ALL, 0, 0)
    table = jnp.sum(table.astype(F32), axis=0).T
    kept = behind(kept, table)
    kept = lax.all_to_all(kept.astype(BF), ("y", "core", "z"), 0, 0)
    kept = behind(kept, grad_down)
    group_cuts = whole_columns(kept.reshape(s_size, z_size, up_rows, 5 * cut), 5)
    self_cuts = whole_columns(self_cuts, 3)
    return (
        result.astype(BF)[None],
        grad_hidden[None],
        grad_memory[None],
        jnp.stack([self_cuts, jnp.concatenate([group_cuts[:1], group_cuts[3:]])]),
        jnp.stack([group_cuts[2], group_cuts[1]]),
        grad_up,
        grad_down,
        table[:7],
        table[16:24].reshape(-1),
        table[7:10],
        table[10:13],
    )


def solution(mesh):
    seq, fsdp = mesh.shape["seq"], mesh.shape["fsdp"]
    split = Mesh(mesh.devices.reshape(seq // 2, 2, 4, fsdp // 4), ALL)
    placed = (
        P(FSDP, SEQ, None),
        P(FSDP, SEQ, None),
        P(FSDP, SEQ, None),
        P(FSDP, SEQ),
        P(FSDP, SEQ),
        P(),
        P(None, None, FSDP, None),
        P(None, FSDP, None),
        P(FSDP, None),
        P(FSDP, None),
        P(None, FSDP),
        P(FSDP),
        P(None, FSDP),
        P(None, FSDP),
    )
    return jax.shard_map(
        body,
        mesh=split,
        in_specs=placed,
        out_specs=(
            P(FSDP, SEQ, None),
            P(FSDP, SEQ, None),
            P(FSDP, SEQ, None),
            P(None, None, ALL, None),
            P(None, ALL, None),
            P(ALL, None),
            P(ALL, None),
            P(None, ALL),
            P(ALL),
            P(None, ALL),
            P(None, ALL),
        ),
        check_vma=False,
    )
```

```python
import functools
import math

import jax
import jax.numpy as jnp
from jax import lax
from jax.experimental import pallas as pl
from jax.experimental.pallas import tpu as pltpu
from jax.sharding import Mesh
from jax.sharding import PartitionSpec as P

HEADS = 16
EPSILON = 1e-05
NEGATIVE = -1e30
GELU_IN = math.sqrt(2.0 / math.pi)
GELU_CUBE = 0.044715
SEQ = ("y", "core")
FSDP = ("z", "x")
PLANE = ("x", "y", "core")
ALL = ("y", "core", "z", "x")
BF = jnp.bfloat16
F32 = jnp.float32
VMEM_LIMIT = 52 * 1024 * 1024


def matmul(left, right):
    return jnp.dot(left, right, preferred_element_type=F32)


def swap(value, axis, step):
    return lax.ppermute(value, axis, [(i, i ^ step) for i in range(lax.axis_size(axis))])


def norm_parts(values):
    centred = values - jnp.mean(values, axis=-1, keepdims=True)
    scale = lax.rsqrt(jnp.mean(centred * centred, axis=-1, keepdims=True) + EPSILON)
    return centred * scale, scale


def norm_back(normed, scale, gain, grad):
    inner = grad * gain
    means = jnp.mean(inner, axis=-1, keepdims=True)
    along = jnp.mean(inner * normed, axis=-1, keepdims=True)
    return (
        scale * (inner - means - normed * along),
        jnp.sum(grad * normed, axis=0, keepdims=True),
        jnp.sum(grad, axis=0, keepdims=True),
    )


def nt(left, right):
    return lax.dot_general(left, right, (((1,), (1,)), ((), ())), preferred_element_type=F32)


def tn(left, right):
    return lax.dot_general(left, right, (((0,), (0,)), ((), ())), preferred_element_type=F32)


def total_rows(values):
    return jnp.sum(values, axis=0, keepdims=True)


def call(kernel, outs, scratch, scalars, *operands, flops=0):
    vmem = pl.BlockSpec(memory_space=pltpu.VMEM)
    moved = sum(o.size * o.dtype.itemsize for o in operands)
    return pl.pallas_call(
        kernel,
        out_shape=[jax.ShapeDtypeStruct(shape, kind) for shape, kind in outs],
        in_specs=[pl.BlockSpec(memory_space=pltpu.SMEM)] + [vmem] * len(operands),
        out_specs=[vmem] * len(outs),
        scratch_shapes=[pltpu.VMEM(shape, kind) for shape, kind in scratch],
        compiler_params=pltpu.CompilerParams(vmem_limit_bytes=VMEM_LIMIT),
        cost_estimate=pl.CostEstimate(flops=flops, bytes_accessed=moved, transcendentals=0),
    )(scalars, *operands)


def softmax_rows(scores, bias):
    scores = scores + bias
    top = jnp.max(scores, axis=1, keepdims=True)
    raised = jnp.exp(scores - top)
    whole = jnp.maximum(jnp.sum(raised, axis=1, keepdims=True), 1.0)
    scale = jnp.where(top > 0.5 * NEGATIVE, 1.0 / whole, 0.0)
    return raised * scale, top, scale


def softmax_again(scores, bias, top, scale):
    return jnp.exp(scores + bias - top) * scale


def softmax_back(chance, chance_grad):
    return chance * (chance_grad - jnp.sum(chance * chance_grad, axis=1, keepdims=True))


def bias_of(query_seg, key_seg, query_pos=None, key_pos=None):
    allowed = (query_seg == key_seg) & (query_seg != 0)
    if query_pos is not None:
        allowed = allowed & (key_pos <= query_pos)
    return jnp.where(allowed, 0.0, NEGATIVE)


def self_forward(
    z_size, x_size, held, lane, heads, at, lines, row, seg, seg_line, pos, pos_line,
    weights, params, up_bias, normed, query, key, value, stats, mixed,
):
    z_place, x_place = at[0], at[1]
    width = row.shape[1]
    cut = query.shape[1]
    row_len = row.shape[0]
    block = min(row_len, 512)
    for j in range(z_size * x_size):
        kx, kz = (j % x_size) ^ x_place, (j // x_size) ^ z_place
        for m in range(3):
            weights[m, j * held : (j + 1) * held, :] = lines[kx, kz, m * held : (m + 1) * held, :]
        small = lines[kx, kz, 3 * held :, :].astype(F32)
        for r in range(13):
            o, c = divmod(r * lane, cut)
            params[r : r + 1, j * lane : (j + 1) * lane] = small[o : o + 1, c : c + lane]
    part = up_bias.shape[1] // x_size
    for xx in range(x_size):
        small = lines[xx ^ x_place, 0, 3 * held :, :].astype(F32)
        for r in range(part // lane):
            o, c = divmod((13 + r) * lane, cut)
            first = xx * part + r * lane
            up_bias[:, first : first + lane] = small[o : o + 1, c : c + lane]
    gain, shift = params[7:8, :], params[10:11, :]
    both = jnp.zeros((2, cut), F32)
    for j in range(width // cut):
        both = jnp.where(at[2] == j, params[0:2, j * cut : (j + 1) * cut], both)
    query_bias, value_bias = both[0:1], both[1:2]
    for b in range(row_len // block):
        rows = slice(b * block, (b + 1) * block)
        unit, _ = norm_parts(row[rows, :].astype(F32))
        h = (unit * gain + shift).astype(BF)
        normed[rows, :] = h
        query[rows, :] = (matmul(h, weights[0]) + query_bias).astype(BF)
        key[rows, :] = matmul(h, weights[1]).astype(BF)
        value[rows, :] = (matmul(h, weights[2]) + value_bias).astype(BF)
    size = cut // heads
    score_scale = 1.0 / math.sqrt(size)
    for b in range(row_len // block):
        rows = slice(b * block, (b + 1) * block)
        bias = bias_of(seg[rows, :], seg_line[...], pos[rows, :], pos_line[...])
        for h in range(heads):
            cols = slice(h * size, (h + 1) * size)
            scores = nt(query[rows, cols], key[:, cols]) * score_scale
            chance, top, scale = softmax_rows(scores, bias)
            stats[rows, h : h + 1] = top
            stats[rows, 64 + h : 65 + h] = scale
            mixed[rows, cols] = matmul(chance.astype(BF), value[:, cols]).astype(BF)


def matrix(rest, m):
    values = rest[:, m]
    return values.reshape(values.shape[0] * values.shape[1], values.shape[2])


def middle_forward(
    s_size, at, parts, inputs, rest, params, sources, seg, source_seg,
    after_self, after_cross, left, query, stats, keys, normed,
):
    width = inputs.shape[1]
    cut = width // s_size
    for j in range(s_size):
        left[:, 2 * width + j * cut : 2 * width + (j + 1) * cut] = parts[at[j]]
        for n in range(2):
            keys[n, :, j * cut : (j + 1) * cut] = sources[at[j], n]
    x1 = (
        inputs[...].astype(F32)
        + matmul(left[:, 2 * width :], matrix(rest, 1))
        + params[2:3, :]
    )
    after_self[...] = x1
    unit, _ = norm_parts(x1)
    left[:, :width] = (unit * params[8:9, :] + params[11:12, :]).astype(BF)
    query[...] = (matmul(left[:, :width], matrix(rest, 0)) + params[3:4, :]).astype(BF)
    bias = bias_of(seg[...], source_seg[...])
    size = width // HEADS
    score_scale = 1.0 / math.sqrt(size)
    for h in range(HEADS):
        cols = slice(h * size, (h + 1) * size)
        scores = nt(query[:, cols], keys[0, :, cols]) * score_scale
        chance, top, scale = softmax_rows(scores, bias)
        stats[:, h : h + 1] = top
        stats[:, 64 + h : 65 + h] = scale
        left[:, width + h * size : width + (h + 1) * size] = matmul(
            chance.astype(BF), keys[1, :, cols]
        ).astype(BF)
    x2 = x1 + matmul(left[:, width : 2 * width], matrix(rest, 2)) + params[5:6, :]
    after_cross[...] = x2
    unit, _ = norm_parts(x2)
    normed[...] = (unit * params[9:10, :] + params[12:13, :]).astype(BF)


def middle_backward(
    s_size, at, terms, out_grad, after_self, after_cross, rest, params, query,
    keys, stats, seg, source_seg,
    branch, self_grad, pair, sums,
):
    tokens, width = out_grad.shape
    cut = width // s_size
    size = width // HEADS
    score_scale = 1.0 / math.sqrt(size)
    down = out_grad[...].astype(F32)
    grad = terms[...]
    unit, scale = norm_parts(after_cross[...])
    moved, gain, shift = norm_back(unit, scale, params[9:10, :], grad)
    sums[2:3, :] = gain
    sums[5:6, :] = shift
    x2_grad = down + moved
    d2 = x2_grad.astype(BF)
    sums[6:7, :] = total_rows(d2.astype(F32))
    sums[7:8, :] = total_rows(down)
    for j in range(s_size):
        pair[at[j], :tokens, cut:] = d2[:, j * cut : (j + 1) * cut]
    head_grad = nt(d2, matrix(rest, 2)).astype(BF)
    bias = bias_of(seg[...], source_seg[...])
    per = HEADS // s_size
    grads = []
    for h in range(HEADS):
        cols = slice(h * size, (h + 1) * size)
        q, do = query[:, cols], head_grad[:, cols]
        k, v = keys[0, :, cols], keys[1, :, cols]
        scores = nt(q, k) * score_scale
        chance = softmax_again(scores, bias, stats[:, h : h + 1], stats[:, 64 + h : 65 + h])
        score_grad = softmax_back(chance, nt(do, v)).astype(BF)
        grads.append((matmul(score_grad, k) * score_scale).astype(BF))
        to = slice((h % per) * size, (h % per + 1) * size)
        pair[at[h // per], tokens:, to] = (tn(score_grad, q) * score_scale).astype(BF)
        to = slice(cut + to.start, cut + to.stop)
        pair[at[h // per], tokens:, to] = tn(chance.astype(BF), do).astype(BF)
    query_grad = jnp.concatenate(grads, axis=1)
    sums[8:9, :] = total_rows(query_grad.astype(F32))
    for j in range(s_size):
        pair[at[j], :tokens, :cut] = query_grad[:, j * cut : (j + 1) * cut]
    unit, scale = norm_parts(after_self[...])
    moved, gain, shift = norm_back(unit, scale, params[8:9, :], nt(query_grad, matrix(rest, 0)))
    sums[1:2, :] = gain
    sums[4:5, :] = shift
    x1_grad = x2_grad + moved
    self_grad[...] = x1_grad
    d1 = x1_grad.astype(BF)
    branch[...] = d1
    sums[9:10, :] = total_rows(d1.astype(F32))


def feed_forward(
    steps, normed, down, w_up, w_down, up_bias,
    activated, pre_grad, partial, bias_grad,
    held, total,
):
    step = pl.program_id(0)
    groups, z_size, share, columns = w_up.shape
    per = groups * share
    for z in range(z_size):
        held[z * per : (z + 1) * per, :] = w_up[:, z].reshape(per, columns)
    u = matmul(normed[...], held[...]) + up_bias[...]
    square = u * u
    bent = jnp.tanh(GELU_IN * (u + GELU_CUBE * square * u))
    half = 0.5 * (1.0 + bent)
    activated[...] = (u * half).astype(BF)
    slope = half + 0.5 * u * (1.0 - bent * bent) * (GELU_IN + 3.0 * GELU_IN * GELU_CUBE * square)
    du = (nt(down[...], w_down[...]) * slope).astype(BF)
    pre_grad[...] = du
    bias_grad[...] = total_rows(du.astype(F32))
    term = nt(du, held[...])

    @pl.when(step == 0)
    def _():
        total[...] = term

    @pl.when(step > 0)
    def _():
        total[...] += term

    @pl.when(step == steps - 1)
    def _():
        partial[...] = total[...].astype(BF)


def feed_forward_gradients(
    s_size, z_size, x_size, up_rows, at, normed, pre_grad, activated, down, w_down,
    out, mixed,
):
    width = normed.shape[1]
    half = pre_grad.shape[1] // 2
    places = z_size * x_size
    unit = out.shape[1] - 2 * z_size * up_rows
    for b in range(x_size * s_size):
        term = tn(activated[:, b * unit : (b + 1) * unit], down[...])
        out[b, 2 * z_size * up_rows :, :] = term.astype(BF)
    for t in range(width // 256):
        cols = slice(t * 256, (t + 1) * 256)
        mixed[:, cols] = matmul(activated[...], w_down[:, cols]).astype(BF)
    tile = places * up_rows
    for s in range(s_size):
        for i in range(2):
            term = tn(normed[:, s * tile : (s + 1) * tile], pre_grad[:, i * half : (i + 1) * half])
            term = term.astype(BF)
            for f in range(places):
                z, x = divmod(f, x_size)
                first = (i * z_size + z) * up_rows
                b = ((s % 2) * (s_size // 2) + s // 2) * x_size + x
                out[b, first : first + up_rows, :] = term[f * up_rows : (f + 1) * up_rows]


def self_backward(
    heads, at, branch, w_out, query, key, value, stats, seg, seg_line, pos, pos_line, weights, normed,
    cuts, partial, sums,
    grads, key_total, value_total,
):
    row_len, cut = query.shape
    block = min(row_len, 512)
    size = cut // heads
    score_scale = 1.0 / math.sqrt(size)
    for b in range(row_len // block):
        rows = slice(b * block, (b + 1) * block)
        head_grad = nt(branch[rows, :], w_out[...]).astype(BF)
        bias = bias_of(seg[rows, :], seg_line[...], pos[rows, :], pos_line[...])
        for h in range(heads):
            cols = slice(h * size, (h + 1) * size)
            q, do, k, v = query[rows, cols], head_grad[:, cols], key[:, cols], value[:, cols]
            chance = softmax_again(
                nt(q, k) * score_scale, bias, stats[rows, h : h + 1], stats[rows, 64 + h : 65 + h]
            )
            score_grad = softmax_back(chance, nt(do, v)).astype(BF)
            grads[rows, cols] = (matmul(score_grad, k) * score_scale).astype(BF)
            key_term = tn(score_grad, q) * score_scale
            value_term = tn(chance.astype(BF), do)
            if b == 0:
                key_total[:, cols] = key_term
                value_total[:, cols] = value_term
            else:
                key_total[:, cols] += key_term
                value_total[:, cols] += value_term
    grads[:, cut : 2 * cut] = key_total[...].astype(BF)
    grads[:, 2 * cut :] = value_total[...].astype(BF)
    sums[0:1, :] = total_rows(grads[:, :cut].astype(F32))
    sums[1:2, :] = total_rows(grads[:, 2 * cut :].astype(F32))
    tile = min(256, normed.shape[1])
    for t in range(normed.shape[1] // tile):
        rows = slice(t * tile, (t + 1) * tile)
        cuts[rows, :] = tn(normed[:, rows], grads[...]).astype(BF)
    for b in range(row_len // block):
        rows = slice(b * block, (b + 1) * block)
        grad = nt(grads[rows, :cut], weights[0]) + nt(grads[rows, cut : 2 * cut], weights[1])
        partial[rows, :] = (grad + nt(grads[rows, 2 * cut :], weights[2])).astype(BF)


def group_gradients(at, own, swapped, pair, branch_cut, sources, source_grad, out):
    (y_size, rows, _), cut = own.shape, branch_cut.shape[1]
    y_place = lax.div(at[2], 2)
    width = sources.shape[1]
    tile = min(256, width)
    for t in range(width // tile):
        to = slice(t * tile, (t + 1) * tile)
        for n in range(3):
            cols = slice(n * width + t * tile, n * width + (t + 1) * tile)
            right = branch_cut if n == 2 else pair
            first = n * cut if n < 2 else 0
            term = jnp.zeros((tile, cut), F32)
            for k in range(y_size):
                near = slice(k * rows, (k + 1) * rows)
                far = slice((y_size + k) * rows, (y_size + k + 1) * rows)
                term = term + tn(own[y_place ^ k, :, cols], right[near, first : first + cut])
                term = term + tn(swapped[y_place ^ k, :, cols], right[far, first : first + cut])
            out[to, n * cut : (n + 1) * cut] = term.astype(BF)
        for n in range(2):
            out[to, (3 + n) * cut : (4 + n) * cut] = tn(sources[:, to], source_grad[n]).astype(BF)


def last_step(
    lanes, at, line, others, inputs, params, self_grad, sums, cut_sums, up_bias_grad,
    grad_hidden, table, rows,
):
    unit, scale = norm_parts(inputs[...].astype(F32))
    grad = line[...] + jnp.sum(others[...].astype(F32), axis=0)
    moved, gain, shift = norm_back(unit, scale, params[7:8, :], grad)
    grad_hidden[...] = self_grad[...] + moved
    rows[...] = jnp.zeros(rows.shape, F32)
    rows[0:2, :] = cut_sums[0:2, :]
    rows[2:3, :] = sums[9:10, :]
    rows[3:4, :] = sums[8:9, :]
    rows[4:5, :] = cut_sums[2:3, :]
    rows[5:7, :] = sums[6:8, :]
    rows[7:8, :] = gain
    rows[8:10, :] = sums[1:3, :]
    rows[10:11, :] = shift
    rows[11:13, :] = sums[4:6, :]
    mine = up_bias_grad.shape[1] // 8
    at_lane = pl.ds(pl.multiple_of(at[0] * mine, mine), mine)
    for k in range(8):
        parts = [
            up_bias_grad[:, first : first + lanes]
            for first in range(k * lanes, up_bias_grad.shape[1], 8 * lanes)
        ]
        rows[16 + k : 17 + k, at_lane] = jnp.concatenate(parts, axis=1)
    table[...] = rows[...].T.astype(BF)


def gather_pair(value):
    lines = [value] + [swap(value, "y", k) for k in range(1, lax.axis_size("y"))]
    lines = jnp.concatenate(lines) if len(lines) > 1 else value
    return lines, swap(lines, "core", 1)


def gather_seq(value):
    return jnp.concatenate(gather_pair(value))


def scatter_seq(partial):
    line = partial[0].astype(F32) + swap(partial[1].astype(BF), "core", 1).astype(F32)
    total = line[0]
    for k in range(1, lax.axis_size("y")):
        total = total + swap(line[k].astype(BF), "y", k).astype(F32)
    return total


def exchange_seq(value):
    line = jnp.stack([value[0], swap(value[1], "core", 1)])
    lines = [line[:, 0]] + [swap(line[:, k], "y", k) for k in range(1, lax.axis_size("y"))]
    return jnp.stack(lines, axis=1)


def trade_z(parts):
    return lax.all_to_all(parts, "z", 0, 0)


def gather_z(value):
    return trade_z(jnp.broadcast_to(value, (lax.axis_size("z"),) + value.shape))


def behind(value, other):
    last = other[(-1,) * other.ndim].astype(F32) * 0.0
    return value + last.astype(value.dtype)


def pick(value, at, axis=0):
    return lax.dynamic_index_in_dim(value, at, axis, keepdims=False)


def body(
    hidden_in,
    memory,
    out_grad,
    segment_ids,
    memory_segments,
    deal,
    attn_in,
    attn_out,
    fc1,
    fc2,
    proj_bias,
    fc1_bias,
    norm_gain,
    norm_bias,
):
    y_size, z_size, x_size = lax.axis_size("y"), lax.axis_size("z"), lax.axis_size("x")
    s_size, f_size = y_size * 2, z_size * x_size
    y_place, core_place = lax.axis_index("y"), lax.axis_index("core")
    z_place, x_place = lax.axis_index("z"), lax.axis_index("x")
    s_place = y_place * 2 + core_place
    f_place = z_place * x_size + x_place
    place = s_place * f_size + f_place
    count = s_size * f_size
    tokens, width = hidden_in.shape[1:]
    sources_len = memory.shape[1]
    held = attn_in.shape[2]
    share = held // s_size
    lane = width // f_size
    cut = width // s_size
    row_len = s_size * tokens
    blocks = [(c, k) for c in range(2) for k in range(y_size)]
    block_of = [((j % 2) ^ core_place) * y_size + ((j // 2) ^ y_place) for j in range(s_size)]
    owners = jnp.stack([(y_place ^ k) * 2 + (core_place ^ c) for c, k in blocks])

    def cut_cols(value, at):
        return lax.dynamic_slice_in_dim(value, at * cut, cut, value.ndim - 1)

    here = jnp.stack([z_place, x_place, s_place, core_place]).astype(jnp.int32)
    block_list = jnp.stack(block_of).astype(jnp.int32)

    small = jnp.concatenate(
        [
            proj_bias.reshape(-1).astype(BF),
            norm_gain.reshape(-1).astype(BF),
            norm_bias.reshape(-1).astype(BF),
            fc1_bias.astype(BF),
        ]
    )
    small_len = small.shape[0]
    small_rows = -(-small_len // (16 * cut)) * 16
    small = jnp.pad(small, (0, small_rows * cut - small_len)).reshape(small_rows, cut)
    early = jnp.concatenate([cut_cols(attn_in[0], s_place).astype(BF).reshape(3 * held, cut), small])

    rest = jnp.concatenate(
        [
            lax.dynamic_slice_in_dim(attn_in[1, 0], s_place * share, share, 0),
            lax.dynamic_slice_in_dim(attn_out, s_place * share, share, 1).reshape(-1, width),
        ]
    ).astype(BF)
    labels = jnp.concatenate([segment_ids[0], memory_segments[0]]).astype(BF)
    label_rows = -(-labels.shape[0] // (16 * width)) * 16
    labels = jnp.pad(labels, (0, label_rows * width - labels.shape[0])).reshape(label_rows, width)
    row = jnp.concatenate([hidden_in[0], memory[0], labels])
    row_lines = [row] + [swap(row, "y", k) for k in range(1, y_size)]
    row_lines = jnp.concatenate(row_lines)
    row = jnp.concatenate([row_lines, swap(row_lines, "core", 1)])
    early_lines = [early] + [swap(early, "z", k) for k in range(1, z_size)]
    early_lines = jnp.stack(early_lines)
    unit = fc2.shape[0] // s_size
    hidden = x_size * fc2.shape[0]
    down_share = lax.dynamic_slice_in_dim(fc2, s_place * unit, unit, 0).astype(BF)
    down_lines = [swap(down_share, "x", k) for k in range(1, x_size)]
    send = behind(early_lines, down_lines[-1])
    down_lines = [behind(line, early_lines) for line in down_lines]
    down_lines = [[line] + [swap(line, "y", k) for k in range(1, y_size)] for line in down_lines]

    up_share = lax.dynamic_slice_in_dim(fc1, s_place * share, share, 0).astype(BF)
    up_share = up_share.reshape(share, z_size, hidden).transpose(1, 0, 2).reshape(z_size, -1, width)
    memory_cuts = cut_cols(attn_in[1, 1:], s_place).astype(BF).reshape(1, -1, width)
    memory_cuts = jnp.broadcast_to(memory_cuts, (z_size,) + memory_cuts.shape[1:])
    down_grad = out_grad[0]
    down_copies = jnp.broadcast_to(down_grad, (z_size,) + down_grad.shape)
    over_z = trade_z(jnp.concatenate([up_share, memory_cuts, down_copies], axis=1))
    down_all = over_z[:, -tokens:].reshape(z_size * tokens, width)
    over_z = over_z[:, :-tokens]

    rest = lax.all_gather(rest, FSDP + SEQ).reshape(count, 3, share, width)
    if share % 16:
        rest = rest.transpose(1, 0, 2, 3).reshape(1, 3, width, width)
    early = jnp.stack([early_lines] + [swap(send, "x", k) for k in range(1, x_size)])

    row = row.reshape(s_size, tokens + sources_len + label_rows, width)
    row_inputs = row[:, :tokens].reshape(row_len, width)
    labels = row[:, tokens + sources_len :].reshape(s_size, label_rows * width).astype(jnp.int32)
    row_seg = labels[:, :tokens].reshape(-1)
    row_sources = jnp.concatenate(
        [pick(row, block_of[j])[tokens : tokens + sources_len] for j in range(s_size)]
    )
    source_seg = jnp.concatenate(
        [pick(labels, block_of[j])[tokens : tokens + sources_len] for j in range(s_size)]
    )
    half_rows = tokens // 2
    offsets = jnp.arange(half_rows, dtype=jnp.int32)
    row_pos = (deal.reshape(s_size, 2)[owners][:, :, None] * half_rows + offsets).reshape(-1)
    row_places = (row_seg[:, None], row_seg[None], row_pos[:, None], row_pos[None])
    places = (segment_ids[0][:, None], source_seg[None])

    heads = HEADS // s_size
    weights, params, up_bias, normed_row, query, key, value, stats, self_cut = call(
        functools.partial(self_forward, z_size, x_size, held, lane, heads),
        [
            ((3, width, cut), BF),
            ((16, width), F32),
            ((1, hidden), F32),
            ((row_len, width), BF),
            ((row_len, cut), BF),
            ((row_len, cut), BF),
            ((row_len, cut), BF),
            ((row_len, 128), F32),
            ((row_len, cut), BF),
        ],
        [],
        behind(here, down_lines[-1][-1]),
        early,
        row_inputs,
        *row_places,
        flops=2 * row_len * cut * (3 * width + 2 * row_len),
    )
    parts = exchange_seq(self_cut.reshape(2, y_size, tokens, cut)).reshape(s_size, tokens, cut)

    late_z = behind(over_z, self_cut)
    memory_lines = late_z[:, up_share.shape[1] :].reshape(z_size, 2, held, cut)
    memory_lines = jnp.stack([memory_lines] + [swap(memory_lines, "x", k) for k in range(1, x_size)])
    w_memory = jnp.stack([pick(memory_lines, j ^ x_place) for j in range(x_size)])
    w_memory = w_memory.transpose(2, 1, 0, 3, 4).reshape(2, width, cut)
    source_key = matmul(row_sources, w_memory[0]).astype(BF)
    value_bias = cut_cols(params[4], s_place)
    source_value = (matmul(row_sources, w_memory[1]) + value_bias).astype(BF)
    sources_row = s_size * sources_len
    source_all = gather_seq(jnp.stack([source_key, source_value])[None])

    up_parts = behind(late_z[:, : up_share.shape[1]], source_all)
    up_parts = behind(behind(up_parts, parts), rest)
    up_parts = up_parts.reshape(z_size, share, hidden)

    after_self, after_cross, left, query_cross, cross_stats, source_keys, normed_three = call(
        functools.partial(middle_forward, s_size),
        [
            ((tokens, width), F32),
            ((tokens, width), F32),
            ((tokens, 3 * width), BF),
            ((tokens, width), BF),
            ((tokens, 128), F32),
            ((2, sources_row, width), BF),
            ((tokens, width), BF),
        ],
        [],
        block_list,
        parts,
        hidden_in[0],
        rest,
        params,
        source_all,
        *places,
        flops=2 * tokens * width * (3 * width + 2 * sources_row),
    )

    w_up = lax.all_gather(up_parts, PLANE).reshape(s_size * x_size, z_size, share, hidden)
    if share % 16:
        w_up = w_up.transpose(1, 0, 2, 3).reshape(1, 1, width, hidden)
    down_lines = [behind(jnp.concatenate(lines), parts) for lines in down_lines]
    down_lines = [jnp.concatenate([lines, swap(lines, "core", 1)]) for lines in down_lines]
    down_lines = [line.reshape(s_size, unit, width) for line in down_lines]
    down_lines = [
        jnp.concatenate([pick(line, block_of[j]) for j in range(s_size)]) for line in down_lines
    ]
    down_lines = jnp.stack([fc2.astype(BF)] + down_lines)
    w_down = jnp.concatenate([pick(down_lines, j ^ x_place) for j in range(x_size)])

    normed_all = gather_z(normed_three).reshape(z_size * tokens, width)
    group = z_size * tokens
    columns = 512
    activated, pre_grad, partial, grad_up_bias = pl.pallas_call(
        functools.partial(feed_forward, hidden // columns),
        grid=(hidden // columns,),
        out_shape=[
            jax.ShapeDtypeStruct((group, hidden), BF),
            jax.ShapeDtypeStruct((group, hidden), BF),
            jax.ShapeDtypeStruct((group, width), BF),
            jax.ShapeDtypeStruct((1, hidden), F32),
        ],
        in_specs=[
            pl.BlockSpec((group, width), lambda i: (0, 0)),
            pl.BlockSpec((group, width), lambda i: (0, 0)),
            pl.BlockSpec(w_up.shape[:3] + (columns,), lambda i: (0, 0, 0, i)),
            pl.BlockSpec((columns, width), lambda i: (i, 0)),
            pl.BlockSpec((1, columns), lambda i: (0, i)),
        ],
        out_specs=[
            pl.BlockSpec((group, columns), lambda i: (0, i)),
            pl.BlockSpec((group, columns), lambda i: (0, i)),
            pl.BlockSpec((group, width), lambda i: (0, 0)),
            pl.BlockSpec((1, columns), lambda i: (0, i)),
        ],
        scratch_shapes=[pltpu.VMEM((width, columns), BF), pltpu.VMEM((group, width), F32)],
        compiler_params=pltpu.CompilerParams(vmem_limit_bytes=VMEM_LIMIT),
        cost_estimate=pl.CostEstimate(
            flops=6 * group * width * hidden, bytes_accessed=12 << 20, transcendentals=group * hidden
        ),
    )(normed_all, down_all, w_up, w_down, up_bias)
    terms = partial.reshape(z_size, tokens, width)
    terms = [swap(pick(terms, z_place ^ k), "z", k) if k else pick(terms, z_place) for k in range(z_size)]
    terms = sum(term.astype(F32) for term in terms)
    up_rows = width // count
    half = hidden // 2
    first_rows = 2 * z_size * up_rows
    if up_rows % 16:
        late = behind(activated, partial)
        grad_down = tn(late, down_all).astype(BF)
        grad_up = [tn(normed_all, pre_grad[:, i * half : (i + 1) * half]) for i in range(2)]
        grad_up = jnp.stack(grad_up).astype(BF)
        grad_up = grad_up.reshape(2, y_size, 2, z_size, x_size, up_rows, half)
        grad_up = grad_up.transpose(2, 1, 4, 0, 3, 5, 6).reshape(x_size * s_size, -1, width)
        grad_down = grad_down.reshape(x_size * s_size, unit, width)
        grad_mlp = jnp.concatenate([grad_up, grad_down], axis=1)
        mixed_down = matmul(activated, w_down).astype(BF)
    else:
        grad_mlp, mixed_down = call(
            functools.partial(feed_forward_gradients, s_size, z_size, x_size, up_rows),
            [((x_size * s_size, first_rows + unit, width), BF), ((group, width), BF)],
            [],
            here,
            normed_all,
            pre_grad,
            activated,
            down_all,
            w_down,
            flops=6 * group * width * hidden,
        )
    left_own = lax.all_gather(left, "y")
    terms = behind(behind(terms, mixed_down), left_own)
    grad_mlp = lax.psum_scatter(grad_mlp, ("core", "y", "x"), scatter_dimension=0)
    grad_up = grad_mlp[:-unit].reshape(2, z_size, up_rows, half)
    owner = [
        (((y * 2 + c) * z_size + z) * x_size + x, ((z * 2 + c) * y_size + y) * x_size + x)
        for y in range(y_size)
        for c in range(2)
        for z in range(z_size)
        for x in range(x_size)
    ]
    grad_down = lax.ppermute(grad_mlp[-unit:], ALL, owner).astype(F32)
    grad_up = jnp.stack(
        [
            swap(pick(grad_up, z_place ^ k, 1), "z", k) if k else pick(grad_up, z_place, 1)
            for k in range(z_size)
        ]
    )
    grad_up = jnp.stack([pick(grad_up, z_place ^ j) for j in range(z_size)])
    grad_up = grad_up.transpose(2, 0, 1, 3).reshape(up_rows, -1).astype(F32)

    branch, self_grad, pair, sums = call(
        functools.partial(middle_backward, s_size),
        [
            ((tokens, width), BF),
            ((tokens, width), F32),
            ((s_size, tokens + sources_row, 2 * cut), BF),
            ((16, width), F32),
        ],
        [],
        block_list,
        terms,
        down_grad,
        after_self,
        after_cross,
        rest,
        params,
        query_cross,
        source_keys,
        cross_stats,
        *places,
        flops=2 * tokens * width * (2 * width + 5 * sources_row),
    )

    branch_row = gather_seq(branch)
    left_swapped = swap(behind(left_own, terms), "core", 1)
    w_out = rest[:, 1].reshape(width, width)
    w_out = lax.dynamic_slice_in_dim(w_out, s_place * cut, cut, 0)
    self_cuts, partial, cut_sums = call(
        functools.partial(self_backward, heads),
        [((width, 3 * cut), BF), ((row_len, width), BF), ((8, cut), F32)],
        [((row_len, 3 * cut), BF), ((row_len, cut), F32), ((row_len, cut), F32)],
        here,
        branch_row,
        w_out,
        query,
        key,
        value,
        stats,
        *row_places,
        weights,
        normed_row,
        flops=2 * row_len * cut * (7 * width + 5 * row_len),
    )

    pair = exchange_seq(pair.reshape((2, y_size) + pair.shape[1:])).reshape(pair.shape)
    pair = behind(pair, self_cuts)
    source_grad = jnp.sum(pair[:, tokens:].astype(F32), axis=0).astype(BF)
    source_grad = jnp.stack([source_grad[:, :cut], source_grad[:, cut:]])
    pair = pair[:, :tokens].reshape(row_len, 2 * cut)

    results = trade_z(behind(mixed_down, branch).reshape(z_size, tokens, width))
    result = after_cross + jnp.sum(results.astype(F32), axis=0) + params[6]
    def whole_columns(grads, number):
        grads = jnp.sum(grads.astype(F32), axis=1).reshape(s_size, up_rows, number, cut)
        return grads.transpose(2, 1, 0, 3).reshape(number, up_rows, width)

    grad_memory = nt(source_grad[0], w_memory[0]) + nt(source_grad[1], w_memory[1])
    grad_memory = grad_memory.reshape(s_size, sources_len, width)
    grad_memory = jnp.stack([pick(grad_memory, owners[j]) for j in range(s_size)])
    grad_memory = scatter_seq(grad_memory.reshape(2, y_size, sources_len, width))

    partial = partial.reshape(2, y_size, tokens, width)
    line = partial[0].astype(F32) + swap(partial[1], "core", 1).astype(F32)
    others = jnp.stack([swap(line[k].astype(BF), "y", k) for k in range(1, y_size)])
    cut_sums = jnp.concatenate([cut_sums[:2], jnp.sum(source_grad[1].astype(F32), axis=0)[None]])
    cut_sums = lax.dynamic_update_slice(
        jnp.zeros((3, width), F32), cut_sums, (jnp.int32(0), (s_place * cut).astype(jnp.int32))
    )
    grad_hidden, table = call(
        functools.partial(last_step, up_rows),
        [((tokens, width), F32), ((width, 128), BF)],
        [((128, width), F32)],
        here,
        line[0],
        others,
        hidden_in[0],
        params,
        self_grad,
        sums,
        cut_sums,
        grad_up_bias,
    )

    (group_cuts,) = call(
        group_gradients,
        [((width, 5 * cut), BF)],
        [],
        here,
        left_own,
        left_swapped,
        pair,
        cut_cols(branch_row, s_place),
        row_sources,
        source_grad,
        flops=2 * row_len * cut * 3 * width,
    )
    group_cuts = group_cuts.reshape(s_size * z_size, x_size, up_rows, 5 * cut)
    kept = pick(group_cuts, x_place, 1).astype(F32)
    for k in range(1, x_size):
        kept = kept + swap(pick(group_cuts, x_place ^ k, 1), "x", k).astype(F32)

    self_cuts = behind(self_cuts, results).reshape(count, up_rows, 3 * cut)
    self_cuts = lax.all_to_all(self_cuts, ALL, 0, 0).reshape(s_size, f_size, up_rows, 3 * cut)
    kept = behind(kept, grad_memory)
    table = behind(behind(table, self_cuts), grad_up)
    table = lax.all_to_all(table.reshape(count, up_rows, 128), ALL, 0, 0)
    table = jnp.sum(table.astype(F32), axis=0).T
    kept = behind(kept, table)
    kept = lax.all_to_all(kept.astype(BF), ("y", "core", "z"), 0, 0)
    kept = behind(kept, grad_down)
    group_cuts = whole_columns(kept.reshape(s_size, z_size, up_rows, 5 * cut), 5)
    self_cuts = whole_columns(self_cuts, 3)
    return (
        result.astype(BF)[None],
        grad_hidden[None],
        grad_memory[None],
        jnp.stack([self_cuts, jnp.concatenate([group_cuts[:1], group_cuts[3:]])]),
        jnp.stack([group_cuts[2], group_cuts[1]]),
        grad_up,
        grad_down,
        table[:7],
        table[16:24].reshape(-1),
        table[7:10],
        table[10:13],
    )


def solution(mesh):
    seq, fsdp = mesh.shape["seq"], mesh.shape["fsdp"]
    split = Mesh(mesh.devices.reshape(seq // 2, 2, 4, fsdp // 4), ALL)
    placed = (
        P(FSDP, SEQ, None),
        P(FSDP, SEQ, None),
        P(FSDP, SEQ, None),
        P(FSDP, SEQ),
        P(FSDP, SEQ),
        P(),
        P(None, None, FSDP, None),
        P(None, FSDP, None),
        P(FSDP, None),
        P(FSDP, None),
        P(None, FSDP),
        P(FSDP),
        P(None, FSDP),
        P(None, FSDP),
    )
    return jax.shard_map(
        body,
        mesh=split,
        in_specs=placed,
        out_specs=(
            P(FSDP, SEQ, None),
            P(FSDP, SEQ, None),
            P(FSDP, SEQ, None),
            P(None, None, ALL, None),
            P(None, ALL, None),
            P(ALL, None),
            P(ALL, None),
            P(None, ALL),
            P(ALL),
            P(None, ALL),
            P(None, ALL),
        ),
        check_vma=False,
    )
```
